32 devices in a mesh: dp: 8 (over y, x, core), seq: 4 (over z).
Axes of the slice: x: 2, y: 2, z: 4, core: 2. Of those that a mesh axis runs over, the one named last changes fastest.
Arguments:
- tokens: bfloat16 [8, 1024, 1152], P('dp', 'seq'), may hold values from -6 to 6
- timesteps: int32 [8], P('dp'), may hold values from 0 to 999
- rel_index: int32 [1024, 1024], P('seq'), may hold values from 0 to 3968, as said below
- time_table: bfloat16 [1000, 1152], replicated, may hold values from -6 to 6
- bias_table: float32 [16, 3969], replicated, may hold values from -6 to 6
- gain_one: float32 [1152], replicated, may hold values from 0.25 to 1.75
- shift_one: float32 [1152], replicated, may hold values from -4 to 4
- w_query: bfloat16 [1152, 1152], replicated, may hold values from -0.1875 to 0.1875
- w_key: bfloat16 [1152, 1152], replicated, may hold values from -0.1875 to 0.1875
- w_value: bfloat16 [1152, 1152], replicated, may hold values from -0.1875 to 0.1875
- t_query: bfloat16 [1152, 1152], replicated, may hold values from -0.1875 to 0.1875
- t_value: bfloat16 [1152, 1152], replicated, may hold values from -0.1875 to 0.1875
- b_query: float32 [1152], replicated, may hold values from -6 to 6
- b_value: float32 [1152], replicated, may hold values from -6 to 6
- w_out: bfloat16 [1152, 1152], replicated, may hold values from -1.5 to 1.5
- b_out: float32 [1152], replicated, may hold values from -4 to 4
- gain_two: float32 [1152], replicated, may hold values from 0.25 to 1.75
- shift_two: float32 [1152], replicated, may hold values from -4 to 4
- w_up: bfloat16 [1152, 4608], replicated, may hold values from -0.1875 to 0.1875
- b_up: float32 [4608], replicated, may hold values from -4 to 4
- w_down: bfloat16 [4608, 1152], replicated, may hold values from -0.09375 to 0.09375
- b_down: float32 [1152], replicated, may hold values from -4 to 4
- cotangent: bfloat16 [8, 1024, 1152], P('dp', 'seq'), may hold values from -6 to 6
Outputs:
- result: bfloat16 [8, 1024, 1152], P('dp', 'seq')
- grad_tokens: bfloat16 [8, 1024, 1152], P('dp', 'seq')
- grad_w_query: float32 [1152, 1152], P('dp', 'seq')
- grad_w_key: float32 [1152, 1152], P('dp', 'seq')
- grad_w_value: float32 [1152, 1152], P('dp', 'seq')
- grad_t_query: float32 [1152, 1152], P('dp', 'seq')
- grad_t_value: float32 [1152, 1152], P('dp', 'seq')
- grad_w_out: float32 [1152, 1152], P('dp', 'seq')
- grad_w_up: float32 [1152, 4608], P('dp', 'seq')
- grad_w_down: float32 [4608, 1152], P('dp', 'seq')
- grad_gain_one: float32 [1152], replicated
- grad_shift_one: float32 [1152], replicated
- grad_b_query: float32 [1152], replicated
- grad_b_value: float32 [1152], replicated
- grad_b_out: float32 [1152], replicated
- grad_gain_two: float32 [1152], replicated
- grad_shift_two: float32 [1152], replicated
- grad_b_up: float32 [4608], replicated
- grad_b_down: float32 [1152], replicated
- grad_bias_table: float32 [16, 3969], replicated
- grad_time_table: float32 [1000, 1152], replicated
The draws below stay inside these ranges and needn't reach their ends.
Inputs may be any that keep to these rules, and one draw needn't show every extreme that they name: rel_index[i, j] = (r_i - r_j + 31) * 63 + c_i - c_j + 31, where token i sits at row r_i and column c_i of a 32 by 32 grid, each place taken by one token, in an order drawn from the seed.
All inputs are finite; a program needn't handle non-finite values.
Results may differ from the reference program's by a relative error of at most 0.018.
Values may be sent and summed in bfloat16 or wider, within the bound.
No kernel may reach another device: no remote copies, remote signals or barrier semaphores. Data moves between devices by JAX's collectives and lax.ppermute only.
A program may use at most 384 MiB of HBM per device.

```python
import jax
import jax.numpy as jnp
from jax import lax

D = 1152
HEADS = 16
HDIM = 72
FF = 4608
STEPS = 1000
GRID = 32
LEN = 1024
IMAGES = 8
NREL = 3969


def draw_rel_index(key, part):
    key = jax.random.fold_in(key, 7)
    places = jax.random.permutation(key, GRID * GRID).astype(jnp.int32)
    prow = places // GRID
    pcol = places % GRID
    across = (prow[:, None] - prow[None, :] + GRID - 1) * (2 * GRID - 1)
    return (across + pcol[:, None] - pcol[None, :] + GRID - 1).astype(jnp.int32)


def plant(result, rng, smallest, high):
    longest = result.shape.index(max(result.shape))
    spots = []
    for shift in (0, 1):
        where = [jax.random.randint(jax.random.fold_in(rng, axis), (), 0, length) for axis, length in enumerate(result.shape)]
        where[longest] = (where[longest] + shift) % result.shape[longest]
        spots.append(tuple(where))
    return result.at[spots[0]].set(smallest).at[spots[1]].set(high)


def steps_of(stream_key, extent, cuts, low, largest):
    level = 1.0
    for axis_at, shards_of in cuts:
        heights = jax.random.uniform(jax.random.fold_in(jax.random.fold_in(stream_key, 6), axis_at), (shards_of,), jnp.float32, low / len(cuts), largest / len(cuts))
        level = level * jnp.repeat(jnp.exp(heights), extent[axis_at] // shards_of).reshape((-1,) + (1,) * (len(extent) - 1 - axis_at))
    return level


def noise(own_key, shape, deviation, limit, cuts=(), kind=jnp.bfloat16):
    level = steps_of(own_key, shape, cuts, -0.22, 0.18) if cuts else 1.0
    result = jax.random.normal(own_key, shape, jnp.float32) * deviation * level
    return jnp.minimum(jnp.maximum(result, -limit), limit).astype(kind)


def setup_inputs(seed: int = 0) -> dict:
    seeds = jax.random.split(jax.random.key(seed), 24)
    return {
        "tokens": noise(seeds[0], (IMAGES, LEN, D), 1.0, 6.0, ((0, 8), (1, 4))),
        "timesteps": plant(jax.random.randint(seeds[1], (IMAGES,), 0, STEPS), jax.random.fold_in(seeds[1], 1), 0, STEPS - 1).astype(jnp.int32),
        "rel_index": draw_rel_index(jax.random.fold_in(seeds[23], 71), 0),
        "time_table": noise(seeds[3], (STEPS, D), 1.0, 6.0),
        "bias_table": noise(seeds[4], (HEADS, NREL), 1.0, 6.0, (), jnp.float32),
        "gain_one": jnp.clip(1.0 + 0.15 * jax.random.normal(seeds[5], (D,), jnp.float32), 0.25, 1.75),
        "shift_one": noise(seeds[6], (D,), 0.3, 4.0, (), jnp.float32),
        "w_query": noise(seeds[7], (D, D), D ** -0.5, 0.1875),
        "w_key": noise(seeds[8], (D, D), D ** -0.5, 0.1875),
        "w_value": noise(seeds[9], (D, D), D ** -0.5, 0.1875),
        "t_query": noise(seeds[10], (D, D), D ** -0.5, 0.1875),
        "t_value": noise(seeds[11], (D, D), D ** -0.5, 0.1875),
        "b_query": noise(seeds[12], (D,), 0.5, 6.0, (), jnp.float32),
        "b_value": noise(seeds[13], (D,), 0.5, 6.0, (), jnp.float32),
        "w_out": noise(seeds[14], (D, D), (D * 16 // LEN) ** -0.5, 1.5),
        "b_out": noise(seeds[15], (D,), 0.3, 4.0, (), jnp.float32),
        "gain_two": jnp.clip(1.0 + 0.15 * jax.random.normal(seeds[16], (D,), jnp.float32), 0.25, 1.75),
        "shift_two": noise(seeds[17], (D,), 0.3, 4.0, (), jnp.float32),
        "w_up": noise(seeds[18], (D, FF), D ** -0.5, 0.1875),
        "b_up": noise(seeds[19], (FF,), 0.3, 4.0, (), jnp.float32),
        "w_down": noise(seeds[20], (FF, D), FF ** -0.5, 0.09375),
        "b_down": noise(seeds[21], (D,), 0.3, 4.0, (), jnp.float32),
        "cotangent": noise(seeds[22], (IMAGES, LEN, D), 1.0, 6.0, ((0, 8), (1, 4))),
    }


@jax.custom_vjp
def low(v):
    return lax.optimization_barrier(v.astype(jnp.bfloat16)).astype(jnp.float32)

@jax.custom_vjp
def low_back(v):
    return v

def low_keep(v):
    return (low(v), None)

def low_pass(kept, grad):
    return (grad,)

def back_keep(v):
    return (v, None)

def back_low(kept, grad):
    return (low(grad),)
low.defvjp(low_keep, low_pass)
low_back.defvjp(back_keep, back_low)

def product(left, right):
    return jnp.dot(left, right, precision=lax.Precision.HIGHEST)

def layer_norm(values, gain, shift):
    average = lax.optimization_barrier(jnp.mean(values, axis=-1, keepdims=True))
    centered = values - average
    variance = lax.optimization_barrier(jnp.mean(centered * centered, axis=-1, keepdims=True))
    return centered * lax.rsqrt(variance + 1e-06) * gain + shift

def reference(tokens, timesteps, rel_index, time_table, bias_table, gain_one, shift_one, w_query, w_key, w_value, t_query, t_value, b_query, b_value, w_out, b_out, gain_two, shift_two, w_up, b_up, w_down, b_down, cotangent):
    scale = HDIM ** (-0.5)

    def forward(tokens_f, table_f, bias_f, gain_one, shift_one, w_query, w_key, w_value, t_query, t_value, b_query, b_value, w_out, b_out, gain_two, shift_two, w_up, b_up, w_down, b_down):
        embeds = table_f[timesteps]
        bias_full = bias_f[:, rel_index]

        def image(pair):
            values_in, embed = pair
            normed = low(layer_norm(values_in, gain_one, shift_one))
            query = low(low_back((product(normed, w_query) + product(embed, t_query) + b_query) * scale))
            keys = low(low_back(product(normed, w_key)))
            values = low(low_back(product(normed, w_value) + product(embed, t_value) + b_value))
            query = query.reshape(LEN, HEADS, HDIM)
            keys = keys.reshape(LEN, HEADS, HDIM)
            values = values.reshape(LEN, HEADS, HDIM)
            scores = jnp.einsum('qhd,khd->hqk', query, keys, precision=lax.Precision.HIGHEST) + bias_full
            scores = low_back(scores)
            top = lax.optimization_barrier(jnp.max(scores, axis=-1, keepdims=True))
            expo = jnp.exp(scores - top)
            probs = low(expo / lax.optimization_barrier(jnp.sum(expo, axis=-1, keepdims=True)))
            mixed = jnp.einsum('hqk,khd->qhd', probs, values, precision=lax.Precision.HIGHEST).reshape(LEN, D)
            mixed = low(low_back(mixed))
            middle = values_in + low_back(product(mixed, w_out) + b_out)
            normed_two = low(layer_norm(middle, gain_two, shift_two))
            inner = low_back(product(normed_two, w_up) + b_up)
            activated = low(jax.nn.gelu(inner, approximate=False))
            return middle + low_back(product(activated, w_down) + b_down)
        return lax.map(jax.checkpoint(image), (tokens_f, embeds))
    inputs = (tokens, time_table, bias_table, gain_one, shift_one, w_query, w_key, w_value, t_query, t_value, b_query, b_value, w_out, b_out, gain_two, shift_two, w_up, b_up, w_down, b_down)
    floats = tuple((array.astype(jnp.float32) for array in inputs))
    primal, pullback = jax.vjp(forward, *floats)
    grads = pullback(cotangent.astype(jnp.float32))
    g_tokens, g_table, g_bias, g_gain_one, g_shift_one, g_query, g_key, g_value, g_tquery, g_tvalue, g_bquery, g_bvalue, g_out, g_bout, g_gain_two, g_shift_two, g_up, g_bup, g_down, g_bdown = grads
    return (primal.astype(jnp.bfloat16), g_tokens.astype(jnp.bfloat16), g_query, g_key, g_value, g_tquery, g_tvalue, g_out, g_up, g_down, g_gain_one, g_shift_one, g_bquery, g_bvalue, g_bout, g_gain_two, g_shift_two, g_bup, g_bdown, g_bias, g_table)
```

```python
from functools import partial

import jax
import jax.numpy as jnp
from jax import lax
from jax.experimental import pallas as pl
from jax.experimental.pallas import tpu as pltpu
from jax.sharding import PartitionSpec as P

GRID = 32
SPAN = 2 * GRID - 1
STRIP = 2 * GRID * GRID
LANES = 128
BLOCK = 256
NORM_EPS = 1e-06
f32, bf16 = jnp.float32, jnp.bfloat16
HIGHEST = lax.Precision.HIGHEST
VMEM_LIMIT = 58 * 1024 * 1024


def dot(left, right, left_dim=1, right_dim=0):
    return lax.dot_general(
        left, right, (((left_dim,), (right_dim,)), ((), ())), preferred_element_type=f32
    )


def normalize(values):
    centered = values - jnp.mean(values, axis=-1, keepdims=True)
    scaled = lax.rsqrt(jnp.mean(centered * centered, axis=-1, keepdims=True) + NORM_EPS)
    return centered * scaled, scaled


def norm_back(grad_norm, normed, scaled, gain):
    inner = grad_norm * gain
    return scaled * (
        inner
        - jnp.mean(inner, axis=-1, keepdims=True)
        - normed * jnp.mean(inner * normed, axis=-1, keepdims=True)
    )


def fold_rows(values, op):
    return op(values.reshape(values.shape[0] // 8, 8, values.shape[1]), axis=0)


def strip_place(key_row):
    first = (GRID - 1 - key_row) * GRID
    return (first % LANES) // GRID, first // LANES * LANES


def widen(rows, height):
    fill = jnp.zeros((height - rows.shape[0], rows.shape[1]), rows.dtype)
    return jnp.concatenate([rows, fill], axis=0)


def build_permutation(place_ref, perm):
    length = perm.shape[0]

    def rows_of(i, carry):
        first = pl.multiple_of(i * BLOCK, BLOCK)
        spots = lax.broadcasted_iota(jnp.int32, (BLOCK, length), 0) + first
        hit = spots == place_ref[...]
        perm[pl.ds(first, BLOCK), :] = jnp.where(hit, 1.0, 0.0).astype(bf16)
        return carry

    lax.fori_loop(0, length // BLOCK, rows_of, 0)


def attend_kernel(
    head_size,
    x_ref,
    gain_ref,
    shift_ref,
    weight_ref,
    add_ref,
    place_ref,
    strips_ref,
    mixed_tok_ref,
    qkv_ref,
    expo_ref,
    inverse_ref,
    mixed_ref,
    hat_ref,
    perm,
    by_token,
    by_place,
    query_s,
    key_s,
    value_s,
    scores_s,
):
    head = pl.program_id(0)
    length = x_ref.shape[0]
    tiles = length // BLOCK
    group = mixed_ref.shape[0]
    scale = head_size ** (-0.5)

    @pl.when(head == 0)
    def _():
        build_permutation(place_ref, perm)

        def project(i, carry):
            span = pl.ds(pl.multiple_of(i * BLOCK, BLOCK), BLOCK)
            hat, _ = normalize(x_ref[span, :].astype(f32))
            hat_ref[span, :] = hat.astype(bf16)
            act = (hat * gain_ref[...] + shift_ref[...]).astype(bf16)
            part = dot(weight_ref[...], act, 1, 1) + add_ref[...]
            by_token[:group, span] = (part[:group] * scale).astype(bf16)
            by_token[group:, span] = part[group:].astype(bf16)
            return carry

        lax.fori_loop(0, tiles, project, 0)

        def arrange(i, carry):
            span = pl.ds(pl.multiple_of(i * BLOCK, BLOCK), BLOCK)
            part = dot(by_token[...], perm[span, :], 1, 1)
            by_place[:, span] = part
            qkv_ref[:, span] = part.astype(bf16)
            return carry

        lax.fori_loop(0, tiles, arrange, 0)

    def rows_of(which):
        first = pl.multiple_of(which * group + head * head_size, 8)
        return by_place[pl.ds(first, head_size), :]

    query_s[...] = widen(rows_of(0), LANES).astype(bf16)
    key_s[...] = jnp.transpose(widen(rows_of(1), LANES)).astype(bf16)
    value_s[...] = widen(rows_of(2), value_s.shape[0]).astype(bf16)
    own_rows = pl.ds(pl.multiple_of(head * head_size, 8), head_size)

    def tile(t, carry):
        first = pl.multiple_of(t * BLOCK, BLOCK)
        span = pl.ds(first, BLOCK)
        query = query_s[:, span]
        peak = jnp.full((8, BLOCK), -jnp.inf, f32)
        for c in range(tiles):
            keys = slice(c * BLOCK, (c + 1) * BLOCK)
            pieces = []
            for key_row in range(c * BLOCK // GRID, (c + 1) * BLOCK // GRID):
                shift, start = strip_place(key_row)
                pieces.append(strips_ref[0, shift, :, pl.ds(first + start, BLOCK)])
            scores = dot(key_s[keys, :], query) + jnp.concatenate(pieces, axis=0)
            scores_s[keys, :] = scores
            peak = jnp.maximum(peak, fold_rows(scores, jnp.max))
        peak = jnp.max(peak, axis=0, keepdims=True)
        total = jnp.zeros((8, BLOCK), f32)
        mixed = jnp.zeros((value_s.shape[0], BLOCK), f32)
        for c in range(tiles):
            keys = slice(c * BLOCK, (c + 1) * BLOCK)
            expo = jnp.exp(scores_s[keys, :] - peak)
            total = total + fold_rows(expo, jnp.sum)
            low = expo.astype(bf16)
            expo_ref[0, keys, span] = low
            mixed = mixed + dot(value_s[:, keys], low)
        inverse = 1.0 / jnp.sum(total, axis=0, keepdims=True)
        inverse_ref[0, :, span] = inverse
        mixed_ref[own_rows, span] = (mixed * inverse)[:head_size]
        return carry

    lax.fori_loop(0, tiles, tile, 0)

    @pl.when(head == pl.num_programs(0) - 1)
    def _():
        low = mixed_ref[...].astype(bf16)
        for b in range(tiles):
            mixed_tok_ref[b] = dot(low, perm[:, b * BLOCK : (b + 1) * BLOCK]).astype(bf16)


def attend_back_kernel(
    head_size,
    grad_ref,
    qkv_ref,
    expo_ref,
    inverse_ref,
    mixed_ref,
    place_ref,
    out_ref,
    strips_ref,
    perm,
    by_place,
    grad_place,
    grads,
    query_s,
    key_s,
    value_s,
    grad_s,
    grad_t,
    offset_s,
    grad_key,
    grad_value,
):
    head = pl.program_id(0)
    group, length = mixed_ref.shape
    tiles = length // BLOCK
    scale = head_size ** (-0.5)

    @pl.when(head == 0)
    def _():
        build_permutation(place_ref, perm)

        def arrange(i, carry):
            span = pl.ds(pl.multiple_of(i * BLOCK, BLOCK), BLOCK)
            part = jnp.zeros((group, BLOCK), f32)
            for b in range(tiles):
                part = part + dot(grad_ref[b], perm[span, b * BLOCK : (b + 1) * BLOCK], 1, 1)
            grad_place[:, span] = part
            by_place[:, span] = qkv_ref[:, span].astype(f32)
            return carry

        lax.fori_loop(0, tiles, arrange, 0)

    own_rows = pl.ds(pl.multiple_of(head * head_size, 8), head_size)

    def rows_of(which):
        first = pl.multiple_of(which * group + head * head_size, 8)
        return by_place[pl.ds(first, head_size), :]

    query_s[...] = jnp.transpose(widen(rows_of(0), LANES)).astype(bf16)
    key_s[...] = widen(rows_of(1), key_s.shape[0]).astype(bf16)
    value_s[...] = jnp.transpose(widen(rows_of(2), LANES)).astype(bf16)
    grad = grad_place[own_rows, :]
    inverse = inverse_ref[0]
    offset_s[...] = inverse * jnp.sum(grad * mixed_ref[own_rows, :], axis=0, keepdims=True)
    grad = widen(grad * inverse, LANES)
    grad_s[...] = grad.astype(bf16)
    grad_t[...] = jnp.transpose(grad).astype(bf16)
    grad_key[...] = jnp.zeros_like(grad_key)
    grad_value[...] = jnp.zeros_like(grad_value)
    strips_ref[...] = jnp.zeros_like(strips_ref)

    def tile(t, carry):
        first = pl.multiple_of(t * BLOCK, BLOCK)
        span = pl.ds(first, BLOCK)
        grad_tile = grad_s[:, span]
        offset = offset_s[:, span]
        grad_query = jnp.zeros((key_s.shape[0], BLOCK), f32)
        for c in range(tiles):
            keys = slice(c * BLOCK, (c + 1) * BLOCK)
            expo = expo_ref[0, keys, span]
            grad_scores = expo.astype(f32) * (dot(value_s[keys, :], grad_tile) - offset)
            for row in range(BLOCK // GRID):
                shift, start = strip_place(c * BLOCK // GRID + row)
                strips_ref[0, shift, :, pl.ds(first + start, BLOCK)] += grad_scores[
                    row * GRID : (row + 1) * GRID
                ]
            low = grad_scores.astype(bf16)
            grad_query = grad_query + dot(key_s[:, keys], low)
            grad_key[keys, :] += dot(low, query_s[span, :])
            grad_value[keys, :] += dot(expo, grad_t[span, :])
        grads[own_rows, span] = grad_query[:head_size] * scale
        return carry

    lax.fori_loop(0, tiles, tile, 0)
    for which, total in ((1, grad_key), (2, grad_value)):
        first = pl.multiple_of(which * group + head * head_size, 8)
        grads[pl.ds(first, head_size), :] = jnp.transpose(total[...])[:head_size]

    @pl.when(head == pl.num_programs(0) - 1)
    def _():
        low = grads[...].astype(bf16)
        for b in range(tiles):
            out_ref[b] = dot(low, perm[:, b * BLOCK : (b + 1) * BLOCK]).astype(bf16)


def mlp_kernel(
    mixed_ref,
    x_ref,
    dy_ref,
    w_out_ref,
    b_out_ref,
    gain_ref,
    shift_ref,
    b_down_ref,
    b_up_ref,
    w_up_ref,
    w_down_ref,
    result_ref,
    act_ref,
    inner_ref,
    norm_ref,
    middle_ref,
    branch_ref,
    grad_mixed_ref,
    sums_ref,
    up_sum_ref,
    middle_s,
    hat_s,
    scaled_s,
    result_s,
    grad_s,
):
    step = pl.program_id(0)

    @pl.when(step == 0)
    def _():
        mixed = jnp.transpose(mixed_ref[...])
        middle = x_ref[...].astype(f32) + dot(mixed, w_out_ref[...]) + b_out_ref[...]
        hat, scaled = normalize(middle)
        middle_s[...] = middle
        hat_s[...] = hat
        scaled_s[...] = scaled
        norm_ref[...] = (hat * gain_ref[...] + shift_ref[...]).astype(bf16)
        result_s[...] = jnp.zeros_like(result_s)
        grad_s[...] = jnp.zeros_like(grad_s)

    inner = dot(norm_ref[...], w_up_ref[...]) + b_up_ref[...]
    cdf = 0.5 * (1.0 + lax.erf(inner * (0.5**0.5)))
    pdf = jnp.exp(-0.5 * inner * inner) * 0.3989422804014327
    act = (inner * cdf).astype(bf16)
    grad_inner = dot(dy_ref[...], w_down_ref[...], 1, 1) * (cdf + inner * pdf)
    low = grad_inner.astype(bf16)
    act_ref[...] = jnp.transpose(act)
    inner_ref[...] = jnp.transpose(low)
    up_sum_ref[...] = jnp.sum(low.astype(f32), axis=0, keepdims=True)
    result_s[...] += dot(act, w_down_ref[...])
    grad_s[...] += dot(low, w_up_ref[...], 1, 1)

    @pl.when(step == pl.num_programs(0) - 1)
    def _():
        result_ref[...] = (middle_s[...] + result_s[...] + b_down_ref[...]).astype(bf16)
        dy = dy_ref[...].astype(f32)
        grad_norm, hat = grad_s[...], hat_s[...]
        grad_middle = dy + norm_back(grad_norm, hat, scaled_s[...], gain_ref[...])
        branch = grad_middle.astype(bf16)
        middle_ref[...] = grad_middle
        branch_ref[...] = branch
        grad_mixed_ref[...] = dot(w_out_ref[...], branch, 1, 1).astype(bf16)
        sums_ref[...] = jnp.zeros_like(sums_ref)
        sums_ref[0:1, :] = jnp.sum(dy, axis=0, keepdims=True)
        sums_ref[1:2, :] = jnp.sum(grad_norm * hat, axis=0, keepdims=True)
        sums_ref[2:3, :] = jnp.sum(grad_norm, axis=0, keepdims=True)
        sums_ref[3:4, :] = jnp.sum(branch.astype(f32), axis=0, keepdims=True)


def whole(shape):
    zeros = (0,) * len(shape)
    return pl.BlockSpec(shape, lambda s: zeros, pipeline_mode=pl.Buffered(1))


def kept(shape):
    zeros = (0,) * len(shape)
    return pl.BlockSpec(shape, lambda s: zeros)


def per_head(shape):
    rest = (0,) * (len(shape) - 1)
    return pl.BlockSpec((1,) + tuple(shape[1:]), lambda s: (s,) + rest)


def params():
    return pltpu.CompilerParams(
        dimension_semantics=("arbitrary",), vmem_limit_bytes=VMEM_LIMIT
    )


def shape_of(shape, kind):
    return jax.ShapeDtypeStruct(shape, kind)


def attend(x_all, gain, shift, weight, add, place, strips, head_size):
    length, width = x_all.shape
    heads = strips.shape[0]
    group = heads * head_size
    tall = -(-head_size // 16) * 16
    outs = (
        shape_of((length // BLOCK, group, BLOCK), bf16),
        shape_of((3 * group, length), bf16),
        shape_of((heads, length, length), bf16),
        shape_of((heads, 1, length), f32),
        shape_of((group, length), f32),
        shape_of((length, width), bf16),
    )
    return pl.pallas_call(
        partial(attend_kernel, head_size),
        grid=(heads,),
        in_specs=[whole(a.shape) for a in (x_all, gain, shift, weight, add, place)]
        + [per_head(strips.shape)],
        out_specs=[
            kept(outs[0].shape),
            kept(outs[1].shape),
            per_head(outs[2].shape),
            per_head(outs[3].shape),
            kept(outs[4].shape),
            kept(outs[5].shape),
        ],
        out_shape=outs,
        scratch_shapes=[
            pltpu.VMEM((length, length), bf16),
            pltpu.VMEM((3 * group, length), bf16),
            pltpu.VMEM((3 * group, length), f32),
            pltpu.VMEM((LANES, length), bf16),
            pltpu.VMEM((length, LANES), bf16),
            pltpu.VMEM((tall, length), bf16),
            pltpu.VMEM((length, BLOCK), f32),
        ],
        compiler_params=params(),
        name="attend",
    )(x_all, gain, shift, weight, add, place, strips)


def attend_back(grad_mixed, qkv, expo, inverse, mixed, place, head_size):
    heads, length, _ = expo.shape
    group = heads * head_size
    tall = -(-head_size // 16) * 16
    outs = (
        shape_of((length // BLOCK, 3 * group, BLOCK), bf16),
        shape_of((heads, LANES // GRID, GRID, STRIP), f32),
    )
    return pl.pallas_call(
        partial(attend_back_kernel, head_size),
        grid=(heads,),
        in_specs=[
            whole(grad_mixed.shape),
            whole(qkv.shape),
            per_head(expo.shape),
            per_head(inverse.shape),
            whole(mixed.shape),
            whole(place.shape),
        ],
        out_specs=[kept(outs[0].shape), per_head(outs[1].shape)],
        out_shape=outs,
        scratch_shapes=[
            pltpu.VMEM((length, length), bf16),
            pltpu.VMEM((3 * group, length), f32),
            pltpu.VMEM((group, length), f32),
            pltpu.VMEM((3 * group, length), f32),
            pltpu.VMEM((length, LANES), bf16),
            pltpu.VMEM((tall, length), bf16),
            pltpu.VMEM((length, LANES), bf16),
            pltpu.VMEM((LANES, length), bf16),
            pltpu.VMEM((length, LANES), bf16),
            pltpu.VMEM((1, length), f32),
            pltpu.VMEM((length, LANES), f32),
            pltpu.VMEM((length, LANES), f32),
        ],
        compiler_params=params(),
        name="attend_back",
    )(grad_mixed, qkv, expo, inverse, mixed, place)


def mlp(mixed, x, dy, w_out, b_out, gain, shift, b_down, b_up, w_up, w_down):
    rows, width = x.shape
    hidden = w_up.shape[1]
    step = 512
    outs = (
        shape_of((rows, width), bf16),
        shape_of((hidden, rows), bf16),
        shape_of((hidden, rows), bf16),
        shape_of((rows, width), bf16),
        shape_of((rows, width), f32),
        shape_of((rows, width), bf16),
        shape_of((width, rows), bf16),
        shape_of((8, width), f32),
        shape_of((1, hidden), f32),
    )
    down = pl.BlockSpec((step, rows), lambda s: (s, 0))
    return pl.pallas_call(
        mlp_kernel,
        grid=(hidden // step,),
        in_specs=[whole(a.shape) for a in (mixed, x, dy, w_out, b_out, gain, shift, b_down)]
        + [
            pl.BlockSpec((1, step), lambda s: (0, s)),
            pl.BlockSpec((width, step), lambda s: (0, s)),
            pl.BlockSpec((step, width), lambda s: (s, 0)),
        ],
        out_specs=[kept(outs[0].shape), down, down]
        + [kept(o.shape) for o in outs[3:8]]
        + [pl.BlockSpec((1, step), lambda s: (0, s))],
        out_shape=outs,
        scratch_shapes=[
            pltpu.VMEM((rows, width), f32),
            pltpu.VMEM((rows, width), f32),
            pltpu.VMEM((rows, 1), f32),
            pltpu.VMEM((rows, width), f32),
            pltpu.VMEM((rows, width), f32),
        ],
        compiler_params=params(),
        name="mlp",
    )(mixed, x, dy, w_out, b_out, gain, shift, b_down, b_up, w_up, w_down)


def key_places(rel_index):
    first = rel_index[0]
    top = jnp.max(first)
    row = top // SPAN - first // SPAN
    column = top % SPAN - first % SPAN
    return (row * GRID + column)[None, :].astype(jnp.int32)


def bias_strips(table):
    heads = table.shape[0]
    square = table.reshape(heads, SPAN, SPAN)
    strip = jnp.stack(
        [square[:, :, GRID - 1 - c : SPAN - c] for c in range(GRID)], axis=1
    ).reshape(heads, GRID, SPAN * GRID)
    strip = jnp.pad(strip, ((0, 0), (0, 0), (0, STRIP + LANES - SPAN * GRID)))
    return jnp.stack(
        [strip[:, :, s * GRID : s * GRID + STRIP] for s in range(LANES // GRID)], axis=1
    )


def table_grad(strips):
    heads = strips.shape[0]
    total = sum(
        jnp.pad(strips[:, s], ((0, 0), (0, 0), (s * GRID, LANES - s * GRID)))
        for s in range(LANES // GRID)
    )
    parts = total[:, :, : SPAN * GRID].reshape(heads, GRID, SPAN, GRID)
    sides = jnp.arange(GRID, dtype=jnp.int32)
    place = GRID - 1 - sides[:, None] + sides[None, :]
    onehot = (place[:, :, None] == jnp.arange(SPAN, dtype=jnp.int32)).astype(f32)
    return jnp.einsum("hjai,jib->hab", parts, onehot, precision=HIGHEST).reshape(
        heads, SPAN * SPAN
    )


def per_device(
    tokens,
    timesteps,
    rel_index,
    time_table,
    bias_table,
    gain_one,
    shift_one,
    w_query,
    w_key,
    w_value,
    t_query,
    t_value,
    b_query,
    b_value,
    w_out,
    b_out,
    gain_two,
    shift_two,
    w_up,
    b_up,
    w_down,
    b_down,
    cotangent,
):
    _, local, width = tokens.shape
    hidden = w_up.shape[1]
    heads = bias_table.shape[0]
    head_size = width // heads
    n_dp, n_seq = lax.axis_size("dp"), lax.axis_size("seq")
    dp, seq = lax.axis_index("dp"), lax.axis_index("seq")
    own_heads = heads // n_seq
    group = own_heads * head_size
    scale = head_size ** (-0.5)
    table_rows = time_table.shape[0]

    def own_columns(array):
        return lax.dynamic_slice_in_dim(array, seq * group, group, axis=array.ndim - 1)

    x = tokens[0]
    dy = cotangent[0]
    x_all = lax.all_gather(x, "seq", axis=0, tiled=True)
    dy_all = lax.all_gather(dy, "dp", axis=0)
    steps_all = lax.all_gather(timesteps, "dp", axis=0, tiled=True)

    place = key_places(rel_index)
    strips = bias_strips(lax.dynamic_slice_in_dim(bias_table, seq * own_heads, own_heads, 0))
    weight = jnp.concatenate([own_columns(w).T for w in (w_query, w_key, w_value)], axis=0)
    embed = lax.dynamic_slice_in_dim(time_table, timesteps[0], 1, 0)
    tq_own, tv_own = own_columns(t_query), own_columns(t_value)
    query_add = dot(embed, tq_own)[0] + own_columns(b_query)
    value_add = dot(embed, tv_own)[0] + own_columns(b_value)
    add = jnp.concatenate([query_add, jnp.zeros((group,), f32), value_add])[:, None]

    mixed_tok, qkv, expo, inverse, mixed, hat_one = attend(
        x_all, gain_one[None], shift_one[None], weight, add, place, strips, head_size
    )
    mixed_own = lax.all_to_all(mixed_tok, "seq", 0, 0).reshape(width, local)
    (
        result,
        act_t,
        inner_t,
        norm_two,
        grad_middle,
        branch,
        grad_mixed,
        sums_two,
        up_sum,
    ) = mlp(
        mixed_own,
        x,
        dy,
        w_out,
        b_out[None],
        gain_two[None],
        shift_two[None],
        b_down[None],
        b_up[None],
        w_up,
        w_down,
    )
    norm_all = lax.all_gather(norm_two, "dp", axis=0)
    branch_all = lax.all_gather(branch, "dp", axis=0)
    grad_heads = lax.all_to_all(grad_mixed.reshape(n_seq, group, local), "seq", 0, 0)

    down_rows, out_rows = hidden // n_dp, width // n_dp
    up_columns = hidden // n_dp // n_seq
    parts = jnp.concatenate(
        [
            act_t.reshape(n_dp, down_rows, local),
            jnp.swapaxes(inner_t.reshape(n_seq, n_dp, up_columns, local), 0, 1).reshape(
                n_dp, down_rows, local
            ),
            mixed_own.reshape(n_dp, out_rows, local),
        ],
        axis=1,
    )
    parts = lax.all_to_all(parts, "dp", 0, 0)

    def over_sources(left, right):
        return lax.dot_general(
            left, right, (((0, 2), (0, 1)), ((), ())), preferred_element_type=f32
        )

    part_down = over_sources(parts[:, :down_rows], dy_all)
    part_up = over_sources(parts[:, down_rows : 2 * down_rows], norm_all)
    part_out = over_sources(parts[:, 2 * down_rows :], branch_all)
    by_column = lax.psum_scatter(
        jnp.concatenate([part_down, part_out], axis=0).astype(bf16),
        "seq",
        scatter_dimension=1,
        tiled=True,
    ).astype(f32)
    grad_w_down, grad_w_out = by_column[:down_rows], by_column[down_rows:]
    up_t = lax.psum_scatter(
        part_up.astype(bf16).reshape(n_seq, up_columns, width), "seq", scatter_dimension=0
    )
    up_t = lax.all_to_all(
        up_t.reshape(up_columns, n_dp, out_rows), "dp", split_axis=1, concat_axis=0
    )
    grad_w_up = jnp.transpose(up_t.reshape(hidden // n_seq, out_rows)).astype(f32)

    grads, grad_strips = attend_back(
        grad_heads, qkv, expo, inverse, mixed, place, head_size
    )
    grads_all = lax.all_to_all(grads, "seq", 0, 0)
    product = lax.dot_general(
        hat_one.reshape(n_seq, local, width),
        grads,
        (((0, 1), (0, 2)), ((), ())),
        preferred_element_type=f32,
    )
    grad_sums = jnp.sum(grads.astype(f32), axis=(0, 2))
    weight_wide = weight.T.astype(f32)
    grad_gain_one = jnp.sum(product * weight_wide, axis=1)
    grad_shift_one = jnp.sum(weight_wide * grad_sums[None, :], axis=1)
    grad_qkv = gain_one[:, None] * product + shift_one[:, None] * grad_sums[None, :]
    grad_qkv = lax.psum_scatter(
        grad_qkv.astype(bf16), "dp", scatter_dimension=0, tiled=True
    ).astype(f32)

    pieces = grads_all.reshape(n_seq, 3, group, local)
    grad_norm_one = sum(
        lax.dot_general(
            pieces[:, which].reshape(width, local),
            w,
            (((0,), (1,)), ((), ())),
            preferred_element_type=f32,
        )
        for which, w in enumerate((w_query, w_key, w_value))
    )
    hat_local, scaled_local = normalize(x.astype(f32))
    grad_tokens = (
        grad_middle + norm_back(grad_norm_one, hat_local, scaled_local, gain_one)
    ).astype(bf16)

    query_sum, value_sum = grad_sums[:group], grad_sums[2 * group :]
    grad_embed = jnp.dot(tq_own.astype(f32), query_sum, precision=HIGHEST) + jnp.dot(
        tv_own.astype(f32), value_sum, precision=HIGHEST
    )
    own_image = lax.broadcasted_iota(jnp.int32, (n_dp, 1), 0) == dp

    def slot(row):
        return jnp.where(own_image, row[None, :], 0.0).reshape(-1)

    apart = [table_grad(grad_strips).reshape(-1), query_sum, value_sum]
    summed = [
        slot(grad_embed),
        up_sum[0],
        sums_two[:4].reshape(-1),
        grad_gain_one,
        grad_shift_one,
    ]
    images = [slot(jnp.concatenate([query_sum, value_sum]))]
    sizes = [sum(a.shape[0] for a in part) for part in (apart, summed, images)]
    vector = lax.psum(jnp.concatenate(apart + summed + images), "dp")
    image_sums = vector[sizes[0] + sizes[1] :].reshape(n_dp, 2 * group)
    vector = lax.all_gather(vector[: sizes[0] + sizes[1]], "seq", axis=0)
    table_size = own_heads * SPAN * SPAN
    grad_bias_table = vector[:, :table_size].reshape(heads, SPAN * SPAN)
    grad_b_query = vector[:, table_size : table_size + group].reshape(-1)
    grad_b_value = vector[:, table_size + group : sizes[0]].reshape(-1)
    both = jnp.sum(vector[:, sizes[0] :], axis=0)
    embed_size = n_dp * width
    embed_rows = both[:embed_size].reshape(n_dp, width)
    grad_b_up = both[embed_size : embed_size + hidden]
    rest = both[embed_size + hidden :].reshape(6, width)
    grad_b_down, grad_gain_two, grad_shift_two, grad_b_out, grad_gain_one, grad_shift_one = (
        rest[r] for r in range(6)
    )

    embeds = lax.dynamic_slice_in_dim(
        jnp.take(time_table, steps_all, axis=0), dp * out_rows, out_rows, axis=1
    ).astype(f32)
    grad_t_query = jnp.dot(embeds.T, image_sums[:, :group], precision=HIGHEST)
    grad_t_value = jnp.dot(embeds.T, image_sums[:, group:], precision=HIGHEST)
    onehot = (
        steps_all[:, None] == jnp.arange(table_rows, dtype=jnp.int32)[None, :]
    ).astype(f32)
    grad_time_table = jnp.dot(onehot.T, embed_rows, precision=HIGHEST)

    return (
        result[None],
        grad_tokens[None],
        grad_qkv[:, :group],
        grad_qkv[:, group : 2 * group],
        grad_qkv[:, 2 * group :],
        grad_t_query,
        grad_t_value,
        grad_w_out,
        grad_w_up,
        grad_w_down,
        grad_gain_one,
        grad_shift_one,
        grad_b_query,
        grad_b_value,
        grad_b_out,
        grad_gain_two,
        grad_shift_two,
        grad_b_up,
        grad_b_down,
        grad_bias_table,
        grad_time_table,
    )


def solution(mesh):
    split, copied, by_block = P("dp", "seq", None), P(), P("dp", "seq")
    in_specs = (split, P("dp"), P("seq", None)) + (copied,) * 19 + (split,)
    out_specs = (split, split) + (by_block,) * 8 + (copied,) * 11
    return jax.shard_map(
        per_device, mesh=mesh, in_specs=in_specs, out_specs=out_specs, check_vma=False
    )
```

```python
from functools import partial

import jax
import jax.numpy as jnp
from jax import lax
from jax.experimental import pallas as pl
from jax.experimental.pallas import tpu as pltpu
from jax.sharding import PartitionSpec as P

GRID = 32
SPAN = 2 * GRID - 1
STRIP = 2 * GRID * GRID
LANES = 128
BLOCK = 256
NORM_EPS = 1e-06
f32, bf16 = jnp.float32, jnp.bfloat16
GAIN_ONE, SHIFT_ONE, B_QUERY, B_VALUE, B_OUT, GAIN_TWO, SHIFT_TWO, B_DOWN = range(8)
HIGHEST = lax.Precision.HIGHEST
SCALE = 0.2
VMEM_LIMIT = 58 * 1024 * 1024


def dot(left, right, left_dim=1, right_dim=0):
    return lax.dot_general(
        left, right, (((left_dim,), (right_dim,)), ((), ())), preferred_element_type=f32
    )


def normalize(values):
    centered = values - jnp.mean(values, axis=-1, keepdims=True)
    scaled = lax.rsqrt(jnp.mean(centered * centered, axis=-1, keepdims=True) + NORM_EPS)
    return centered * scaled, scaled


def norm_back(grad_norm, normed, scaled, gain):
    inner = grad_norm * gain
    return scaled * (
        inner
        - jnp.mean(inner, axis=-1, keepdims=True)
        - normed * jnp.mean(inner * normed, axis=-1, keepdims=True)
    )


def fold_rows(values, op):
    return op(values.reshape(values.shape[0] // 8, 8, values.shape[1]), axis=0)


def strip_place(key_row):
    first = (GRID - 1 - key_row) * GRID
    return (first % LANES) // GRID, first // LANES * LANES


def widen(rows, height):
    fill = jnp.zeros((height - rows.shape[0], rows.shape[1]), rows.dtype)
    return jnp.concatenate([rows, fill], axis=0)


def rows_for(group, half, count):
    return pl.ds(pl.multiple_of((2 * group + half) * count, 16), count)


def block_of(index):
    return pl.ds(pl.multiple_of(index * BLOCK, BLOCK), BLOCK)


def build_permutation(place_ref, perm):
    length = perm.shape[0]

    def rows_of(i, carry):
        first = pl.multiple_of(i * BLOCK, BLOCK)
        spots = lax.broadcasted_iota(jnp.int32, (BLOCK, length), 0) + first
        hit = spots == place_ref[...]
        perm[pl.ds(first, BLOCK), :] = jnp.where(hit, 1.0, 0.0).astype(bf16)
        return carry

    lax.fori_loop(0, length // BLOCK, rows_of, 0)


def strips_kernel(table_ref, strips_ref):
    quarter = lax.broadcasted_iota(jnp.int32, (GRID, LANES), 1) // GRID
    per_tile = LANES // GRID

    def tile(n, carry):
        for s in range(per_tile):
            whole_tile = jnp.zeros((GRID, LANES), f32)
            for k in range(per_tile):
                row = table_ref[0, pl.ds(per_tile * n + s + k, 1), :]
                turned = pltpu.roll(
                    jnp.broadcast_to(row, (GRID, LANES)),
                    (GRID * k - GRID + 1) % LANES,
                    1,
                    stride=1,
                    stride_axis=0,
                )
                whole_tile = jnp.where(quarter == k, turned, whole_tile)
            strips_ref[0, s, :, pl.ds(pl.multiple_of(n * LANES, LANES), LANES)] = whole_tile
        return carry

    lax.fori_loop(0, STRIP // LANES, tile, 0)


def project_kernel(
    scale,
    groups,
    seq_ref,
    x_ref,
    embed_ref,
    rows_ref,
    wk_hbm,
    wq_hbm,
    tq_hbm,
    wv_hbm,
    tv_hbm,
    *refs,
):
    outs, (hat_ref, held, turned, sems) = refs[: 2 * groups], refs[2 * groups :]
    sources = (wk_hbm, wq_hbm, tq_hbm, wv_hbm, tv_hbm)
    copies = [
        pltpu.make_async_copy(source, held.at[n], sems.at[n]) for n, source in enumerate(sources)
    ]
    for copy in copies:
        copy.start()
    hat, _ = normalize(x_ref[...].astype(f32))
    hat_ref[...] = hat.astype(bf16)
    act = (hat * rows_ref[GAIN_ONE] + rows_ref[SHIFT_ONE]).astype(bf16)
    embed = jnp.broadcast_to(embed_ref[...].astype(f32), (16, embed_ref.shape[1])).astype(bf16)
    count = outs[0].shape[0] // 3
    seq = seq_ref[0]

    def put(which, value):
        turned[which] = jnp.transpose(value.astype(bf16))
        for k in range(groups):
            for h in range(2):
                outs[h * groups + k][which * count : (which + 1) * count, :] = turned[
                    which, rows_for(k ^ seq, h, count), :
                ]

    copies[0].wait()
    put(1, dot(act, held[0]))
    copies[1].wait()
    copies[2].wait()
    time_query = dot(embed, held[2])[0:1]
    put(0, (dot(act, held[1]) + time_query + rows_ref[B_QUERY]) * scale)
    copies[3].wait()
    copies[4].wait()
    time_value = dot(embed, held[4])[0:1]
    put(2, dot(act, held[3]) + time_value + rows_ref[B_VALUE])


def attend_kernel(
    head_size,
    groups,
    seq_ref,
    place_ref,
    strips_ref,
    *refs,
):
    own, outs = refs[:groups], refs[groups : 2 * groups]
    qkv_ref, expo_ref, inverse_ref, mixed_ref = refs[2 * groups : 2 * groups + 4]
    perm, by_place, query_s, key_s, value_s, scores_s = refs[2 * groups + 4 :]
    seq = seq_ref[0]
    head = pl.program_id(0)
    group, length = mixed_ref.shape
    tiles = length // BLOCK

    @pl.when(head == 0)
    def _():
        build_permutation(place_ref, perm)

        def arrange(i, carry):
            span = pl.ds(pl.multiple_of(i * BLOCK, BLOCK), BLOCK)
            part = jnp.zeros((3 * group, BLOCK), f32)
            for k in range(groups):
                part = part + dot(own[k][...], perm[span, block_of(k ^ seq)], 1, 1)
            by_place[:, span] = part
            qkv_ref[:, span] = part.astype(bf16)
            return carry

        lax.fori_loop(0, tiles, arrange, 0)

    def rows_of(which):
        first = pl.multiple_of(which * group + head * head_size, 8)
        return by_place[pl.ds(first, head_size), :]

    query_s[...] = widen(rows_of(0), LANES).astype(bf16)
    key_s[...] = jnp.transpose(widen(rows_of(1), LANES)).astype(bf16)
    value_s[...] = widen(rows_of(2), value_s.shape[0]).astype(bf16)
    own_rows = pl.ds(pl.multiple_of(head * head_size, 8), head_size)

    def tile(t, carry):
        first = pl.multiple_of(t * BLOCK, BLOCK)
        span = pl.ds(first, BLOCK)
        query = query_s[:, span]
        peak = jnp.full((8, BLOCK), -jnp.inf, f32)
        for c in range(tiles):
            keys = slice(c * BLOCK, (c + 1) * BLOCK)
            pieces = []
            for key_row in range(c * BLOCK // GRID, (c + 1) * BLOCK // GRID):
                shift, start = strip_place(key_row)
                pieces.append(strips_ref[0, shift, :, pl.ds(first + start, BLOCK)])
            scores = dot(key_s[keys, :], query) + jnp.concatenate(pieces, axis=0)
            scores_s[keys, :] = scores
            peak = jnp.maximum(peak, fold_rows(scores, jnp.max))
        peak = jnp.max(peak, axis=0, keepdims=True)
        total = jnp.zeros((8, BLOCK), f32)
        mixed = jnp.zeros((value_s.shape[0], BLOCK), f32)
        for c in range(tiles):
            keys = slice(c * BLOCK, (c + 1) * BLOCK)
            expo = jnp.exp(scores_s[keys, :] - peak)
            total = total + fold_rows(expo, jnp.sum)
            low = expo.astype(bf16)
            expo_ref[0, keys, span] = low
            mixed = mixed + dot(value_s[:, keys], low)
        inverse = 1.0 / jnp.sum(total, axis=0, keepdims=True)
        inverse_ref[0, :, span] = inverse
        mixed_ref[own_rows, span] = (mixed * inverse)[:head_size]
        return carry

    lax.fori_loop(0, tiles, tile, 0)

    @pl.when(head == pl.num_programs(0) - 1)
    def _():
        low = mixed_ref[...].astype(bf16)
        for k in range(groups):
            outs[k][...] = dot(low, perm[:, block_of(k ^ seq)]).astype(bf16)


def attend_back_kernel(
    head_size,
    groups,
    seq_ref,
    qkv_ref,
    expo_ref,
    inverse_ref,
    mixed_ref,
    place_ref,
    *refs,
):
    given, outs = refs[:groups], refs[groups : 2 * groups]
    (
        strips_ref,
        perm,
        by_place,
        grad_place,
        grads,
        query_s,
        key_s,
        value_s,
        grad_s,
        grad_t,
        offset_s,
        grad_key,
        grad_value,
    ) = refs[2 * groups :]
    seq = seq_ref[0]
    head = pl.program_id(0)
    group, length = mixed_ref.shape
    tiles = length // BLOCK
    scale = head_size ** (-0.5)

    @pl.when(head == 0)
    def _():
        build_permutation(place_ref, perm)

        def arrange(i, carry):
            span = pl.ds(pl.multiple_of(i * BLOCK, BLOCK), BLOCK)
            part = jnp.zeros((group, BLOCK), f32)
            for k in range(groups):
                part = part + dot(given[k][...], perm[span, block_of(k ^ seq)], 1, 1)
            grad_place[:, span] = part
            by_place[:, span] = qkv_ref[:, span].astype(f32)
            return carry

        lax.fori_loop(0, tiles, arrange, 0)

    own_rows = pl.ds(pl.multiple_of(head * head_size, 8), head_size)

    def rows_of(which):
        first = pl.multiple_of(which * group + head * head_size, 8)
        return by_place[pl.ds(first, head_size), :]

    query_s[...] = jnp.transpose(widen(rows_of(0), LANES)).astype(bf16)
    key_s[...] = widen(rows_of(1), key_s.shape[0]).astype(bf16)
    value_s[...] = jnp.transpose(widen(rows_of(2), LANES)).astype(bf16)
    grad = grad_place[own_rows, :]
    inverse = inverse_ref[0]
    offset_s[...] = inverse * jnp.sum(grad * mixed_ref[own_rows, :], axis=0, keepdims=True)
    grad = widen(grad * inverse, LANES)
    grad_s[...] = grad.astype(bf16)
    grad_t[...] = jnp.transpose(grad).astype(bf16)
    grad_key[...] = jnp.zeros_like(grad_key)
    grad_value[...] = jnp.zeros_like(grad_value)
    strips_ref[...] = jnp.zeros_like(strips_ref)

    def tile(t, carry):
        first = pl.multiple_of(t * BLOCK, BLOCK)
        span = pl.ds(first, BLOCK)
        grad_tile = grad_s[:, span]
        offset = offset_s[:, span]
        grad_query = jnp.zeros((key_s.shape[0], BLOCK), f32)
        for c in range(tiles):
            keys = slice(c * BLOCK, (c + 1) * BLOCK)
            expo = expo_ref[0, keys, span]
            grad_scores = expo.astype(f32) * (dot(value_s[keys, :], grad_tile) - offset)
            for row in range(BLOCK // GRID):
                shift, start = strip_place(c * BLOCK // GRID + row)
                strips_ref[0, shift, :, pl.ds(first + start, BLOCK)] += grad_scores[
                    row * GRID : (row + 1) * GRID
                ]
            low = grad_scores.astype(bf16)
            grad_query = grad_query + dot(key_s[:, keys], low)
            grad_key[keys, :] += dot(low, query_s[span, :])
            grad_value[keys, :] += dot(expo, grad_t[span, :])
        grads[own_rows, span] = grad_query[:head_size] * scale
        return carry

    lax.fori_loop(0, tiles, tile, 0)
    for which, total in ((1, grad_key), (2, grad_value)):
        first = pl.multiple_of(which * group + head * head_size, 8)
        grads[pl.ds(first, head_size), :] = jnp.transpose(total[...])[:head_size]

    @pl.when(head == pl.num_programs(0) - 1)
    def _():
        low = grads[...].astype(bf16)
        for k in range(groups):
            outs[k][...] = dot(low, perm[:, block_of(k ^ seq)]).astype(bf16)


def mlp_first_kernel(
    groups,
    step,
    seq_ref,
    x_ref,
    dy_ref,
    rows_ref,
    b_up_ref,
    w_out_hbm,
    w_up_hbm,
    w_down_hbm,
    *refs,
):
    given = refs[: 2 * groups]
    act_hbm, act_t_hbm, inner_hbm, norm_t_ref, mixed_t_ref, middle_ref, up_sum_ref = refs[
        2 * groups : 2 * groups + 7
    ]
    (
        w_out_s,
        w_up_s,
        w_down_s,
        act_s,
        act_t_s,
        inner_s,
        norm_s,
        sem,
        up_sems,
        down_sems,
        act_sems,
        act_t_sems,
        inner_sems,
    ) = refs[2 * groups + 7 :]
    chunks = w_up_s.shape[0]
    seq = seq_ref[0]

    def span_of(i):
        return pl.ds(pl.multiple_of(i * step, step), step)

    def fetch(i):
        return (
            pltpu.make_async_copy(w_up_hbm.at[:, span_of(i)], w_up_s.at[i], up_sems.at[i]),
            pltpu.make_async_copy(w_down_hbm.at[span_of(i), :], w_down_s.at[i], down_sems.at[i]),
        )

    def put(i):
        return (
            pltpu.make_async_copy(act_s.at[i], act_hbm.at[:, span_of(i)], act_sems.at[i]),
            pltpu.make_async_copy(act_t_s.at[i], act_t_hbm.at[span_of(i), :], act_t_sems.at[i]),
            pltpu.make_async_copy(inner_s.at[i], inner_hbm.at[:, span_of(i)], inner_sems.at[i]),
        )

    def begin(i, carry):
        for copy in fetch(i):
            copy.start()
        return carry

    out_copy = pltpu.make_async_copy(w_out_hbm, w_out_s, sem.at[0])
    out_copy.start()
    lax.fori_loop(0, chunks, begin, 0)
    count = given[0].shape[0]
    for k in range(groups):
        for h in range(2):
            mixed_t_ref[rows_for(k ^ seq, h, count), :] = given[h * groups + k][...]
    mixed = jnp.transpose(mixed_t_ref[...])
    out_copy.wait()
    middle = x_ref[...].astype(f32) + dot(mixed, w_out_s[...]) + rows_ref[B_OUT]
    hat, _ = normalize(middle)
    middle_ref[...] = middle
    norm = (hat * rows_ref[GAIN_TWO] + rows_ref[SHIFT_TWO]).astype(bf16)
    norm_s[...] = norm
    norm_t_ref[...] = jnp.transpose(norm)

    def chunk(i, carry):
        for copy in fetch(i):
            copy.wait()
        inner = dot(norm_s[...], w_up_s[i]) + b_up_ref[:, span_of(i)]
        cdf = 0.5 * (1.0 + lax.erf(inner * (0.5**0.5)))
        pdf = jnp.exp(-0.5 * inner * inner) * 0.3989422804014327
        act = (inner * cdf).astype(bf16)
        low = (dot(dy_ref[...], w_down_s[i], 1, 1) * (cdf + inner * pdf)).astype(bf16)
        act_s[i] = act
        act_t_s[i] = jnp.transpose(act)
        inner_s[i] = low
        up_sum_ref[:, span_of(i)] = jnp.sum(low.astype(f32), axis=0, keepdims=True)
        for copy in put(i):
            copy.start()
        return carry

    lax.fori_loop(0, chunks, chunk, 0)

    def finish(i, carry):
        for copy in put(i):
            copy.wait()
        return carry

    lax.fori_loop(0, chunks, finish, 0)


def mlp_second_kernel(
    groups,
    step,
    seq_ref,
    middle_ref,
    dy_ref,
    rows_ref,
    act_ref,
    inner_ref,
    w_out_hbm,
    w_up_hbm,
    w_down_hbm,
    *refs,
):
    outs = refs[: 2 * groups]
    result_ref, grad_middle_ref, branch_ref, sums_ref = refs[2 * groups : 2 * groups + 4]
    (
        w_out_s,
        w_up_s,
        w_down_s,
        result_s,
        grad_s,
        mixed_s,
        sem,
        up_sems,
        down_sems,
    ) = refs[2 * groups + 4 :]
    chunks = w_up_s.shape[0]
    seq = seq_ref[0]

    def span_of(i):
        return pl.ds(pl.multiple_of(i * step, step), step)

    def fetch(i):
        return (
            pltpu.make_async_copy(w_up_hbm.at[:, span_of(i)], w_up_s.at[i], up_sems.at[i]),
            pltpu.make_async_copy(w_down_hbm.at[span_of(i), :], w_down_s.at[i], down_sems.at[i]),
        )

    def begin(i, carry):
        for copy in fetch(i):
            copy.start()
        return carry

    lax.fori_loop(0, chunks, begin, 0)
    out_copy = pltpu.make_async_copy(w_out_hbm, w_out_s, sem.at[0])
    out_copy.start()
    result_s[...] = middle_ref[...] + rows_ref[B_DOWN]
    grad_s[...] = jnp.zeros_like(grad_s)

    def chunk(i, carry):
        for copy in fetch(i):
            copy.wait()
        result_s[...] += dot(act_ref[:, span_of(i)], w_down_s[i])
        grad_s[...] += dot(inner_ref[:, span_of(i)], w_up_s[i], 1, 1)
        return carry

    lax.fori_loop(0, chunks, chunk, 0)
    result_ref[...] = result_s[...].astype(bf16)
    hat, scaled = normalize(middle_ref[...])
    dy = dy_ref[...].astype(f32)
    grad_norm = grad_s[...]
    grad_middle = dy + norm_back(grad_norm, hat, scaled, rows_ref[GAIN_TWO])
    branch = grad_middle.astype(bf16)
    grad_middle_ref[...] = grad_middle
    branch_ref[...] = branch
    out_copy.wait()
    mixed_s[...] = dot(w_out_s[...], branch, 1, 1).astype(bf16)
    count = outs[0].shape[0]
    for k in range(groups):
        for h in range(2):
            outs[h * groups + k][...] = mixed_s[rows_for(k ^ seq, h, count), :]
    sums_ref[...] = jnp.concatenate(
        [
            jnp.sum(dy, axis=0, keepdims=True),
            jnp.sum(grad_norm * hat, axis=0, keepdims=True),
            jnp.sum(grad_norm, axis=0, keepdims=True),
            jnp.sum(branch.astype(f32), axis=0, keepdims=True),
            jnp.zeros((4, dy.shape[1]), f32),
        ],
        axis=0,
    )


def up_grad_kernel(
    order_ref, own_ref, other_ref, inner_ref, inner_other, keep_0, send_0, keep_1, send_1
):
    step = pl.program_id(0)
    total = dot(own_ref[0], inner_ref[...]) + dot(other_ref[0], inner_other[...])
    low = total.astype(bf16)
    half = low.shape[0] // 2
    first = step < pl.num_programs(0) // 2

    @pl.when(first)
    def _():
        keep_0[0], send_0[0] = low[:half], low[half:]

    @pl.when(jnp.logical_not(first))
    def _():
        keep_1[0], send_1[0] = low[:half], low[half:]


def down_grad_kernel(act_ref, dy_ref, out_ref, total_s):
    source = pl.program_id(0)
    part = dot(act_ref[0], dy_ref[0])

    @pl.when(source == 0)
    def _():
        total_s[...] = part

    @pl.when(source > 0)
    def _():
        total_s[...] += part

    @pl.when(source == pl.num_programs(0) - 1)
    def _():
        out_ref[...] = jnp.transpose(total_s[...].astype(bf16))


def qkv_grad_kernel(groups, seq_ref, hat_ref, weight_ref, rows_ref, *refs):
    given, (out_ref, sums_ref, norms_ref) = refs[: 2 * groups], refs[2 * groups :]
    seq = seq_ref[0]
    count = given[0].shape[0]
    gain, shift = rows_ref[GAIN_ONE], rows_ref[SHIFT_ONE]
    norms = jnp.zeros(norms_ref.shape, f32)
    for h in range(2):
        span = slice(h * count, (h + 1) * count)
        product = jnp.zeros((count, hat_ref.shape[2]), f32)
        sums = jnp.zeros((count, 1), f32)
        for k in range(groups):
            grads = given[h * groups + k][...]
            product = product + dot(grads, hat_ref[k ^ seq])
            sums = sums + jnp.sum(grads.astype(f32), axis=1, keepdims=True)
        weight = weight_ref[span, :].astype(f32)
        norms = norms + jnp.concatenate(
            [
                jnp.sum(weight * product, axis=0, keepdims=True),
                jnp.sum(weight * sums, axis=0, keepdims=True),
                jnp.zeros((6, weight.shape[1]), f32),
            ],
            axis=0,
        )
        sums_ref[span, :] = sums
        out_ref[h] = jnp.transpose((product * gain + sums * shift).astype(bf16))
    norms_ref[...] = norms


def tokens_kernel(groups, seq_ref, x_ref, middle_ref, rows_ref, wq_hbm, wk_hbm, wv_hbm, *refs):
    given, (out_ref, held, grads_s, sems) = refs[: 2 * groups], refs[2 * groups :]
    copies = [
        pltpu.make_async_copy(source, held.at[n], sems.at[n])
        for n, source in enumerate((wq_hbm, wk_hbm, wv_hbm))
    ]
    for copy in copies:
        copy.start()
    seq = seq_ref[0]
    count = given[0].shape[0] // 3
    for k in range(groups):
        for h in range(2):
            for which in range(3):
                grads_s[which, rows_for(k ^ seq, h, count), :] = given[h * groups + k][
                    which * count : (which + 1) * count
                ]
    hat, scaled = normalize(x_ref[...].astype(f32))
    total = jnp.zeros(middle_ref.shape, f32)
    for which, copy in enumerate(copies):
        grads = jnp.transpose(grads_s[which])
        copy.wait()
        total = total + dot(grads, held[which], 1, 1)
    out_ref[...] = (
        middle_ref[...] + norm_back(total, hat, scaled, rows_ref[GAIN_ONE])
    ).astype(bf16)


def whole(shape):
    zeros = (0,) * len(shape)
    return pl.BlockSpec(shape, lambda s: zeros, pipeline_mode=pl.Buffered(1))


def kept(shape):
    zeros = (0,) * len(shape)
    return pl.BlockSpec(shape, lambda s: zeros)


def per_head(shape):
    rest = (0,) * (len(shape) - 1)
    return pl.BlockSpec((1,) + tuple(shape[1:]), lambda s: (s,) + rest)


def params(grid=True):
    return pltpu.CompilerParams(
        dimension_semantics=("arbitrary",) if grid else None, vmem_limit_bytes=VMEM_LIMIT
    )


def takes(microseconds):
    return pl.CostEstimate(
        flops=int(microseconds * SCALE * 1e9), bytes_accessed=int(microseconds * SCALE * 3e6), transcendentals=0
    )


IN_VMEM = pl.BlockSpec(memory_space=pltpu.VMEM)
IN_SMEM = pl.BlockSpec(memory_space=pltpu.SMEM)
IN_HBM = pl.BlockSpec(memory_space=pl.ANY)


def shape_of(shape, kind):
    return jax.ShapeDtypeStruct(shape, kind)


def bias_strips(table):
    heads = table.shape[0]
    out = shape_of((heads, LANES // GRID, GRID, STRIP), f32)
    return pl.pallas_call(
        strips_kernel,
        grid=(heads,),
        in_specs=[per_head(table.shape)],
        out_specs=per_head(out.shape),
        out_shape=out,
        compiler_params=params(),
        cost_estimate=takes(9),
        name="strips",
    )(table)


def project(seq, x, embed, rows, weights, groups, scale):
    count, width = x.shape
    part = shape_of((3 * width // groups // 2, count), bf16)
    outs = pl.pallas_call(
        partial(project_kernel, scale, groups),
        in_specs=[IN_SMEM] + [IN_VMEM] * 3 + [IN_HBM] * 5,
        out_specs=[IN_VMEM] * (2 * groups + 1),
        out_shape=(part,) * (2 * groups) + (shape_of((count, width), bf16),),
        scratch_shapes=[
            pltpu.VMEM((5, width, width), bf16),
            pltpu.VMEM((3, width, count), bf16),
            pltpu.SemaphoreType.DMA((5,)),
        ],
        compiler_params=params(False),
        cost_estimate=takes(9),
        name="project",
    )(seq, x, embed, rows, *weights)
    return outs[:groups], outs[groups : 2 * groups], outs[2 * groups]


def attend(seq, own, place, strips, half, head_size):
    heads = strips.shape[0] // 2
    length = place.shape[1]
    group = heads * head_size
    groups = len(own)
    tall = -(-head_size // 16) * 16
    saved = (
        shape_of((3 * group, length), bf16),
        shape_of((heads, length, length), bf16),
        shape_of((heads, 1, length), f32),
        shape_of((group, length), f32),
    )
    own_strips = pl.BlockSpec(
        (1,) + strips.shape[1:], lambda s: (half * heads + s, 0, 0, 0)
    )
    outs = pl.pallas_call(
        partial(attend_kernel, head_size, groups),
        grid=(heads,),
        in_specs=[IN_SMEM, whole(place.shape), own_strips] + [whole(a.shape) for a in own],
        out_specs=[kept((group, BLOCK))] * groups
        + [
            kept(saved[0].shape),
            per_head(saved[1].shape),
            per_head(saved[2].shape),
            kept(saved[3].shape),
        ],
        out_shape=(shape_of((group, BLOCK), bf16),) * groups + saved,
        scratch_shapes=[
            pltpu.VMEM((length, length), bf16),
            pltpu.VMEM((3 * group, length), f32),
            pltpu.VMEM((LANES, length), bf16),
            pltpu.VMEM((length, LANES), bf16),
            pltpu.VMEM((tall, length), bf16),
            pltpu.VMEM((length, BLOCK), f32),
        ],
        compiler_params=params(),
        cost_estimate=takes(13),
        name="attend",
    )(seq, place, strips, *own)
    return outs[:groups], outs[groups:]


def attend_back(seq, grad_mixed, qkv, expo, inverse, mixed, place, head_size):
    heads, length, _ = expo.shape
    group = heads * head_size
    groups = len(grad_mixed)
    tall = -(-head_size // 16) * 16
    strips = shape_of((heads, LANES // GRID, GRID, STRIP), f32)
    outs = pl.pallas_call(
        partial(attend_back_kernel, head_size, groups),
        grid=(heads,),
        in_specs=[
            IN_SMEM,
            whole(qkv.shape),
            per_head(expo.shape),
            per_head(inverse.shape),
            whole(mixed.shape),
            whole(place.shape),
        ]
        + [whole(a.shape) for a in grad_mixed],
        out_specs=[kept((3 * group, BLOCK))] * groups + [per_head(strips.shape)],
        out_shape=(shape_of((3 * group, BLOCK), bf16),) * groups + (strips,),
        scratch_shapes=[
            pltpu.VMEM((length, length), bf16),
            pltpu.VMEM((3 * group, length), f32),
            pltpu.VMEM((group, length), f32),
            pltpu.VMEM((3 * group, length), f32),
            pltpu.VMEM((length, LANES), bf16),
            pltpu.VMEM((tall, length), bf16),
            pltpu.VMEM((length, LANES), bf16),
            pltpu.VMEM((LANES, length), bf16),
            pltpu.VMEM((length, LANES), bf16),
            pltpu.VMEM((1, length), f32),
            pltpu.VMEM((length, LANES), f32),
            pltpu.VMEM((length, LANES), f32),
        ],
        compiler_params=params(),
        cost_estimate=takes(16),
        name="attend_back",
    )(seq, qkv, expo, inverse, mixed, place, *grad_mixed)
    return outs[:groups], outs[groups]


def mlp_first(seq, mixed, x, dy, rows, b_up, w_out, w_up, w_down):
    count, width = x.shape
    hidden = w_up.shape[1]
    step = 512
    chunks = hidden // step
    dma = pltpu.SemaphoreType.DMA
    return pl.pallas_call(
        partial(mlp_first_kernel, len(mixed) // 2, step),
        in_specs=[IN_SMEM] + [IN_VMEM] * 4 + [IN_HBM] * 3 + [IN_VMEM] * len(mixed),
        out_specs=[IN_HBM] * 3 + [IN_VMEM] * 4,
        out_shape=(
            shape_of((count, hidden), bf16),
            shape_of((hidden, count), bf16),
            shape_of((count, hidden), bf16),
            shape_of((width, count), bf16),
            shape_of((width, count), bf16),
            shape_of((count, width), f32),
            shape_of((1, hidden), f32),
        ),
        scratch_shapes=[
            pltpu.VMEM((width, width), bf16),
            pltpu.VMEM((chunks, width, step), bf16),
            pltpu.VMEM((chunks, step, width), bf16),
            pltpu.VMEM((chunks, count, step), bf16),
            pltpu.VMEM((chunks, step, count), bf16),
            pltpu.VMEM((chunks, count, step), bf16),
            pltpu.VMEM((count, width), bf16),
            dma((1,)),
        ]
        + [dma((chunks,))] * 5,
        compiler_params=params(False),
        cost_estimate=takes(14),
        name="mlp_first",
    )(seq, x, dy, rows, b_up, w_out, w_up, w_down, *mixed)


def mlp_second(seq, middle, dy, rows, act, inner, w_out, w_up, w_down, groups):
    count, width = middle.shape
    hidden = w_up.shape[1]
    step = 512
    chunks = hidden // step
    part = shape_of((width // groups // 2, count), bf16)
    dma = pltpu.SemaphoreType.DMA
    outs = pl.pallas_call(
        partial(mlp_second_kernel, groups, step),
        in_specs=[IN_SMEM] + [IN_VMEM] * 5 + [IN_HBM] * 3,
        out_specs=[IN_VMEM] * (2 * groups + 4),
        out_shape=(part,) * (2 * groups)
        + (
            shape_of((count, width), bf16),
            shape_of((count, width), f32),
            shape_of((count, width), bf16),
            shape_of((8, width), f32),
        ),
        scratch_shapes=[
            pltpu.VMEM((width, width), bf16),
            pltpu.VMEM((chunks, width, step), bf16),
            pltpu.VMEM((chunks, step, width), bf16),
            pltpu.VMEM((count, width), f32),
            pltpu.VMEM((count, width), f32),
            pltpu.VMEM((width, count), bf16),
            dma((1,)),
            dma((chunks,)),
            dma((chunks,)),
        ],
        compiler_params=params(False),
        cost_estimate=takes(14),
        name="mlp_second",
    )(seq, middle, dy, rows, act, inner, w_out, w_up, w_down)
    return outs[:groups], outs[groups : 2 * groups], outs[2 * groups :]


def up_grad(order, own, other, inner, inner_other):
    _, rows, count = own.shape
    groups = order.shape[0]
    width = inner.shape[1] // groups
    side = groups // 2
    wide = pl.BlockSpec((count, width), lambda s, order_ref: (0, order_ref[s]))
    left = pl.BlockSpec((1, rows, count), lambda s, order_ref: (s // side, 0, 0))
    block = (1, rows // 2, width)
    early = pl.BlockSpec(block, lambda s, order_ref: (jnp.minimum(s, side - 1), 0, 0))
    late = pl.BlockSpec(block, lambda s, order_ref: (jnp.maximum(s - side, 0), 0, 0))
    return pl.pallas_call(
        up_grad_kernel,
        grid_spec=pltpu.PrefetchScalarGridSpec(
            num_scalar_prefetch=1,
            grid=(groups,),
            in_specs=[left, left, wide, wide],
            out_specs=[early, early, late, late],
        ),
        out_shape=(shape_of((side, rows // 2, width), bf16),) * 4,
        compiler_params=params(),
        cost_estimate=takes(8),
        name="up_grad",
    )(order, own, other, inner, inner_other)


def down_grad(act, dy):
    sources, rows, _ = act.shape
    width = dy.shape[2]
    return pl.pallas_call(
        down_grad_kernel,
        grid=(sources,),
        in_specs=[per_head(act.shape), per_head(dy.shape)],
        out_specs=kept((width, rows)),
        out_shape=shape_of((width, rows), bf16),
        scratch_shapes=[pltpu.VMEM((rows, width), f32)],
        compiler_params=params(),
        cost_estimate=takes(8),
        name="down_grad",
    )(act, dy)


def qkv_grad(seq, grads, hat, weight, rows):
    count, width = weight.shape
    return pl.pallas_call(
        partial(qkv_grad_kernel, len(grads) // 2),
        in_specs=[IN_SMEM] + [IN_VMEM] * (3 + len(grads)),
        out_specs=[IN_VMEM] * 3,
        out_shape=(
            shape_of((2, width, count // 2), bf16),
            shape_of((count, 1), f32),
            shape_of((8, width), f32),
        ),
        compiler_params=params(False),
        cost_estimate=takes(9),
        name="qkv_grad",
    )(seq, hat, weight, rows, *grads)


def token_grad(seq, grads, x, middle, rows, weights):
    count, width = x.shape
    return pl.pallas_call(
        partial(tokens_kernel, len(grads) // 2),
        in_specs=[IN_SMEM] + [IN_VMEM] * 3 + [IN_HBM] * 3 + [IN_VMEM] * len(grads),
        out_specs=IN_VMEM,
        out_shape=shape_of((count, width), bf16),
        scratch_shapes=[
            pltpu.VMEM((3, width, width), bf16),
            pltpu.VMEM((3, width, count), bf16),
            pltpu.SemaphoreType.DMA((3,)),
        ],
        compiler_params=params(False),
        cost_estimate=takes(9),
        name="token_grad",
    )(seq, x, middle, rows, *weights, *grads)


def exchange(array, axis, step):
    size = lax.axis_size(axis)
    return lax.ppermute(array, axis, [(i, i ^ step) for i in range(size)])


def sum_over(vector, axis):
    step = 1
    while step < lax.axis_size(axis):
        vector = vector + exchange(vector, axis, step)
        step *= 2
    return vector


def gather_rows(vector, axis):
    size, index = lax.axis_size(axis), lax.axis_index(axis)
    rows = vector[None]
    step = 1
    while step < size:
        rows = jnp.concatenate([rows, exchange(rows, axis, step)], axis=0)
        step *= 2
    return jnp.concatenate(
        [lax.dynamic_index_in_dim(rows, n ^ index, 0) for n in range(size)], axis=0
    )


def swap(parts, axis):
    return [parts[0]] + [exchange(parts[k], axis, k) for k in range(1, len(parts))]


def halve(array, axis, dim, step, bit):
    keep = lax.dynamic_index_in_dim(array, bit, dim, keepdims=False)
    send = lax.dynamic_index_in_dim(array, 1 - bit, dim, keepdims=False)
    return (keep.astype(f32) + exchange(send, axis, step).astype(f32)).astype(bf16)


def halve_bits(array, dim, bits, order):
    index = lax.axis_index("dp")
    left = sorted(bits, reverse=True)
    for bit in order:
        array = halve(array, "dp", dim + left.index(bit), 1 << bit, (index >> bit) & 1)
        left.remove(bit)
    return array


def add_low(left, right):
    return (left.astype(f32) + right.astype(f32)).astype(bf16)


def two_halves(keep, received, dim):
    size = keep.shape[dim] // 2
    return [
        add_low(*(lax.slice_in_dim(a, n * size, (n + 1) * size, axis=dim) for a in (keep, received)))
        for n in range(2)
    ]


def tie(*arrays):
    return lax.optimization_barrier(arrays)


def key_places(rel_index):
    first = rel_index[0]
    top = jnp.max(first)
    row = top // SPAN - first // SPAN
    column = top % SPAN - first % SPAN
    return (row * GRID + column)[None, :].astype(jnp.int32)


def table_grad(strips):
    heads = strips.shape[0]
    total = sum(
        jnp.pad(strips[:, s], ((0, 0), (0, 0), (s * GRID, LANES - s * GRID)))
        for s in range(LANES // GRID)
    )
    parts = total[:, :, : SPAN * GRID].reshape(heads, GRID, SPAN, GRID)
    sides = jnp.arange(GRID, dtype=jnp.int32)
    place = GRID - 1 - sides[:, None] + sides[None, :]
    onehot = (place[:, :, None] == jnp.arange(SPAN, dtype=jnp.int32)).astype(f32)
    return jnp.einsum("hjai,jib->hab", parts, onehot, precision=HIGHEST).reshape(
        heads, SPAN * SPAN
    )


def per_device(
    tokens,
    timesteps,
    rel_index,
    time_table,
    bias_table,
    gain_one,
    shift_one,
    w_query,
    w_key,
    w_value,
    t_query,
    t_value,
    b_query,
    b_value,
    w_out,
    b_out,
    gain_two,
    shift_two,
    w_up,
    b_up,
    w_down,
    b_down,
    cotangent,
):
    _, local, width = tokens.shape
    hidden = w_up.shape[1]
    heads = bias_table.shape[0]
    head_size = width // heads
    n_dp, n_seq = lax.axis_size("dp"), lax.axis_size("seq")
    dp, seq = lax.axis_index("dp"), lax.axis_index("seq")
    own_heads = heads // n_seq
    group = own_heads * head_size
    half = group // 2
    scale = head_size ** (-0.5)
    table_rows = time_table.shape[0]
    down_rows, out_rows = hidden // n_dp, width // n_dp

    def own_columns(array):
        return lax.dynamic_slice_in_dim(array, seq * group, group, axis=array.ndim - 1)

    x, dy = tokens[0], cotangent[0]
    rows = jnp.stack(
        [gain_one, shift_one, b_query, b_value, b_out, gain_two, shift_two, b_down]
    )[:, None]
    here = seq.astype(jnp.int32)[None]
    embed = lax.dynamic_slice_in_dim(time_table, timesteps[0], 1, 0)
    *mine, hat_one = project(
        here, x, embed, rows, (w_key, w_query, t_query, w_value, t_value), n_seq, scale
    )
    mine = [swap(parts, "seq") for parts in mine]
    dy_all = lax.all_gather(dy, "dp", axis=0)
    place = key_places(rel_index)
    table = lax.dynamic_slice_in_dim(bias_table, seq * own_heads, own_heads, 0)
    table = jnp.pad(
        table.reshape(own_heads, SPAN, SPAN), ((0, 0), (0, 72 - SPAN), (0, LANES - SPAN))
    )
    table, hat_one = tie(table, hat_one)
    strips = bias_strips(table)
    weight = jnp.concatenate([own_columns(w).T for w in (w_query, w_key, w_value)], axis=0)
    weight = jnp.swapaxes(weight.reshape(3, 2, half, width), 0, 1).reshape(6 * half, width)
    place, dy_all, weight = tie(place, dy_all, weight)
    tokens_0, saved_0 = attend(here, mine[0], place, strips, 0, head_size)
    mine_1, hat_one, tokens_0, place = tie(mine[1], hat_one, tokens_0, place)
    mixed_0 = swap(tokens_0, "seq")
    hat_all = lax.all_gather(hat_one, "seq", axis=0)
    tokens_1, saved_1 = attend(here, mine_1, place, strips, 1, head_size)
    mixed_1 = swap(tokens_1, "seq")
    act, act_t, grad_inner, norm_t, mixed_t, middle, up_sum = mlp_first(
        here, mixed_0 + mixed_1, x, dy, rows, b_up[None], w_out, w_up, w_down
    )

    chip, core = dp // 2, dp % 2
    by_core = norm_t.reshape(n_dp // 2, 2, out_rows, local)

    dp_bits = list(range(n_dp.bit_length() - 1))
    chip_bits = dp_bits[1:]
    bits = len(chip_bits)
    turned_bits = [sum(((n >> b) & 1) << (bits - 1 - b) for b in range(bits)) for n in range(1 << bits)]
    orders = [chip_bits, chip_bits[::-1]]
    places = jnp.stack([jnp.array(turned_bits), jnp.arange(1 << bits)]) ^ chip

    def rows_of(core):
        own = lax.dynamic_index_in_dim(by_core, core, 1, keepdims=False)
        return jnp.take(own, places, axis=0).reshape(2, width // 2, local)

    norm_other = exchange(rows_of(1 - core), "dp", 1)
    inner_other = exchange(grad_inner, "dp", 1)
    seq_order = (jnp.arange(n_seq) ^ seq).astype(jnp.int32)
    up_parts = up_grad(seq_order, rows_of(core), norm_other, grad_inner, inner_other)
    act_parts = lax.all_to_all(act_t.reshape(n_dp, down_rows, local), "dp", 0, 0)
    middle, dy_all, up_parts = tie(middle, dy_all, up_parts)
    grad_0, grad_1, (result, grad_middle, branch, sums_two) = mlp_second(
        here, middle, dy, rows, act, grad_inner, w_out, w_up, w_down, n_seq
    )
    out_part = dot(mixed_t, branch).astype(bf16)
    grad_0, grad_1 = swap(grad_0, "seq"), swap(grad_1, "seq")
    part_down = down_grad(act_parts, dy_all)
    part_down, grad_0 = tie(part_down, grad_0)
    grad_w_down = lax.psum_scatter(part_down, "seq", scatter_dimension=0, tiled=True)
    grads_0, strips_0 = attend_back(here, grad_0, *saved_0, place, head_size)
    grads_0, grad_1 = tie(grads_0, grad_1)
    heads_0 = swap(grads_0, "seq")
    halves = [
        two_halves(keep, exchange(send, "dp", 1 << o[0]), 1)
        for keep, send, o in zip(up_parts[::2], up_parts[1::2], orders)
    ]
    halves, grad_1 = tie(halves, grad_1)
    grads_1, strips_1 = attend_back(here, grad_1, *saved_1, place, head_size)
    heads_1 = swap(grads_1, "seq")
    for n in range(1, bits):
        halves = [
            two_halves(keep, exchange(send, "dp", 1 << o[n]), 1 if n + 1 < bits else 0)
            for (keep, send), o in zip(halves, orders)
        ]
    halves, weight, grads_1 = tie(halves, weight, grads_1)
    product, sums_one, norms = qkv_grad(here, list(grads_0) + list(grads_1), hat_all, weight, rows)
    near = [add_low(keep, exchange(send, "seq", 1)) for keep, send in halves]
    grad_w_up = (near[0].astype(f32) + exchange(near[1], "seq", 2).astype(f32))[0]
    grad_w_down = jnp.transpose(grad_w_down).astype(f32)

    bits_shape = (2,) * len(dp_bits)
    grad_qkv = halve_bits(
        product.reshape((2,) + bits_shape + (out_rows, 3 * half)), 1, dp_bits, dp_bits
    )
    grad_qkv = grad_qkv.astype(f32).reshape(2, out_rows, 3, half)
    grad_qkv = jnp.transpose(grad_qkv, (1, 2, 0, 3)).reshape(out_rows, 3, group)
    out_part = halve_bits(
        out_part.reshape(bits_shape + (out_rows, width)), 0, dp_bits, dp_bits[:1] + dp_bits[:0:-1]
    )
    out_part = jnp.swapaxes(out_part.reshape(out_rows, n_seq, group), 0, 1)
    grad_w_out = jnp.sum(lax.all_to_all(out_part, "seq", 0, 0).astype(f32), axis=0)
    grad_tokens = token_grad(
        here, heads_0 + heads_1, x, grad_middle, rows, (w_query, w_key, w_value)
    )

    sums_one = jnp.swapaxes(sums_one.reshape(2, 3, half), 0, 1).reshape(3, group)
    query_sum, value_sum = sums_one[0], sums_one[2]
    tq_own, tv_own = own_columns(t_query), own_columns(t_value)
    grad_embed = jnp.dot(tq_own.astype(f32), query_sum, precision=HIGHEST) + jnp.dot(
        tv_own.astype(f32), value_sum, precision=HIGHEST
    )
    own_image = lax.broadcasted_iota(jnp.int32, (n_dp, 1), 0) == dp

    def slot(row):
        return jnp.where(own_image, row[None, :], 0.0).reshape(-1)

    apart = [table_grad(jnp.concatenate([strips_0, strips_1])).reshape(-1), query_sum, value_sum]
    summed = [
        slot(grad_embed),
        up_sum[0],
        sums_two[:4].reshape(-1),
        norms[:2].reshape(-1),
    ]
    images = [slot(jnp.concatenate([query_sum, value_sum, timesteps.astype(f32)]))]
    sizes = [sum(a.shape[0] for a in part) for part in (apart, summed, images)]
    vector = sum_over(jnp.concatenate(apart + summed + images), "dp")
    image_sums = vector[sizes[0] + sizes[1] :].reshape(n_dp, 2 * group + 1)
    steps_all = image_sums[:, 2 * group].astype(jnp.int32)
    vector = gather_rows(vector[: sizes[0] + sizes[1]], "seq")
    table_size = own_heads * SPAN * SPAN
    grad_bias_table = vector[:, :table_size].reshape(heads, SPAN * SPAN)
    grad_b_query = vector[:, table_size : table_size + group].reshape(-1)
    grad_b_value = vector[:, table_size + group : sizes[0]].reshape(-1)
    both = jnp.sum(vector[:, sizes[0] :], axis=0)
    embed_size = n_dp * width
    embed_rows = both[:embed_size].reshape(n_dp, width)
    grad_b_up = both[embed_size : embed_size + hidden]
    rest = both[embed_size + hidden :].reshape(6, width)
    grad_b_down, grad_gain_two, grad_shift_two, grad_b_out, grad_gain_one, grad_shift_one = (
        rest[r] for r in range(6)
    )

    embeds = lax.dynamic_slice_in_dim(
        jnp.take(time_table, steps_all, axis=0), dp * out_rows, out_rows, axis=1
    ).astype(f32)
    grad_t_query = jnp.dot(embeds.T, image_sums[:, :group], precision=HIGHEST)
    grad_t_value = jnp.dot(embeds.T, image_sums[:, group : 2 * group], precision=HIGHEST)
    onehot = (
        steps_all[:, None] == jnp.arange(table_rows, dtype=jnp.int32)[None, :]
    ).astype(f32)
    grad_time_table = jnp.dot(onehot.T, embed_rows, precision=HIGHEST)

    return (
        result[None],
        grad_tokens[None],
        grad_qkv[:, 0],
        grad_qkv[:, 1],
        grad_qkv[:, 2],
        grad_t_query,
        grad_t_value,
        grad_w_out,
        grad_w_up,
        grad_w_down,
        grad_gain_one,
        grad_shift_one,
        grad_b_query,
        grad_b_value,
        grad_b_out,
        grad_gain_two,
        grad_shift_two,
        grad_b_up,
        grad_b_down,
        grad_bias_table,
        grad_time_table,
    )


def solution(mesh):
    split, copied, by_block = P("dp", "seq", None), P(), P("dp", "seq")
    in_specs = (split, P("dp"), P("seq", None)) + (copied,) * 19 + (split,)
    out_specs = (split, split) + (by_block,) * 8 + (copied,) * 11
    return jax.shard_map(
        per_device, mesh=mesh, in_specs=in_specs, out_specs=out_specs, check_vma=False
    )
```

```python
from functools import partial

import jax
import jax.numpy as jnp
from jax import lax
from jax.experimental import pallas as pl
from jax.experimental.pallas import tpu as pltpu
from jax.sharding import PartitionSpec as P

GRID = 32
SPAN = 2 * GRID - 1
STRIP = 2 * GRID * GRID
LANES = 128
BLOCK = 256
NORM_EPS = 1e-06
f32, bf16 = jnp.float32, jnp.bfloat16
HIGHEST = lax.Precision.HIGHEST
SCALE = 0.2
VMEM_LIMIT = 58 * 1024 * 1024


def dot(left, right, left_dim=1, right_dim=0):
    return lax.dot_general(
        left, right, (((left_dim,), (right_dim,)), ((), ())), preferred_element_type=f32
    )


def normalize(values):
    centered = values - jnp.mean(values, axis=-1, keepdims=True)
    scaled = lax.rsqrt(jnp.mean(centered * centered, axis=-1, keepdims=True) + NORM_EPS)
    return centered * scaled, scaled


def norm_back(grad_norm, normed, scaled, gain):
    inner = grad_norm * gain
    return scaled * (
        inner
        - jnp.mean(inner, axis=-1, keepdims=True)
        - normed * jnp.mean(inner * normed, axis=-1, keepdims=True)
    )


def row_of(ref):
    return ref[...].reshape(1, ref.shape[0])


def fold_rows(values, op):
    return op(values.reshape(values.shape[0] // 8, 8, values.shape[1]), axis=0)


def strip_place(key_row):
    first = (GRID - 1 - key_row) * GRID
    return (first % LANES) // GRID, first // LANES * LANES


def widen(rows, height):
    fill = jnp.zeros((height - rows.shape[0], rows.shape[1]), rows.dtype)
    return jnp.concatenate([rows, fill], axis=0)


def rows_for(group, half, count):
    return pl.ds(pl.multiple_of((2 * group + half) * count, 16), count)


def block_of(index):
    return pl.ds(pl.multiple_of(index * BLOCK, BLOCK), BLOCK)


def build_permutation(place_ref, perm):
    length = perm.shape[0]

    def rows_of(i, carry):
        first = pl.multiple_of(i * BLOCK, BLOCK)
        spots = lax.broadcasted_iota(jnp.int32, (BLOCK, length), 0) + first
        hit = spots == place_ref[...]
        perm[pl.ds(first, BLOCK), :] = jnp.where(hit, 1.0, 0.0).astype(bf16)
        return carry

    lax.fori_loop(0, length // BLOCK, rows_of, 0)


def strips_kernel(table_ref, strips_ref):
    lane = lax.broadcasted_iota(jnp.int32, (GRID, LANES), 1)
    per_tile = LANES // GRID

    def tile_of(n):
        whole_tile = jnp.zeros((GRID, LANES), f32)
        for k in range(per_tile):
            row = table_ref[0, pl.ds(per_tile * n + k, 1), :]
            turned = pltpu.roll(
                jnp.broadcast_to(row, (GRID, LANES)),
                (GRID * k - GRID + 1) % LANES,
                1,
                stride=1,
                stride_axis=0,
            )
            whole_tile = jnp.where(lane // GRID == k, turned, whole_tile)
        return whole_tile

    tiles = [tile_of(n) for n in range(STRIP // LANES + 1)]
    for n in range(STRIP // LANES):
        span = slice(n * LANES, (n + 1) * LANES)
        strips_ref[0, 0, :, span] = tiles[n]
        for s in range(1, per_tile):
            back = LANES - GRID * s
            strips_ref[0, s, :, span] = jnp.where(
                lane < back, pltpu.roll(tiles[n], back, 1), pltpu.roll(tiles[n + 1], back, 1)
            )


def fold_strips(strips, table_ref):
    lane = lax.broadcasted_iota(jnp.int32, (GRID, LANES), 1)
    row = lax.broadcasted_iota(jnp.int32, (8, LANES), 0)
    per_tile = LANES // GRID

    before = [jnp.zeros((GRID, LANES), f32)] * (per_tile - 1)
    for n in range(STRIP // LANES):
        span = slice(n * LANES, (n + 1) * LANES)
        total = strips[0, 0, :, span]
        turned = []
        for s in range(1, per_tile):
            turned.append(pltpu.roll(strips[0, s, :, span], GRID * s, 1))
            total = total + jnp.where(lane >= GRID * s, turned[-1], before[s - 1])
        before = turned
        for parity in range(2):
            part = jnp.where(lane // GRID % 2 == parity, total, 0.0)
            if parity:
                part = pltpu.roll(part, LANES - GRID, 1)
            part = pltpu.roll(part[:16], 16, 1) + part[16:]
            part = pltpu.roll(part[:8], 8, 1) + part[8:]
            for step in (4, 2, 1):
                part = jnp.where(row % (2 * step) < step, pltpu.roll(part, step, 1), part)
            table_ref[0, parity, n : n + 1, :] = jnp.sum(part, axis=0, keepdims=True)


def project_kernel(
    scale,
    groups,
    seq_ref,
    x_ref,
    embed_ref,
    gain_ref,
    shift_ref,
    b_query_ref,
    b_value_ref,
    wk_hbm,
    wq_hbm,
    tq_hbm,
    wv_hbm,
    tv_hbm,
    *refs,
):
    outs, (hat_ref, held, turned, sems) = refs[: 2 * groups], refs[2 * groups :]
    sources = (wk_hbm, wq_hbm, tq_hbm, wv_hbm, tv_hbm)
    copies = [
        pltpu.make_async_copy(source, held.at[n], sems.at[n]) for n, source in enumerate(sources)
    ]
    for copy in copies:
        copy.start()
    hat, _ = normalize(x_ref[...].astype(f32))
    hat_ref[...] = hat.astype(bf16)
    act = (hat * row_of(gain_ref) + row_of(shift_ref)).astype(bf16)
    embed = jnp.broadcast_to(embed_ref[...].astype(f32), (16, embed_ref.shape[1])).astype(bf16)
    count = outs[0].shape[0] // 3
    seq = seq_ref[0]

    def put(which, value):
        turned[which] = jnp.transpose(value.astype(bf16))
        for k in range(groups):
            for h in range(2):
                outs[h * groups + k][which * count : (which + 1) * count, :] = turned[
                    which, rows_for(k ^ seq, h, count), :
                ]

    copies[0].wait()
    put(1, dot(act, held[0]))
    copies[1].wait()
    copies[2].wait()
    time_query = dot(embed, held[2])[0:1]
    put(0, (dot(act, held[1]) + time_query + row_of(b_query_ref)) * scale)
    copies[3].wait()
    copies[4].wait()
    time_value = dot(embed, held[4])[0:1]
    put(2, dot(act, held[3]) + time_value + row_of(b_value_ref))


def attend_kernel(
    head_size,
    groups,
    seq_ref,
    place_ref,
    strips_ref,
    *refs,
):
    own, outs = refs[:groups], refs[groups : 2 * groups]
    qkv_ref, expo_ref, inverse_ref, mixed_ref = refs[2 * groups : 2 * groups + 4]
    perm, by_place, query_s, key_s, value_s, scores_s = refs[2 * groups + 4 :]
    seq = seq_ref[0]
    head = pl.program_id(0)
    group, length = mixed_ref.shape
    tiles = length // BLOCK

    @pl.when(head == 0)
    def _():
        build_permutation(place_ref, perm)

        def arrange(i, carry):
            span = pl.ds(pl.multiple_of(i * BLOCK, BLOCK), BLOCK)
            part = jnp.zeros((3 * group, BLOCK), f32)
            for k in range(groups):
                part = part + dot(own[k][...], perm[span, block_of(k ^ seq)], 1, 1)
            by_place[:, span] = part
            qkv_ref[:, span] = part.astype(bf16)
            return carry

        lax.fori_loop(0, tiles, arrange, 0)

    def rows_of(which):
        first = pl.multiple_of(which * group + head * head_size, 8)
        return by_place[pl.ds(first, head_size), :]

    query_s[...] = widen(rows_of(0), LANES).astype(bf16)
    key_s[...] = jnp.transpose(widen(rows_of(1), LANES)).astype(bf16)
    value_s[...] = widen(rows_of(2), value_s.shape[0]).astype(bf16)
    own_rows = pl.ds(pl.multiple_of(head * head_size, 8), head_size)

    def tile(t, carry):
        first = pl.multiple_of(t * BLOCK, BLOCK)
        span = pl.ds(first, BLOCK)
        query = query_s[:, span]
        peak = jnp.full((8, BLOCK), -jnp.inf, f32)
        for c in range(tiles):
            keys = slice(c * BLOCK, (c + 1) * BLOCK)
            pieces = []
            for key_row in range(c * BLOCK // GRID, (c + 1) * BLOCK // GRID):
                shift, start = strip_place(key_row)
                pieces.append(strips_ref[0, shift, :, pl.ds(first + start, BLOCK)])
            scores = dot(key_s[keys, :], query) + jnp.concatenate(pieces, axis=0)
            scores_s[keys, :] = scores
            peak = jnp.maximum(peak, fold_rows(scores, jnp.max))
        peak = jnp.max(peak, axis=0, keepdims=True)
        total = jnp.zeros((8, BLOCK), f32)
        mixed = jnp.zeros((value_s.shape[0], BLOCK), f32)
        for c in range(tiles):
            keys = slice(c * BLOCK, (c + 1) * BLOCK)
            expo = jnp.exp(scores_s[keys, :] - peak)
            total = total + fold_rows(expo, jnp.sum)
            low = expo.astype(bf16)
            expo_ref[0, keys, span] = low
            mixed = mixed + dot(value_s[:, keys], low)
        inverse = 1.0 / jnp.sum(total, axis=0, keepdims=True)
        inverse_ref[0, :, span] = inverse
        mixed_ref[own_rows, span] = (mixed * inverse)[:head_size]
        return carry

    lax.fori_loop(0, tiles, tile, 0)

    @pl.when(head == pl.num_programs(0) - 1)
    def _():
        low = mixed_ref[...].astype(bf16)
        for k in range(groups):
            outs[k][...] = dot(low, perm[:, block_of(k ^ seq)]).astype(bf16)


def attend_back_kernel(
    head_size,
    groups,
    seq_ref,
    qkv_ref,
    expo_ref,
    inverse_ref,
    mixed_ref,
    place_ref,
    *refs,
):
    given, outs = refs[:groups], refs[groups : 2 * groups]
    (
        table_ref,
        sums_ref,
        strips_ref,
        perm,
        by_place,
        grad_place,
        grads,
        query_s,
        key_s,
        value_s,
        grad_s,
        grad_t,
        offset_s,
        grad_key,
        grad_value,
    ) = refs[2 * groups :]
    seq = seq_ref[0]
    head = pl.program_id(0)
    group, length = mixed_ref.shape
    tiles = length // BLOCK
    scale = head_size ** (-0.5)

    @pl.when(head == 0)
    def _():
        build_permutation(place_ref, perm)

        def arrange(i, carry):
            span = pl.ds(pl.multiple_of(i * BLOCK, BLOCK), BLOCK)
            part = jnp.zeros((group, BLOCK), f32)
            for k in range(groups):
                part = part + dot(given[k][...], perm[span, block_of(k ^ seq)], 1, 1)
            grad_place[:, span] = part
            by_place[:, span] = qkv_ref[:, span].astype(f32)
            return carry

        lax.fori_loop(0, tiles, arrange, 0)

    own_rows = pl.ds(pl.multiple_of(head * head_size, 8), head_size)

    def rows_of(which):
        first = pl.multiple_of(which * group + head * head_size, 8)
        return by_place[pl.ds(first, head_size), :]

    query_s[...] = jnp.transpose(widen(rows_of(0), LANES)).astype(bf16)
    key_s[...] = widen(rows_of(1), key_s.shape[0]).astype(bf16)
    value_s[...] = jnp.transpose(widen(rows_of(2), LANES)).astype(bf16)
    grad = grad_place[own_rows, :]
    inverse = inverse_ref[0]
    offset_s[...] = inverse * jnp.sum(grad * mixed_ref[own_rows, :], axis=0, keepdims=True)
    grad = widen(grad * inverse, LANES)
    grad_s[...] = grad.astype(bf16)
    grad_t[...] = jnp.transpose(grad).astype(bf16)
    grad_key[...] = jnp.zeros_like(grad_key)
    grad_value[...] = jnp.zeros_like(grad_value)
    strips_ref[...] = jnp.zeros_like(strips_ref)

    def tile(t, carry):
        first = pl.multiple_of(t * BLOCK, BLOCK)
        span = pl.ds(first, BLOCK)
        grad_tile = grad_s[:, span]
        offset = offset_s[:, span]
        grad_query = jnp.zeros((key_s.shape[0], BLOCK), f32)
        for c in range(tiles):
            keys = slice(c * BLOCK, (c + 1) * BLOCK)
            expo = expo_ref[0, keys, span]
            grad_scores = expo.astype(f32) * (dot(value_s[keys, :], grad_tile) - offset)
            for row in range(BLOCK // GRID):
                shift, start = strip_place(c * BLOCK // GRID + row)
                strips_ref[0, shift, :, pl.ds(first + start, BLOCK)] += grad_scores[
                    row * GRID : (row + 1) * GRID
                ]
            low = grad_scores.astype(bf16)
            grad_query = grad_query + dot(key_s[:, keys], low)
            grad_key[keys, :] += dot(low, query_s[span, :])
            grad_value[keys, :] += dot(expo, grad_t[span, :])
        grads[own_rows, span] = grad_query[:head_size] * scale
        return carry

    lax.fori_loop(0, tiles, tile, 0)
    for which, total in ((1, grad_key), (2, grad_value)):
        first = pl.multiple_of(which * group + head * head_size, 8)
        grads[pl.ds(first, head_size), :] = jnp.transpose(total[...])[:head_size]

    @pl.when(head >= 0)
    def _():
        fold_strips(strips_ref, table_ref)

    @pl.when(head == pl.num_programs(0) - 1)
    def _():
        low = grads[...].astype(bf16)
        sums_ref[...] = dot(jnp.ones((8, length), bf16), low, 1, 1)
        for k in range(groups):
            outs[k][...] = dot(low, perm[:, block_of(k ^ seq)]).astype(bf16)


def mlp_first_kernel(
    groups,
    step,
    seq_ref,
    x_ref,
    dy_ref,
    b_out_ref,
    gain_ref,
    shift_ref,
    b_up_ref,
    w_out_hbm,
    w_up_hbm,
    w_down_hbm,
    *refs,
):
    given = refs[: 2 * groups]
    act_hbm, act_t_hbm, inner_hbm, norm_t_ref, mixed_t_ref, middle_ref, up_sum_ref = refs[
        2 * groups : 2 * groups + 7
    ]
    (
        w_out_s,
        w_up_s,
        w_down_s,
        act_s,
        act_t_s,
        inner_s,
        norm_s,
        sem,
        up_sems,
        down_sems,
        act_sems,
        act_t_sems,
        inner_sems,
    ) = refs[2 * groups + 7 :]
    chunks = w_up_s.shape[0]
    seq = seq_ref[0]

    def span_of(i):
        return pl.ds(pl.multiple_of(i * step, step), step)

    def fetch(i):
        return (
            pltpu.make_async_copy(w_up_hbm.at[:, span_of(i)], w_up_s.at[i], up_sems.at[i]),
            pltpu.make_async_copy(w_down_hbm.at[span_of(i), :], w_down_s.at[i], down_sems.at[i]),
        )

    def put(i):
        return (
            pltpu.make_async_copy(act_s.at[i], act_hbm.at[:, span_of(i)], act_sems.at[i]),
            pltpu.make_async_copy(act_t_s.at[i], act_t_hbm.at[span_of(i), :], act_t_sems.at[i]),
            pltpu.make_async_copy(inner_s.at[i], inner_hbm.at[:, span_of(i)], inner_sems.at[i]),
        )

    def begin(i, carry):
        for copy in fetch(i):
            copy.start()
        return carry

    out_copy = pltpu.make_async_copy(w_out_hbm, w_out_s, sem.at[0])
    out_copy.start()
    lax.fori_loop(0, chunks, begin, 0)
    count = given[0].shape[0]
    for k in range(groups):
        for h in range(2):
            mixed_t_ref[rows_for(k ^ seq, h, count), :] = given[h * groups + k][...]
    mixed = jnp.transpose(mixed_t_ref[...])
    out_copy.wait()
    middle = x_ref[...].astype(f32) + dot(mixed, w_out_s[...]) + row_of(b_out_ref)
    hat, _ = normalize(middle)
    middle_ref[...] = middle
    norm = (hat * row_of(gain_ref) + row_of(shift_ref)).astype(bf16)
    norm_s[...] = norm
    norm_t_ref[...] = jnp.transpose(norm)

    def chunk(i, carry):
        for copy in fetch(i):
            copy.wait()
        inner = dot(norm_s[...], w_up_s[i]) + b_up_ref[:, span_of(i)]
        cdf = 0.5 * (1.0 + lax.erf(inner * (0.5**0.5)))
        pdf = jnp.exp(-0.5 * inner * inner) * 0.3989422804014327
        act = (inner * cdf).astype(bf16)
        low = (dot(dy_ref[...], w_down_s[i], 1, 1) * (cdf + inner * pdf)).astype(bf16)
        act_s[i] = act
        act_t_s[i] = jnp.transpose(act)
        inner_s[i] = low
        up_sum_ref[:, span_of(i)] = jnp.sum(low.astype(f32), axis=0, keepdims=True)
        for copy in put(i):
            copy.start()
        return carry

    lax.fori_loop(0, chunks, chunk, 0)

    def finish(i, carry):
        for copy in put(i):
            copy.wait()
        return carry

    lax.fori_loop(0, chunks, finish, 0)


def mlp_second_kernel(
    groups,
    step,
    seq_ref,
    middle_ref,
    dy_ref,
    b_down_ref,
    gain_ref,
    act_ref,
    inner_ref,
    w_out_hbm,
    w_up_hbm,
    w_down_hbm,
    *refs,
):
    outs = refs[:groups]
    result_ref, grad_middle_ref, branch_ref, sums_ref = refs[groups : groups + 4]
    (
        w_out_s,
        w_up_s,
        w_down_s,
        result_s,
        grad_s,
        mixed_s,
        sem,
        up_sems,
        down_sems,
    ) = refs[groups + 4 :]
    chunks = w_up_s.shape[0]

    def span_of(i):
        return pl.ds(pl.multiple_of(i * step, step), step)

    def fetch(i):
        return (
            pltpu.make_async_copy(w_up_hbm.at[:, span_of(i)], w_up_s.at[i], up_sems.at[i]),
            pltpu.make_async_copy(w_down_hbm.at[span_of(i), :], w_down_s.at[i], down_sems.at[i]),
        )

    def begin(i, carry):
        for copy in fetch(i):
            copy.start()
        return carry

    lax.fori_loop(0, chunks, begin, 0)
    out_copy = pltpu.make_async_copy(w_out_hbm, w_out_s, sem.at[0])
    out_copy.start()
    result_s[...] = middle_ref[...] + row_of(b_down_ref)
    grad_s[...] = jnp.zeros_like(grad_s)

    def chunk(i, carry):
        for copy in fetch(i):
            copy.wait()
        result_s[...] += dot(act_ref[:, span_of(i)], w_down_s[i])
        grad_s[...] += dot(inner_ref[:, span_of(i)], w_up_s[i], 1, 1)
        return carry

    lax.fori_loop(0, chunks, chunk, 0)
    result_ref[...] = result_s[...].astype(bf16)
    hat, scaled = normalize(middle_ref[...])
    dy = dy_ref[...].astype(f32)
    grad_norm = grad_s[...]
    grad_middle = dy + norm_back(grad_norm, hat, scaled, row_of(gain_ref))
    branch = grad_middle.astype(bf16)
    grad_middle_ref[...] = grad_middle
    branch_ref[...] = branch
    out_copy.wait()
    mixed_s[...] = dot(w_out_s[...], branch, 1, 1).astype(bf16)
    count = outs[0].shape[0]
    for k in range(groups):
        rows = pl.ds(pl.multiple_of((k ^ seq_ref[0]) * count, 16), count)
        outs[k][...] = mixed_s[rows, :]
    sums_ref[...] = jnp.concatenate(
        [
            jnp.sum(dy, axis=0, keepdims=True),
            jnp.sum(grad_norm * hat, axis=0, keepdims=True),
            jnp.sum(grad_norm, axis=0, keepdims=True),
            jnp.sum(branch.astype(f32), axis=0, keepdims=True),
            jnp.zeros((4, dy.shape[1]), f32),
        ],
        axis=0,
    )


def up_grad_kernel(first_ref, own_ref, other_ref, inner_ref, inner_other, out_ref, own_s, other_s):
    blocks = first_ref.shape[0]
    count = own_s.shape[0] // blocks

    @pl.when(pl.program_id(0) == 0)
    def _():
        for n in range(blocks):
            source = pl.ds(pl.multiple_of(first_ref[n], 16), count)
            own_s[n * count : (n + 1) * count, :] = own_ref[source, :]
            other_s[n * count : (n + 1) * count, :] = other_ref[source, :]

    low = (dot(own_s[...], inner_ref[...]) + dot(other_s[...], inner_other[...])).astype(bf16)
    for n in range(blocks):
        out_ref[n, 0] = low[n * count : (n + 1) * count]


def down_grad_kernel(act_ref, dy_ref, out_ref):
    total = dot(act_ref[0], dy_ref[0])
    for source in range(1, act_ref.shape[0]):
        total = total + dot(act_ref[source], dy_ref[source])
    out_ref[...] = jnp.transpose(total.astype(bf16))


def qkv_grad_kernel(groups, seq_ref, hat_ref, gain_ref, shift_ref, wq_hbm, wk_hbm, wv_hbm, *refs):
    given = refs[: 2 * groups]
    out_ref, norms_ref, held, turned, sems = refs[2 * groups :]
    seq = seq_ref[0]
    count = given[0].shape[0]
    rows = count // 3
    skipped = lax.rem(2 * rows * seq, LANES)
    window = pl.ds(pl.multiple_of(2 * rows * seq - skipped, LANES), held.shape[2])
    copies = [
        pltpu.make_async_copy(source.at[:, window], held.at[n], sems.at[n])
        for n, source in enumerate((wq_hbm, wk_hbm, wv_hbm))
    ]
    for copy in copies:
        copy.start()
    gain, shift = row_of(gain_ref), row_of(shift_ref)
    grad_gain, grad_shift = jnp.zeros_like(gain), jnp.zeros_like(shift)
    for n, copy in enumerate(copies):
        copy.wait()
        turned[n] = jnp.transpose(held[n])
    for h in range(2):
        span = slice(h * count, (h + 1) * count)
        product = jnp.zeros((count, hat_ref.shape[2]), f32)
        sums = jnp.zeros((count, 1), f32)
        for k in range(groups):
            grads = given[h * groups + k][...]
            product = product + dot(grads, hat_ref[k ^ seq])
            sums = sums + jnp.sum(grads.astype(f32), axis=1, keepdims=True)
        out_ref[:, span] = jnp.transpose((product * gain + sums * shift).astype(bf16))
        for n in range(3):
            own = slice(n * rows, (n + 1) * rows)
            first = pl.multiple_of(skipped + h * rows, 16)
            weight = turned[n, pl.ds(first, rows), :].astype(f32)
            grad_gain = grad_gain + jnp.sum(weight * product[own], axis=0, keepdims=True)
            grad_shift = grad_shift + jnp.sum(weight * sums[own], axis=0, keepdims=True)
    norms_ref[...] = jnp.concatenate(
        [grad_gain, grad_shift, jnp.zeros((6, gain.shape[1]), f32)], axis=0
    )


def tokens_kernel(groups, seq_ref, x_ref, middle_ref, gain_ref, wq_hbm, wk_hbm, wv_hbm, *refs):
    given, (out_ref, held, grads_s, sems) = refs[: 2 * groups], refs[2 * groups :]
    copies = [
        pltpu.make_async_copy(source, held.at[n], sems.at[n])
        for n, source in enumerate((wq_hbm, wk_hbm, wv_hbm))
    ]
    for copy in copies:
        copy.start()
    seq = seq_ref[0]
    count = given[0].shape[0] // 3
    for k in range(groups):
        for h in range(2):
            for which in range(3):
                grads_s[which, rows_for(k ^ seq, h, count), :] = given[h * groups + k][
                    which * count : (which + 1) * count
                ]
    hat, scaled = normalize(x_ref[...].astype(f32))
    total = jnp.zeros(middle_ref.shape, f32)
    for which, copy in enumerate(copies):
        grads = jnp.transpose(grads_s[which])
        copy.wait()
        total = total + dot(grads, held[which], 1, 1)
    out_ref[...] = (
        middle_ref[...] + norm_back(total, hat, scaled, row_of(gain_ref))
    ).astype(bf16)


def whole(shape):
    zeros = (0,) * len(shape)
    return pl.BlockSpec(shape, lambda s: zeros, pipeline_mode=pl.Buffered(1))


def kept(shape):
    zeros = (0,) * len(shape)
    return pl.BlockSpec(shape, lambda s: zeros)


def per_head(shape):
    rest = (0,) * (len(shape) - 1)
    return pl.BlockSpec((1,) + tuple(shape[1:]), lambda s: (s,) + rest)


def params(grid=True):
    return pltpu.CompilerParams(
        dimension_semantics=("arbitrary",) if grid else None, vmem_limit_bytes=VMEM_LIMIT
    )


def takes(microseconds):
    return pl.CostEstimate(
        flops=int(microseconds * SCALE * 1e9), bytes_accessed=int(microseconds * SCALE * 3e6), transcendentals=0
    )


IN_VMEM = pl.BlockSpec(memory_space=pltpu.VMEM)
IN_SMEM = pl.BlockSpec(memory_space=pltpu.SMEM)
IN_HBM = pl.BlockSpec(memory_space=pl.ANY)


def shape_of(shape, kind):
    return jax.ShapeDtypeStruct(shape, kind)


def bias_strips(table):
    heads = table.shape[0]
    out = shape_of((heads, LANES // GRID, GRID, STRIP), f32)
    return pl.pallas_call(
        strips_kernel,
        grid=(heads,),
        in_specs=[per_head(table.shape)],
        out_specs=per_head(out.shape),
        out_shape=out,
        compiler_params=params(),
        cost_estimate=takes(9),
        name="strips",
    )(table)


def project(seq, x, embed, vectors, weights, groups, scale):
    count, width = x.shape
    part = shape_of((3 * width // groups // 2, count), bf16)
    outs = pl.pallas_call(
        partial(project_kernel, scale, groups),
        in_specs=[IN_SMEM] + [IN_VMEM] * 6 + [IN_HBM] * 5,
        out_specs=[IN_VMEM] * (2 * groups + 1),
        out_shape=(part,) * (2 * groups) + (shape_of((count, width), bf16),),
        scratch_shapes=[
            pltpu.VMEM((5, width, width), bf16),
            pltpu.VMEM((3, width, count), bf16),
            pltpu.SemaphoreType.DMA((5,)),
        ],
        compiler_params=params(False),
        cost_estimate=takes(9),
        name="project",
    )(seq, x, embed, *vectors, *weights)
    return outs[:groups], outs[groups : 2 * groups], outs[2 * groups]


def attend(seq, own, place, strips, half, head_size):
    heads = strips.shape[0] // 2
    length = place.shape[1]
    group = heads * head_size
    groups = len(own)
    tall = -(-head_size // 16) * 16
    saved = (
        shape_of((3 * group, length), bf16),
        shape_of((heads, length, length), bf16),
        shape_of((heads, 1, length), f32),
        shape_of((group, length), f32),
    )
    own_strips = pl.BlockSpec(
        (1,) + strips.shape[1:], lambda s: (half * heads + s, 0, 0, 0)
    )
    outs = pl.pallas_call(
        partial(attend_kernel, head_size, groups),
        grid=(heads,),
        in_specs=[IN_SMEM, whole(place.shape), own_strips] + [whole(a.shape) for a in own],
        out_specs=[kept((group, BLOCK))] * groups
        + [
            kept(saved[0].shape),
            per_head(saved[1].shape),
            per_head(saved[2].shape),
            kept(saved[3].shape),
        ],
        out_shape=(shape_of((group, BLOCK), bf16),) * groups + saved,
        scratch_shapes=[
            pltpu.VMEM((length, length), bf16),
            pltpu.VMEM((3 * group, length), f32),
            pltpu.VMEM((LANES, length), bf16),
            pltpu.VMEM((length, LANES), bf16),
            pltpu.VMEM((tall, length), bf16),
            pltpu.VMEM((length, BLOCK), f32),
        ],
        compiler_params=params(),
        cost_estimate=takes(13),
        name="attend",
    )(seq, place, strips, *own)
    return outs[:groups], outs[groups:]


def attend_back(seq, half, grad_mixed, qkv, expo, inverse, mixed, place, head_size):
    heads, length, _ = expo.shape
    group = heads * head_size
    groups = len(grad_mixed)
    tall = -(-head_size // 16) * 16
    table = shape_of((heads, 2, STRIP // LANES, LANES), f32)
    given = pl.BlockSpec((group, BLOCK), lambda s: (half, 0), pipeline_mode=pl.Buffered(1))
    outs = pl.pallas_call(
        partial(attend_back_kernel, head_size, groups),
        grid=(heads,),
        in_specs=[
            IN_SMEM,
            whole(qkv.shape),
            per_head(expo.shape),
            per_head(inverse.shape),
            whole(mixed.shape),
            whole(place.shape),
        ]
        + [given] * groups,
        out_specs=[kept((3 * group, BLOCK))] * groups
        + [per_head(table.shape), kept((8, 3 * group))],
        out_shape=(shape_of((3 * group, BLOCK), bf16),) * groups
        + (table, shape_of((8, 3 * group), f32)),
        scratch_shapes=[
            pltpu.VMEM((1, LANES // GRID, GRID, STRIP), f32),
            pltpu.VMEM((length, length), bf16),
            pltpu.VMEM((3 * group, length), f32),
            pltpu.VMEM((group, length), f32),
            pltpu.VMEM((3 * group, length), f32),
            pltpu.VMEM((length, LANES), bf16),
            pltpu.VMEM((tall, length), bf16),
            pltpu.VMEM((length, LANES), bf16),
            pltpu.VMEM((LANES, length), bf16),
            pltpu.VMEM((length, LANES), bf16),
            pltpu.VMEM((1, length), f32),
            pltpu.VMEM((length, LANES), f32),
            pltpu.VMEM((length, LANES), f32),
        ],
        compiler_params=params(),
        cost_estimate=takes(16),
        name="attend_back",
    )(seq, qkv, expo, inverse, mixed, place, *grad_mixed)
    return outs[:groups], outs[groups:]


def mlp_first(seq, mixed, x, dy, vectors, b_up, w_out, w_up, w_down):
    count, width = x.shape
    hidden = w_up.shape[1]
    step = 512
    chunks = hidden // step
    dma = pltpu.SemaphoreType.DMA
    return pl.pallas_call(
        partial(mlp_first_kernel, len(mixed) // 2, step),
        in_specs=[IN_SMEM] + [IN_VMEM] * 6 + [IN_HBM] * 3 + [IN_VMEM] * len(mixed),
        out_specs=[IN_HBM] * 3 + [IN_VMEM] * 4,
        out_shape=(
            shape_of((count, hidden), bf16),
            shape_of((hidden, count), bf16),
            shape_of((count, hidden), bf16),
            shape_of((width, count), bf16),
            shape_of((width, count), bf16),
            shape_of((count, width), f32),
            shape_of((1, hidden), f32),
        ),
        scratch_shapes=[
            pltpu.VMEM((width, width), bf16),
            pltpu.VMEM((chunks, width, step), bf16),
            pltpu.VMEM((chunks, step, width), bf16),
            pltpu.VMEM((chunks, count, step), bf16),
            pltpu.VMEM((chunks, step, count), bf16),
            pltpu.VMEM((chunks, count, step), bf16),
            pltpu.VMEM((count, width), bf16),
            dma((1,)),
        ]
        + [dma((chunks,))] * 5,
        compiler_params=params(False),
        cost_estimate=takes(14),
        name="mlp_first",
    )(seq, x, dy, *vectors, b_up, w_out, w_up, w_down, *mixed)


def mlp_second(seq, middle, dy, vectors, act, inner, w_out, w_up, w_down, groups):
    count, width = middle.shape
    hidden = w_up.shape[1]
    step = 512
    chunks = hidden // step
    part = shape_of((width // groups, count), bf16)
    dma = pltpu.SemaphoreType.DMA
    outs = pl.pallas_call(
        partial(mlp_second_kernel, groups, step),
        in_specs=[IN_SMEM] + [IN_VMEM] * 6 + [IN_HBM] * 3,
        out_specs=[IN_VMEM] * (groups + 4),
        out_shape=(part,) * groups
        + (
            shape_of((count, width), bf16),
            shape_of((count, width), f32),
            shape_of((count, width), bf16),
            shape_of((8, width), f32),
        ),
        scratch_shapes=[
            pltpu.VMEM((width, width), bf16),
            pltpu.VMEM((chunks, width, step), bf16),
            pltpu.VMEM((chunks, step, width), bf16),
            pltpu.VMEM((count, width), f32),
            pltpu.VMEM((count, width), f32),
            pltpu.VMEM((width, count), bf16),
            dma((1,)),
            dma((chunks,)),
            dma((chunks,)),
        ],
        compiler_params=params(False),
        cost_estimate=takes(14),
        name="mlp_second",
    )(seq, middle, dy, *vectors, act, inner, w_out, w_up, w_down)
    return outs[:groups], outs[groups:]


def up_grad(first, own, other, inner, inner_other, groups):
    rows, count = own.shape
    blocks = first.shape[0]
    width = inner.shape[1] // groups
    wide = pl.BlockSpec((count, width), lambda s, first_ref: (0, s))
    left = pl.BlockSpec((rows, count), lambda s, first_ref: (0, 0))
    block = (blocks, 1, rows // 2 // blocks, width)
    return pl.pallas_call(
        up_grad_kernel,
        grid_spec=pltpu.PrefetchScalarGridSpec(
            num_scalar_prefetch=1,
            grid=(groups,),
            in_specs=[left, left, wide, wide],
            out_specs=pl.BlockSpec(block, lambda s, first_ref: (0, s, 0, 0)),
            scratch_shapes=[pltpu.VMEM((rows // 2, count), bf16)] * 2,
        ),
        out_shape=shape_of((blocks, groups) + block[2:], bf16),
        compiler_params=params(),
        cost_estimate=takes(8),
        name="up_grad",
    )(first, own, other, inner, inner_other)


def down_grad(act, dy):
    return pl.pallas_call(
        down_grad_kernel,
        in_specs=[IN_VMEM, IN_VMEM],
        out_specs=IN_VMEM,
        out_shape=shape_of((dy.shape[2], act.shape[1]), bf16),
        compiler_params=params(False),
        cost_estimate=takes(8),
        name="down_grad",
    )(act, dy)


def qkv_grad(seq, grads, hat, gain, shift, weights):
    width = hat.shape[2]
    count = grads[0].shape[0]
    columns = -(-(2 * count // 3 + LANES - GRID) // LANES) * LANES
    return pl.pallas_call(
        partial(qkv_grad_kernel, len(grads) // 2),
        in_specs=[IN_SMEM] + [IN_VMEM] * 3 + [IN_HBM] * 3 + [IN_VMEM] * len(grads),
        out_specs=[IN_VMEM] * 2,
        out_shape=(shape_of((width, 2 * count), bf16), shape_of((8, width), f32)),
        scratch_shapes=[
            pltpu.VMEM((3, width, columns), bf16),
            pltpu.VMEM((3, columns, width), bf16),
            pltpu.SemaphoreType.DMA((3,)),
        ],
        compiler_params=params(False),
        cost_estimate=takes(8),
        name="qkv_grad",
    )(seq, hat, gain, shift, *weights, *grads)


def token_grad(seq, grads, x, middle, gain, weights):
    count, width = x.shape
    return pl.pallas_call(
        partial(tokens_kernel, len(grads) // 2),
        in_specs=[IN_SMEM] + [IN_VMEM] * 3 + [IN_HBM] * 3 + [IN_VMEM] * len(grads),
        out_specs=IN_VMEM,
        out_shape=shape_of((count, width), bf16),
        scratch_shapes=[
            pltpu.VMEM((3, width, width), bf16),
            pltpu.VMEM((3, width, count), bf16),
            pltpu.SemaphoreType.DMA((3,)),
        ],
        compiler_params=params(False),
        cost_estimate=takes(9),
        name="token_grad",
    )(seq, x, middle, gain, *weights, *grads)


def exchange(array, axis, step):
    size = lax.axis_size(axis)
    return lax.ppermute(array, axis, [(i, i ^ step) for i in range(size)])


def sum_over(vector, axis):
    step = 1
    while step < lax.axis_size(axis):
        vector = vector + exchange(vector, axis, step)
        step *= 2
    return vector


def gather_rows(vector, axis):
    size, index = lax.axis_size(axis), lax.axis_index(axis)
    rows = vector[None]
    step = 1
    while step < size:
        rows = jnp.concatenate([rows, exchange(rows, axis, step)], axis=0)
        step *= 2
    return jnp.concatenate(
        [lax.dynamic_index_in_dim(rows, n ^ index, 0) for n in range(size)], axis=0
    )


def swap(parts, axis):
    return [parts[0]] + [exchange(parts[k], axis, k) for k in range(1, len(parts))]


def tie(*arrays):
    return lax.optimization_barrier(arrays)


def key_places(rel_index):
    first = rel_index[0]
    top = jnp.max(first)
    row = top // SPAN - first // SPAN
    column = top % SPAN - first % SPAN
    return (row * GRID + column)[None, :].astype(jnp.int32)


def table_grad(folded):
    heads = folded.shape[0]
    parts = folded.reshape(heads, 2, STRIP // LANES, 2, LANES // 2)
    parts = jnp.transpose(parts, (0, 2, 3, 1, 4)).reshape(heads, 2 * GRID, LANES // 2)
    return parts[:, :SPAN, :SPAN].reshape(heads, SPAN * SPAN)


def per_device(
    tokens,
    timesteps,
    rel_index,
    time_table,
    bias_table,
    gain_one,
    shift_one,
    w_query,
    w_key,
    w_value,
    t_query,
    t_value,
    b_query,
    b_value,
    w_out,
    b_out,
    gain_two,
    shift_two,
    w_up,
    b_up,
    w_down,
    b_down,
    cotangent,
):
    _, local, width = tokens.shape
    hidden = w_up.shape[1]
    heads = bias_table.shape[0]
    head_size = width // heads
    n_dp, n_seq = lax.axis_size("dp"), lax.axis_size("seq")
    dp, seq = lax.axis_index("dp"), lax.axis_index("seq")
    own_heads = heads // n_seq
    group = own_heads * head_size
    half = group // 2
    scale = head_size ** (-0.5)
    table_rows = time_table.shape[0]
    down_rows, out_rows = hidden // n_dp, width // n_dp

    def own_columns(array):
        return lax.dynamic_slice_in_dim(array, seq * group, group, axis=array.ndim - 1)

    x, dy = tokens[0], cotangent[0]
    here = seq.astype(jnp.int32)[None]
    embed = lax.dynamic_slice_in_dim(time_table, timesteps[0], 1, 0)
    *mine, hat_one = project(
        here,
        x,
        embed,
        (gain_one, shift_one, b_query, b_value),
        (w_key, w_query, t_query, w_value, t_value),
        n_seq,
        scale,
    )
    own_0 = swap(mine[0], "seq")
    dy_all = lax.all_gather(dy, "dp", axis=0)
    place = key_places(rel_index)
    table = lax.dynamic_slice_in_dim(bias_table, seq * own_heads, own_heads, 0)
    table = jnp.pad(
        table.reshape(own_heads, SPAN, SPAN), ((0, 0), (0, 72 - SPAN), (0, LANES - SPAN))
    )
    table, hat_one = tie(table, hat_one)
    strips = bias_strips(table)
    own_0, parts_1, place, strips = tie(own_0, mine[1], place, strips)
    own_1 = swap(parts_1, "seq")
    tokens_0, saved_0 = attend(here, own_0, place, strips, 0, head_size)

    own_1, tokens_0, saved_0, place, dy_all = tie(own_1, tokens_0, saved_0, place, dy_all)
    mixed_0 = swap(tokens_0, "seq")
    tokens_1, saved_1 = attend(here, own_1, place, strips, 1, head_size)

    tokens_1, saved_1, mixed_0 = tie(tokens_1, saved_1, mixed_0)
    mixed_1 = swap(tokens_1, "seq")

    mixed_1, hat_one = tie(mixed_1, hat_one)
    hat_all = lax.all_gather(hat_one, "seq", axis=0)
    act, act_t, grad_inner, norm_t, mixed_t, middle, up_sum = mlp_first(
        here,
        mixed_0 + mixed_1,
        x,
        dy,
        (b_out, gain_two, shift_two),
        b_up[None],
        w_out,
        w_up,
        w_down,
    )

    core = dp % 2
    norm_other = exchange(norm_t, "dp", 1)
    inner_other = exchange(grad_inner, "dp", 1)
    act_parts = lax.all_to_all(act_t.reshape(n_dp, down_rows, local), "dp", 0, 0)
    first = (2 * jnp.arange(n_dp // 2) + core) * out_rows
    norm_rows = [norm_t, norm_other]
    if out_rows % 16:
        first = jnp.zeros((1,), jnp.int32)
        norm_rows = [
            jnp.tile(
                lax.dynamic_index_in_dim(
                    a.reshape(n_dp // 2, 2, out_rows, local), core, 1, keepdims=False
                ).reshape(width // 2, local),
                (2, 1),
            )
            for a in norm_rows
        ]
    up_part = up_grad(first.astype(jnp.int32), *norm_rows, grad_inner, inner_other, n_seq)

    up_part, middle, act, mixed_t, up_sum = tie(up_part, middle, act, mixed_t, up_sum)
    grad_mixed, (result, grad_middle, branch, sums_two) = mlp_second(
        here, middle, dy, (b_down, gain_two), act, grad_inner, w_out, w_up, w_down, n_seq
    )

    grad_mixed, result, grad_middle, branch, sums_two, act_parts, hat_all, up_part = tie(
        grad_mixed, result, grad_middle, branch, sums_two, act_parts, hat_all, up_part
    )
    grad_mixed = swap(grad_mixed, "seq")
    if out_rows % 16:
        up_part = jnp.swapaxes(up_part.reshape(n_seq, n_dp // 2, out_rows, -1), 0, 1)
    same_core = [list(range(c, n_dp, 2)) for c in range(2)]
    up_part = lax.all_to_all(up_part, "dp", 0, 0, axis_index_groups=same_core)
    out_part = dot(mixed_t, branch).astype(bf16).reshape(n_dp, out_rows, width)
    part_down = down_grad(act_parts, dy_all)

    part_down, out_part, grad_mixed = tie(part_down, out_part, grad_mixed)
    grad_w_down = lax.psum_scatter(part_down, "seq", scatter_dimension=0, tiled=True)
    grads_0, (table_0, sums_0) = attend_back(here, 0, grad_mixed, *saved_0, place, head_size)

    grads_0, table_0, sums_0, grad_mixed, place = tie(grads_0, table_0, sums_0, grad_mixed, place)
    heads_0 = swap(grads_0, "seq")
    grads_1, (table_1, sums_1) = attend_back(here, 1, grad_mixed, *saved_1, place, head_size)

    grads_1, table_1, sums_1, heads_0, up_part, out_part = tie(
        grads_1, table_1, sums_1, heads_0, up_part, out_part
    )
    heads_1 = swap(grads_1, "seq")
    up_part = jnp.sum(up_part.astype(f32), axis=0).astype(bf16)
    up_part, hat_all, out_part = tie(up_part, hat_all, out_part)
    out_part = lax.all_to_all(out_part, "dp", 0, 0)
    product, norms = qkv_grad(
        here,
        list(grads_0) + list(grads_1),
        hat_all,
        gain_one,
        shift_one,
        (w_query, w_key, w_value),
    )

    heads_1, up_part, product, norms, table_0, table_1, sums_0, sums_1, up_sum, sums_two = tie(
        heads_1, up_part, product, norms, table_0, table_1, sums_0, sums_1, up_sum, sums_two
    )
    grad_w_up = lax.psum_scatter(up_part, "seq", scatter_dimension=0)
    query_sum, value_sum = (
        jnp.concatenate([sums[0, n * half : (n + 1) * half] for sums in (sums_0, sums_1)])
        for n in (0, 2)
    )
    tq_own, tv_own = own_columns(t_query), own_columns(t_value)
    grad_embed = jnp.dot(tq_own.astype(f32), query_sum, precision=HIGHEST) + jnp.dot(
        tv_own.astype(f32), value_sum, precision=HIGHEST
    )
    own_image = lax.broadcasted_iota(jnp.int32, (n_dp, 1), 0) == dp

    def slot(row):
        return jnp.where(own_image, row[None, :], 0.0).reshape(-1)

    apart = [table_grad(jnp.concatenate([table_0, table_1])).reshape(-1), query_sum, value_sum]
    summed = [
        slot(grad_embed),
        up_sum[0],
        sums_two[:4].reshape(-1),
        norms[:2].reshape(-1),
    ]
    images = [slot(jnp.concatenate([query_sum, value_sum, timesteps.astype(f32)]))]
    sizes = [sum(a.shape[0] for a in part) for part in (apart, summed, images)]
    vector = sum_over(jnp.concatenate(apart + summed + images), "dp")

    out_part, product, vector, heads_1 = tie(out_part, product, vector, heads_1)
    grad_qkv = lax.all_to_all(product.reshape(n_dp, out_rows, 3 * group), "dp", 0, 0)
    out_part = jnp.sum(out_part.astype(f32), axis=0).astype(bf16)
    out_part = jnp.swapaxes(out_part.reshape(out_rows, n_seq, group), 0, 1)
    grad_w_out = lax.psum_scatter(out_part, "seq", scatter_dimension=0)
    grad_tokens = token_grad(
        here, heads_0 + heads_1, x, grad_middle, gain_one, (w_query, w_key, w_value)
    )
    grad_w_up = grad_w_up.astype(f32)
    grad_w_down = jnp.transpose(grad_w_down.astype(f32))
    grad_w_out = grad_w_out.astype(f32)
    grad_qkv = jnp.sum(grad_qkv.astype(f32), axis=0).reshape(out_rows, 2, 3, half)
    grad_qkv = jnp.swapaxes(grad_qkv, 1, 2).reshape(out_rows, 3, group)
    image_sums = vector[sizes[0] + sizes[1] :].reshape(n_dp, 2 * group + 1)
    steps_all = image_sums[:, 2 * group].astype(jnp.int32)
    vector = gather_rows(vector[: sizes[0] + sizes[1]], "seq")
    table_size = own_heads * SPAN * SPAN
    grad_bias_table = vector[:, :table_size].reshape(heads, SPAN * SPAN)
    grad_b_query = vector[:, table_size : table_size + group].reshape(-1)
    grad_b_value = vector[:, table_size + group : sizes[0]].reshape(-1)
    both = jnp.sum(vector[:, sizes[0] :], axis=0)
    embed_size = n_dp * width
    embed_rows = both[:embed_size].reshape(n_dp, width)
    grad_b_up = both[embed_size : embed_size + hidden]
    rest = both[embed_size + hidden :].reshape(6, width)
    grad_b_down, grad_gain_two, grad_shift_two, grad_b_out, grad_gain_one, grad_shift_one = (
        rest[r] for r in range(6)
    )

    embeds = lax.dynamic_slice_in_dim(
        jnp.take(time_table, steps_all, axis=0), dp * out_rows, out_rows, axis=1
    ).astype(f32)
    grad_t_query = jnp.dot(embeds.T, image_sums[:, :group], precision=HIGHEST)
    grad_t_value = jnp.dot(embeds.T, image_sums[:, group : 2 * group], precision=HIGHEST)
    onehot = (
        steps_all[:, None] == jnp.arange(table_rows, dtype=jnp.int32)[None, :]
    ).astype(f32)
    grad_time_table = jnp.dot(onehot.T, embed_rows, precision=HIGHEST)

    return (
        result[None],
        grad_tokens[None],
        grad_qkv[:, 0],
        grad_qkv[:, 1],
        grad_qkv[:, 2],
        grad_t_query,
        grad_t_value,
        grad_w_out,
        grad_w_up,
        grad_w_down,
        grad_gain_one,
        grad_shift_one,
        grad_b_query,
        grad_b_value,
        grad_b_out,
        grad_gain_two,
        grad_shift_two,
        grad_b_up,
        grad_b_down,
        grad_bias_table,
        grad_time_table,
    )


def solution(mesh):
    split, copied, by_block = P("dp", "seq", None), P(), P("dp", "seq")
    in_specs = (split, P("dp"), P("seq", None)) + (copied,) * 19 + (split,)
    out_specs = (split, split) + (by_block,) * 8 + (copied,) * 11
    return jax.shard_map(
        per_device, mesh=mesh, in_specs=in_specs, out_specs=out_specs, check_vma=False
    )
```

```python
from functools import partial

import jax
import jax.numpy as jnp
from jax import lax
from jax.experimental import pallas as pl
from jax.experimental.pallas import tpu as pltpu
from jax.sharding import PartitionSpec as P

GRID = 32
SPAN = 2 * GRID - 1
STRIP = 2 * GRID * GRID
LANES = 128
BLOCK = 256
NORM_EPS = 1e-06
f32, bf16 = jnp.float32, jnp.bfloat16
HIGHEST = lax.Precision.HIGHEST
SCALE = 0.2
VMEM_LIMIT = 58 * 1024 * 1024


def dot(left, right, left_dim=1, right_dim=0):
    return lax.dot_general(
        left, right, (((left_dim,), (right_dim,)), ((), ())), preferred_element_type=f32
    )


def normalize(values):
    centered = values - jnp.mean(values, axis=-1, keepdims=True)
    scaled = lax.rsqrt(jnp.mean(centered * centered, axis=-1, keepdims=True) + NORM_EPS)
    return centered * scaled, scaled


def norm_back(grad_norm, normed, scaled, gain):
    inner = grad_norm * gain
    return scaled * (
        inner
        - jnp.mean(inner, axis=-1, keepdims=True)
        - normed * jnp.mean(inner * normed, axis=-1, keepdims=True)
    )


def row_of(ref):
    return ref[...].reshape(1, ref.shape[0])


def fold_rows(values, op):
    return op(values.reshape(values.shape[0] // 8, 8, values.shape[1]), axis=0)


def strip_place(key_row):
    first = (GRID - 1 - key_row) * GRID
    return (first % LANES) // GRID, first // LANES * LANES


def widen(rows, height):
    fill = jnp.zeros((height - rows.shape[0], rows.shape[1]), rows.dtype)
    return jnp.concatenate([rows, fill], axis=0)


def rows_for(group, half, count):
    return pl.ds(pl.multiple_of((2 * group + half) * count, 16), count)


def block_of(index):
    return pl.ds(pl.multiple_of(index * BLOCK, BLOCK), BLOCK)


def build_permutation(place_ref, perm):
    length = perm.shape[0]

    def rows_of(i, carry):
        first = pl.multiple_of(i * BLOCK, BLOCK)
        spots = lax.broadcasted_iota(jnp.int32, (BLOCK, length), 0) + first
        hit = spots == place_ref[...]
        perm[pl.ds(first, BLOCK), :] = jnp.where(hit, 1.0, 0.0).astype(bf16)
        return carry

    lax.fori_loop(0, length // BLOCK, rows_of, 0)


def strips_kernel(table_ref, strips_ref):
    lane = lax.broadcasted_iota(jnp.int32, (GRID, LANES), 1)
    per_tile = LANES // GRID

    def tile_of(n):
        whole_tile = jnp.zeros((GRID, LANES), f32)
        for k in range(per_tile):
            row = table_ref[0, pl.ds(per_tile * n + k, 1), :]
            turned = pltpu.roll(
                jnp.broadcast_to(row, (GRID, LANES)),
                (GRID * k - GRID + 1) % LANES,
                1,
                stride=1,
                stride_axis=0,
            )
            whole_tile = jnp.where(lane // GRID == k, turned, whole_tile)
        return whole_tile

    tiles = [tile_of(n) for n in range(STRIP // LANES + 1)]
    for n in range(STRIP // LANES):
        span = slice(n * LANES, (n + 1) * LANES)
        strips_ref[0, 0, :, span] = tiles[n]
        for s in range(1, per_tile):
            back = LANES - GRID * s
            strips_ref[0, s, :, span] = jnp.where(
                lane < back, pltpu.roll(tiles[n], back, 1), pltpu.roll(tiles[n + 1], back, 1)
            )


def fold_strips(strips, table_ref):
    lane = lax.broadcasted_iota(jnp.int32, (GRID, LANES), 1)
    row = lax.broadcasted_iota(jnp.int32, (8, LANES), 0)
    per_tile = LANES // GRID

    before = [jnp.zeros((GRID, LANES), f32)] * (per_tile - 1)
    for n in range(STRIP // LANES):
        span = slice(n * LANES, (n + 1) * LANES)
        total = strips[0, 0, :, span]
        turned = []
        for s in range(1, per_tile):
            turned.append(pltpu.roll(strips[0, s, :, span], GRID * s, 1))
            total = total + jnp.where(lane >= GRID * s, turned[-1], before[s - 1])
        before = turned
        for parity in range(2):
            part = jnp.where(lane // GRID % 2 == parity, total, 0.0)
            if parity:
                part = pltpu.roll(part, LANES - GRID, 1)
            part = pltpu.roll(part[:16], 16, 1) + part[16:]
            part = pltpu.roll(part[:8], 8, 1) + part[8:]
            for step in (4, 2, 1):
                part = jnp.where(row % (2 * step) < step, pltpu.roll(part, step, 1), part)
            table_ref[0, parity, n : n + 1, :] = jnp.sum(part, axis=0, keepdims=True)


def project_kernel(
    scale,
    groups,
    seq_ref,
    x_ref,
    embed_ref,
    gain_ref,
    shift_ref,
    b_query_ref,
    b_value_ref,
    wk_hbm,
    wq_hbm,
    tq_hbm,
    wv_hbm,
    tv_hbm,
    *refs,
):
    outs, (hat_ref, held, turned, sems) = refs[: 2 * groups], refs[2 * groups :]
    sources = (wk_hbm, wq_hbm, tq_hbm, wv_hbm, tv_hbm)
    copies = [
        pltpu.make_async_copy(source, held.at[n], sems.at[n]) for n, source in enumerate(sources)
    ]
    for copy in copies:
        copy.start()
    hat, _ = normalize(x_ref[...].astype(f32))
    hat_ref[...] = hat.astype(bf16)
    act = (hat * row_of(gain_ref) + row_of(shift_ref)).astype(bf16)
    embed = jnp.broadcast_to(embed_ref[...].astype(f32), (16, embed_ref.shape[1])).astype(bf16)
    count = outs[0].shape[0] // 3
    seq = seq_ref[0]

    def put(which, value):
        turned[which] = jnp.transpose(value.astype(bf16))
        for k in range(groups):
            for h in range(2):
                outs[h * groups + k][which * count : (which + 1) * count, :] = turned[
                    which, rows_for(k ^ seq, h, count), :
                ]

    copies[0].wait()
    put(1, dot(act, held[0]))
    copies[1].wait()
    copies[2].wait()
    time_query = dot(embed, held[2])[0:1]
    put(0, (dot(act, held[1]) + time_query + row_of(b_query_ref)) * scale)
    copies[3].wait()
    copies[4].wait()
    time_value = dot(embed, held[4])[0:1]
    put(2, dot(act, held[3]) + time_value + row_of(b_value_ref))


def attend_kernel(
    head_size,
    groups,
    seq_ref,
    place_ref,
    strips_ref,
    *refs,
):
    own, outs = refs[:groups], refs[groups : 2 * groups]
    qkv_ref, expo_ref, inverse_ref, mixed_ref = refs[2 * groups : 2 * groups + 4]
    perm, by_place, query_s, key_s, value_s, scores_s = refs[2 * groups + 4 :]
    seq = seq_ref[0]
    head = pl.program_id(0)
    group, length = mixed_ref.shape
    tiles = length // BLOCK

    @pl.when(head == 0)
    def _():
        build_permutation(place_ref, perm)

        def arrange(i, carry):
            span = pl.ds(pl.multiple_of(i * BLOCK, BLOCK), BLOCK)
            part = jnp.zeros((3 * group, BLOCK), f32)
            for k in range(groups):
                part = part + dot(own[k][...], perm[span, block_of(k ^ seq)], 1, 1)
            by_place[:, span] = part
            qkv_ref[:, span] = part.astype(bf16)
            return carry

        lax.fori_loop(0, tiles, arrange, 0)

    def rows_of(which):
        first = pl.multiple_of(which * group + head * head_size, 8)
        return by_place[pl.ds(first, head_size), :]

    query_s[...] = widen(rows_of(0), LANES).astype(bf16)
    key_s[...] = jnp.transpose(widen(rows_of(1), LANES)).astype(bf16)
    value_s[...] = widen(rows_of(2), value_s.shape[0]).astype(bf16)
    own_rows = pl.ds(pl.multiple_of(head * head_size, 8), head_size)

    def tile(t, carry):
        first = pl.multiple_of(t * BLOCK, BLOCK)
        span = pl.ds(first, BLOCK)
        query = query_s[:, span]
        peak = jnp.full((8, BLOCK), -jnp.inf, f32)
        for c in range(tiles):
            keys = slice(c * BLOCK, (c + 1) * BLOCK)
            pieces = []
            for key_row in range(c * BLOCK // GRID, (c + 1) * BLOCK // GRID):
                shift, start = strip_place(key_row)
                pieces.append(strips_ref[0, shift, :, pl.ds(first + start, BLOCK)])
            scores = dot(key_s[keys, :], query) + jnp.concatenate(pieces, axis=0)
            scores_s[keys, :] = scores
            peak = jnp.maximum(peak, fold_rows(scores, jnp.max))
        peak = jnp.max(peak, axis=0, keepdims=True)
        total = jnp.zeros((8, BLOCK), f32)
        mixed = jnp.zeros((value_s.shape[0], BLOCK), f32)
        for c in range(tiles):
            keys = slice(c * BLOCK, (c + 1) * BLOCK)
            expo = jnp.exp(scores_s[keys, :] - peak)
            total = total + fold_rows(expo, jnp.sum)
            low = expo.astype(bf16)
            expo_ref[0, keys, span] = low
            mixed = mixed + dot(value_s[:, keys], low)
        inverse = 1.0 / jnp.sum(total, axis=0, keepdims=True)
        inverse_ref[0, :, span] = inverse
        mixed_ref[own_rows, span] = (mixed * inverse)[:head_size]
        return carry

    lax.fori_loop(0, tiles, tile, 0)

    @pl.when(head == pl.num_programs(0) - 1)
    def _():
        low = mixed_ref[...].astype(bf16)
        for k in range(groups):
            outs[k][...] = dot(low, perm[:, block_of(k ^ seq)]).astype(bf16)


def attend_back_kernel(
    head_size,
    groups,
    seq_ref,
    qkv_ref,
    expo_ref,
    inverse_ref,
    mixed_ref,
    place_ref,
    *refs,
):
    given, outs = refs[:groups], refs[groups : 2 * groups]
    (
        table_ref,
        sums_ref,
        strips_ref,
        perm,
        by_place,
        grad_place,
        grads,
        query_s,
        key_s,
        value_s,
        grad_s,
        grad_t,
        offset_s,
        grad_key,
        grad_value,
    ) = refs[2 * groups :]
    seq = seq_ref[0]
    head = pl.program_id(0)
    group, length = mixed_ref.shape
    tiles = length // BLOCK
    scale = head_size ** (-0.5)

    @pl.when(head == 0)
    def _():
        build_permutation(place_ref, perm)

        def arrange(i, carry):
            span = pl.ds(pl.multiple_of(i * BLOCK, BLOCK), BLOCK)
            part = jnp.zeros((group, BLOCK), f32)
            for k in range(groups):
                part = part + dot(given[k][...], perm[span, block_of(k ^ seq)], 1, 1)
            grad_place[:, span] = part
            by_place[:, span] = qkv_ref[:, span].astype(f32)
            return carry

        lax.fori_loop(0, tiles, arrange, 0)

    own_rows = pl.ds(pl.multiple_of(head * head_size, 8), head_size)

    def rows_of(which):
        first = pl.multiple_of(which * group + head * head_size, 8)
        return by_place[pl.ds(first, head_size), :]

    query_s[...] = jnp.transpose(widen(rows_of(0), LANES)).astype(bf16)
    key_s[...] = widen(rows_of(1), key_s.shape[0]).astype(bf16)
    value_s[...] = jnp.transpose(widen(rows_of(2), LANES)).astype(bf16)
    grad = grad_place[own_rows, :]
    inverse = inverse_ref[0]
    offset_s[...] = inverse * jnp.sum(grad * mixed_ref[own_rows, :], axis=0, keepdims=True)
    grad = widen(grad * inverse, LANES)
    grad_s[...] = grad.astype(bf16)
    grad_t[...] = jnp.transpose(grad).astype(bf16)
    grad_key[...] = jnp.zeros_like(grad_key)
    grad_value[...] = jnp.zeros_like(grad_value)
    strips_ref[...] = jnp.zeros_like(strips_ref)

    def tile(t, carry):
        first = pl.multiple_of(t * BLOCK, BLOCK)
        span = pl.ds(first, BLOCK)
        grad_tile = grad_s[:, span]
        offset = offset_s[:, span]
        grad_query = jnp.zeros((key_s.shape[0], BLOCK), f32)
        for c in range(tiles):
            keys = slice(c * BLOCK, (c + 1) * BLOCK)
            expo = expo_ref[0, keys, span]
            grad_scores = expo.astype(f32) * (dot(value_s[keys, :], grad_tile) - offset)
            for row in range(BLOCK // GRID):
                shift, start = strip_place(c * BLOCK // GRID + row)
                strips_ref[0, shift, :, pl.ds(first + start, BLOCK)] += grad_scores[
                    row * GRID : (row + 1) * GRID
                ]
            low = grad_scores.astype(bf16)
            grad_query = grad_query + dot(key_s[:, keys], low)
            grad_key[keys, :] += dot(low, query_s[span, :])
            grad_value[keys, :] += dot(expo, grad_t[span, :])
        grads[own_rows, span] = grad_query[:head_size] * scale
        return carry

    lax.fori_loop(0, tiles, tile, 0)
    for which, total in ((1, grad_key), (2, grad_value)):
        first = pl.multiple_of(which * group + head * head_size, 8)
        grads[pl.ds(first, head_size), :] = jnp.transpose(total[...])[:head_size]

    @pl.when(head >= 0)
    def _():
        fold_strips(strips_ref, table_ref)

    @pl.when(head == pl.num_programs(0) - 1)
    def _():
        low = grads[...].astype(bf16)
        sums_ref[...] = dot(jnp.ones((8, length), bf16), low, 1, 1)
        for k in range(groups):
            outs[k][...] = dot(low, perm[:, block_of(k ^ seq)]).astype(bf16)


def mlp_first_kernel(
    groups,
    step,
    seq_ref,
    x_ref,
    dy_ref,
    b_out_ref,
    gain_ref,
    shift_ref,
    b_up_ref,
    w_out_hbm,
    w_up_hbm,
    w_down_hbm,
    *refs,
):
    given = refs[: 2 * groups]
    act_hbm, act_t_hbm, inner_hbm, turned_ref, middle_ref, up_sum_ref = refs[
        2 * groups : 2 * groups + 6
    ]
    (
        w_out_s,
        w_up_s,
        w_down_s,
        act_s,
        act_t_s,
        inner_s,
        norm_s,
        sem,
        up_sems,
        down_sems,
        act_sems,
        act_t_sems,
        inner_sems,
    ) = refs[2 * groups + 6 :]
    chunks = w_up_s.shape[0]
    seq = seq_ref[0]

    def span_of(i):
        return pl.ds(pl.multiple_of(i * step, step), step)

    def fetch(i):
        return (
            pltpu.make_async_copy(w_up_hbm.at[:, span_of(i)], w_up_s.at[i], up_sems.at[i]),
            pltpu.make_async_copy(w_down_hbm.at[span_of(i), :], w_down_s.at[i], down_sems.at[i]),
        )

    def put(i):
        return (
            pltpu.make_async_copy(act_s.at[i], act_hbm.at[:, span_of(i)], act_sems.at[i]),
            pltpu.make_async_copy(act_t_s.at[i], act_t_hbm.at[span_of(i), :], act_t_sems.at[i]),
            pltpu.make_async_copy(inner_s.at[i], inner_hbm.at[:, span_of(i)], inner_sems.at[i]),
        )

    def begin(i, carry):
        for copy in fetch(i):
            copy.start()
        return carry

    out_copy = pltpu.make_async_copy(w_out_hbm, w_out_s, sem.at[0])
    out_copy.start()
    lax.fori_loop(0, chunks, begin, 0)
    count = given[0].shape[0]
    for k in range(groups):
        for h in range(2):
            turned_ref[1, rows_for(k ^ seq, h, count), :] = given[h * groups + k][...]
    mixed = jnp.transpose(turned_ref[1])
    out_copy.wait()
    middle = x_ref[...].astype(f32) + dot(mixed, w_out_s[...]) + row_of(b_out_ref)
    hat, _ = normalize(middle)
    middle_ref[...] = middle
    norm = (hat * row_of(gain_ref) + row_of(shift_ref)).astype(bf16)
    norm_s[...] = norm
    turned_ref[0] = jnp.transpose(norm)

    def chunk(i, carry):
        for copy in fetch(i):
            copy.wait()
        inner = dot(norm_s[...], w_up_s[i]) + b_up_ref[:, span_of(i)]
        cdf = 0.5 * (1.0 + lax.erf(inner * (0.5**0.5)))
        pdf = jnp.exp(-0.5 * inner * inner) * 0.3989422804014327
        act = (inner * cdf).astype(bf16)
        low = (dot(dy_ref[...], w_down_s[i], 1, 1) * (cdf + inner * pdf)).astype(bf16)
        act_s[i] = act
        act_t_s[i] = jnp.transpose(act)
        inner_s[i] = low
        up_sum_ref[:, span_of(i)] = jnp.sum(low.astype(f32), axis=0, keepdims=True)
        for copy in put(i):
            copy.start()
        return carry

    lax.fori_loop(0, chunks, chunk, 0)

    def finish(i, carry):
        for copy in put(i):
            copy.wait()
        return carry

    lax.fori_loop(0, chunks, finish, 0)


def mlp_second_kernel(
    groups,
    step,
    seq_ref,
    middle_ref,
    dy_ref,
    b_down_ref,
    gain_ref,
    act_ref,
    inner_ref,
    w_out_hbm,
    w_up_hbm,
    w_down_hbm,
    *refs,
):
    outs = refs[:groups]
    result_ref, grad_middle_ref, branch_ref, sums_ref = refs[groups : groups + 4]
    (
        w_out_s,
        w_up_s,
        w_down_s,
        result_s,
        grad_s,
        mixed_s,
        sem,
        up_sems,
        down_sems,
    ) = refs[groups + 4 :]
    chunks = w_up_s.shape[0]

    def span_of(i):
        return pl.ds(pl.multiple_of(i * step, step), step)

    def fetch(i):
        return (
            pltpu.make_async_copy(w_up_hbm.at[:, span_of(i)], w_up_s.at[i], up_sems.at[i]),
            pltpu.make_async_copy(w_down_hbm.at[span_of(i), :], w_down_s.at[i], down_sems.at[i]),
        )

    def begin(i, carry):
        for copy in fetch(i):
            copy.start()
        return carry

    lax.fori_loop(0, chunks, begin, 0)
    out_copy = pltpu.make_async_copy(w_out_hbm, w_out_s, sem.at[0])
    out_copy.start()
    result_s[...] = middle_ref[...] + row_of(b_down_ref)
    grad_s[...] = jnp.zeros_like(grad_s)

    def chunk(i, carry):
        for copy in fetch(i):
            copy.wait()
        result_s[...] += dot(act_ref[:, span_of(i)], w_down_s[i])
        grad_s[...] += dot(inner_ref[:, span_of(i)], w_up_s[i], 1, 1)
        return carry

    lax.fori_loop(0, chunks, chunk, 0)
    result_ref[...] = result_s[...].astype(bf16)
    hat, scaled = normalize(middle_ref[...])
    dy = dy_ref[...].astype(f32)
    grad_norm = grad_s[...]
    grad_middle = dy + norm_back(grad_norm, hat, scaled, row_of(gain_ref))
    branch = grad_middle.astype(bf16)
    grad_middle_ref[...] = grad_middle
    branch_ref[...] = branch
    out_copy.wait()
    mixed_s[...] = dot(w_out_s[...], branch, 1, 1).astype(bf16)
    count = outs[0].shape[0]
    for k in range(groups):
        rows = pl.ds(pl.multiple_of((k ^ seq_ref[0]) * count, 16), count)
        outs[k][...] = mixed_s[rows, :]
    sums_ref[...] = jnp.concatenate(
        [
            jnp.sum(dy, axis=0, keepdims=True),
            jnp.sum(grad_norm * hat, axis=0, keepdims=True),
            jnp.sum(grad_norm, axis=0, keepdims=True),
            jnp.sum(branch.astype(f32), axis=0, keepdims=True),
            jnp.zeros((4, dy.shape[1]), f32),
        ],
        axis=0,
    )


def pair_grad_kernel(
    first_ref,
    own_ref,
    other_ref,
    inner_ref,
    inner_other,
    branch_ref,
    branch_other,
    out_ref,
    own_s,
    other_s,
):
    step = pl.program_id(0)
    last = pl.num_programs(0) - 1
    blocks = first_ref.shape[0]
    count = own_s.shape[0] // blocks

    def choose(which):
        for n in range(blocks):
            source = pl.ds(pl.multiple_of(first_ref[n], 16), count)
            own_s[n * count : (n + 1) * count, :] = own_ref[which, source, :]
            other_s[n * count : (n + 1) * count, :] = other_ref[which, source, :]

    def put(right, right_other):
        low = (dot(own_s[...], right[...]) + dot(other_s[...], right_other[...])).astype(bf16)
        for n in range(blocks):
            out_ref[n, 0] = low[n * count : (n + 1) * count]

    @pl.when(step == 0)
    def _():
        choose(0)

    @pl.when(step < last)
    def _():
        put(inner_ref, inner_other)

    @pl.when(step == last)
    def _():
        choose(1)
        put(branch_ref, branch_other)


def down_grad_kernel(act_ref, dy_ref, out_ref):
    total = dot(act_ref[0], dy_ref[0])
    for source in range(1, act_ref.shape[0]):
        total = total + dot(act_ref[source], dy_ref[source])
    out_ref[...] = jnp.transpose(total.astype(bf16))


def qkv_grad_kernel(groups, seq_ref, hat_ref, gain_ref, shift_ref, *refs):
    sources, given = refs[:5], refs[5 : 2 * groups + 5]
    out_ref, norms_ref, held, turned, sems = refs[2 * groups + 5 :]
    seq = seq_ref[0]
    count = given[0].shape[0]
    rows = count // 3
    skipped = lax.rem(2 * rows * seq, LANES)
    window = pl.ds(pl.multiple_of(2 * rows * seq - skipped, LANES), held.shape[2])
    copies = [
        pltpu.make_async_copy(source.at[:, window], held.at[n], sems.at[n])
        for n, source in enumerate(sources)
    ]
    for copy in copies:
        copy.start()
    gain, shift = row_of(gain_ref), row_of(shift_ref)
    grad_gain, grad_shift = jnp.zeros_like(gain), jnp.zeros_like(shift)
    grad_embed = jnp.zeros_like(gain)
    for n, copy in enumerate(copies):
        copy.wait()
        turned[n] = jnp.transpose(held[n])
    for h in range(2):
        span = slice(h * count, (h + 1) * count)
        product = jnp.zeros((count, hat_ref.shape[2]), f32)
        sums = jnp.zeros((count, 1), f32)
        for k in range(groups):
            grads = given[h * groups + k][...]
            product = product + dot(grads, hat_ref[k ^ seq])
            sums = sums + jnp.sum(grads.astype(f32), axis=1, keepdims=True)
        out_ref[:, span] = jnp.transpose((product * gain + sums * shift).astype(bf16))
        for n in range(3):
            own = slice(n * rows, (n + 1) * rows)
            first = pl.multiple_of(skipped + h * rows, 16)
            weight = turned[n, pl.ds(first, rows), :].astype(f32)
            grad_gain = grad_gain + jnp.sum(weight * product[own], axis=0, keepdims=True)
            grad_shift = grad_shift + jnp.sum(weight * sums[own], axis=0, keepdims=True)
        for n, which in ((3, 0), (4, 2)):
            own = slice(which * rows, (which + 1) * rows)
            first = pl.multiple_of(skipped + h * rows, 16)
            weight = turned[n, pl.ds(first, rows), :].astype(f32)
            grad_embed = grad_embed + jnp.sum(weight * sums[own], axis=0, keepdims=True)
    norms_ref[...] = jnp.concatenate(
        [grad_gain, grad_shift, grad_embed, jnp.zeros((5, gain.shape[1]), f32)], axis=0
    )


def qkv_total_kernel(parts_ref, *out_refs):
    total = parts_ref[0].astype(f32)
    for n in range(1, parts_ref.shape[0]):
        total = total + parts_ref[n].astype(f32)
    count = out_refs[0].shape[1] // 2
    for n, out_ref in enumerate(out_refs):
        second = (n + 3) * count
        out_ref[...] = jnp.concatenate(
            [total[:, n * count : (n + 1) * count], total[:, second : second + count]], axis=1
        )


def tokens_kernel(groups, seq_ref, x_ref, middle_ref, gain_ref, wq_hbm, wk_hbm, wv_hbm, *refs):
    given, (out_ref, held, grads_s, sems) = refs[: 2 * groups], refs[2 * groups :]
    copies = [
        pltpu.make_async_copy(source, held.at[n], sems.at[n])
        for n, source in enumerate((wq_hbm, wk_hbm, wv_hbm))
    ]
    for copy in copies:
        copy.start()
    seq = seq_ref[0]
    count = given[0].shape[0] // 3
    for k in range(groups):
        for h in range(2):
            for which in range(3):
                grads_s[which, rows_for(k ^ seq, h, count), :] = given[h * groups + k][
                    which * count : (which + 1) * count
                ]
    hat, scaled = normalize(x_ref[...].astype(f32))
    total = jnp.zeros(middle_ref.shape, f32)
    for which, copy in enumerate(copies):
        grads = jnp.transpose(grads_s[which])
        copy.wait()
        total = total + dot(grads, held[which], 1, 1)
    out_ref[...] = (
        middle_ref[...] + norm_back(total, hat, scaled, row_of(gain_ref))
    ).astype(bf16)


def whole(shape):
    zeros = (0,) * len(shape)
    return pl.BlockSpec(shape, lambda s: zeros, pipeline_mode=pl.Buffered(1))


def kept(shape):
    zeros = (0,) * len(shape)
    return pl.BlockSpec(shape, lambda s: zeros)


def per_head(shape):
    rest = (0,) * (len(shape) - 1)
    return pl.BlockSpec((1,) + tuple(shape[1:]), lambda s: (s,) + rest)


def params(grid=True):
    return pltpu.CompilerParams(
        dimension_semantics=("arbitrary",) if grid else None, vmem_limit_bytes=VMEM_LIMIT
    )


def takes(microseconds):
    return pl.CostEstimate(
        flops=int(microseconds * SCALE * 1e9), bytes_accessed=int(microseconds * SCALE * 3e6), transcendentals=0
    )


IN_VMEM = pl.BlockSpec(memory_space=pltpu.VMEM)
IN_SMEM = pl.BlockSpec(memory_space=pltpu.SMEM)
IN_HBM = pl.BlockSpec(memory_space=pl.ANY)


def shape_of(shape, kind):
    return jax.ShapeDtypeStruct(shape, kind)


def bias_strips(table):
    heads = table.shape[0]
    out = shape_of((heads, LANES // GRID, GRID, STRIP), f32)
    return pl.pallas_call(
        strips_kernel,
        grid=(heads,),
        in_specs=[per_head(table.shape)],
        out_specs=per_head(out.shape),
        out_shape=out,
        compiler_params=params(),
        cost_estimate=takes(9),
        name="strips",
    )(table)


def project(seq, x, embed, vectors, weights, groups, scale):
    count, width = x.shape
    part = shape_of((3 * width // groups // 2, count), bf16)
    outs = pl.pallas_call(
        partial(project_kernel, scale, groups),
        in_specs=[IN_SMEM] + [IN_VMEM] * 6 + [IN_HBM] * 5,
        out_specs=[IN_VMEM] * (2 * groups + 1),
        out_shape=(part,) * (2 * groups) + (shape_of((count, width), bf16),),
        scratch_shapes=[
            pltpu.VMEM((5, width, width), bf16),
            pltpu.VMEM((3, width, count), bf16),
            pltpu.SemaphoreType.DMA((5,)),
        ],
        compiler_params=params(False),
        cost_estimate=takes(9),
        name="project",
    )(seq, x, embed, *vectors, *weights)
    return outs[:groups], outs[groups : 2 * groups], outs[2 * groups]


def attend(seq, own, place, strips, half, head_size):
    heads = strips.shape[0] // 2
    length = place.shape[1]
    group = heads * head_size
    groups = len(own)
    tall = -(-head_size // 16) * 16
    saved = (
        shape_of((3 * group, length), bf16),
        shape_of((heads, length, length), bf16),
        shape_of((heads, 1, length), f32),
        shape_of((group, length), f32),
    )
    own_strips = pl.BlockSpec(
        (1,) + strips.shape[1:], lambda s: (half * heads + s, 0, 0, 0)
    )
    outs = pl.pallas_call(
        partial(attend_kernel, head_size, groups),
        grid=(heads,),
        in_specs=[IN_SMEM, whole(place.shape), own_strips] + [whole(a.shape) for a in own],
        out_specs=[kept((group, BLOCK))] * groups
        + [
            kept(saved[0].shape),
            per_head(saved[1].shape),
            per_head(saved[2].shape),
            kept(saved[3].shape),
        ],
        out_shape=(shape_of((group, BLOCK), bf16),) * groups + saved,
        scratch_shapes=[
            pltpu.VMEM((length, length), bf16),
            pltpu.VMEM((3 * group, length), f32),
            pltpu.VMEM((LANES, length), bf16),
            pltpu.VMEM((length, LANES), bf16),
            pltpu.VMEM((tall, length), bf16),
            pltpu.VMEM((length, BLOCK), f32),
        ],
        compiler_params=params(),
        cost_estimate=takes(13),
        name="attend",
    )(seq, place, strips, *own)
    return outs[:groups], outs[groups:]


def attend_back(seq, half, grad_mixed, qkv, expo, inverse, mixed, place, head_size):
    heads, length, _ = expo.shape
    group = heads * head_size
    groups = len(grad_mixed)
    tall = -(-head_size // 16) * 16
    table = shape_of((heads, 2, STRIP // LANES, LANES), f32)
    given = pl.BlockSpec((group, BLOCK), lambda s: (half, 0), pipeline_mode=pl.Buffered(1))
    outs = pl.pallas_call(
        partial(attend_back_kernel, head_size, groups),
        grid=(heads,),
        in_specs=[
            IN_SMEM,
            whole(qkv.shape),
            per_head(expo.shape),
            per_head(inverse.shape),
            whole(mixed.shape),
            whole(place.shape),
        ]
        + [given] * groups,
        out_specs=[kept((3 * group, BLOCK))] * groups
        + [per_head(table.shape), kept((8, 3 * group))],
        out_shape=(shape_of((3 * group, BLOCK), bf16),) * groups
        + (table, shape_of((8, 3 * group), f32)),
        scratch_shapes=[
            pltpu.VMEM((1, LANES // GRID, GRID, STRIP), f32),
            pltpu.VMEM((length, length), bf16),
            pltpu.VMEM((3 * group, length), f32),
            pltpu.VMEM((group, length), f32),
            pltpu.VMEM((3 * group, length), f32),
            pltpu.VMEM((length, LANES), bf16),
            pltpu.VMEM((tall, length), bf16),
            pltpu.VMEM((length, LANES), bf16),
            pltpu.VMEM((LANES, length), bf16),
            pltpu.VMEM((length, LANES), bf16),
            pltpu.VMEM((1, length), f32),
            pltpu.VMEM((length, LANES), f32),
            pltpu.VMEM((length, LANES), f32),
        ],
        compiler_params=params(),
        cost_estimate=takes(16),
        name="attend_back",
    )(seq, qkv, expo, inverse, mixed, place, *grad_mixed)
    return outs[:groups], outs[groups:]


def mlp_first(seq, mixed, x, dy, vectors, b_up, w_out, w_up, w_down):
    count, width = x.shape
    hidden = w_up.shape[1]
    step = 512
    chunks = hidden // step
    dma = pltpu.SemaphoreType.DMA
    return pl.pallas_call(
        partial(mlp_first_kernel, len(mixed) // 2, step),
        in_specs=[IN_SMEM] + [IN_VMEM] * 6 + [IN_HBM] * 3 + [IN_VMEM] * len(mixed),
        out_specs=[IN_HBM] * 3 + [IN_VMEM] * 3,
        out_shape=(
            shape_of((count, hidden), bf16),
            shape_of((hidden, count), bf16),
            shape_of((count, hidden), bf16),
            shape_of((2, width, count), bf16),
            shape_of((count, width), f32),
            shape_of((1, hidden), f32),
        ),
        scratch_shapes=[
            pltpu.VMEM((width, width), bf16),
            pltpu.VMEM((chunks, width, step), bf16),
            pltpu.VMEM((chunks, step, width), bf16),
            pltpu.VMEM((chunks, count, step), bf16),
            pltpu.VMEM((chunks, step, count), bf16),
            pltpu.VMEM((chunks, count, step), bf16),
            pltpu.VMEM((count, width), bf16),
            dma((1,)),
        ]
        + [dma((chunks,))] * 5,
        compiler_params=params(False),
        cost_estimate=takes(14),
        name="mlp_first",
    )(seq, x, dy, *vectors, b_up, w_out, w_up, w_down, *mixed)


def mlp_second(seq, middle, dy, vectors, act, inner, w_out, w_up, w_down, groups):
    count, width = middle.shape
    hidden = w_up.shape[1]
    step = 512
    chunks = hidden // step
    part = shape_of((width // groups, count), bf16)
    dma = pltpu.SemaphoreType.DMA
    outs = pl.pallas_call(
        partial(mlp_second_kernel, groups, step),
        in_specs=[IN_SMEM] + [IN_VMEM] * 6 + [IN_HBM] * 3,
        out_specs=[IN_VMEM] * (groups + 4),
        out_shape=(part,) * groups
        + (
            shape_of((count, width), bf16),
            shape_of((count, width), f32),
            shape_of((count, width), bf16),
            shape_of((8, width), f32),
        ),
        scratch_shapes=[
            pltpu.VMEM((width, width), bf16),
            pltpu.VMEM((chunks, width, step), bf16),
            pltpu.VMEM((chunks, step, width), bf16),
            pltpu.VMEM((count, width), f32),
            pltpu.VMEM((count, width), f32),
            pltpu.VMEM((width, count), bf16),
            dma((1,)),
            dma((chunks,)),
            dma((chunks,)),
        ],
        compiler_params=params(False),
        cost_estimate=takes(14),
        name="mlp_second",
    )(seq, middle, dy, *vectors, act, inner, w_out, w_up, w_down)
    return outs[:groups], outs[groups:]


def pair_grad(first, own, other, inner, inner_other, branch, branch_other, groups):
    _, rows, count = own.shape
    blocks = first.shape[0]
    width = inner.shape[1] // groups
    wide = pl.BlockSpec((count, width), lambda s, first_ref: (0, jnp.minimum(s, groups - 1)))
    narrow = pl.BlockSpec((count, width), lambda s, first_ref: (0, 0))
    left = pl.BlockSpec((2, rows, count), lambda s, first_ref: (0, 0, 0))
    block = (blocks, 1, rows // 2 // blocks, width)
    return pl.pallas_call(
        pair_grad_kernel,
        grid_spec=pltpu.PrefetchScalarGridSpec(
            num_scalar_prefetch=1,
            grid=(groups + 1,),
            in_specs=[left, left, wide, wide, narrow, narrow],
            out_specs=pl.BlockSpec(block, lambda s, first_ref: (0, s, 0, 0)),
            scratch_shapes=[pltpu.VMEM((rows // 2, count), bf16)] * 2,
        ),
        out_shape=shape_of((blocks, groups + 1) + block[2:], bf16),
        compiler_params=params(),
        cost_estimate=takes(10),
        name="pair_grad",
    )(first, own, other, inner, inner_other, branch, branch_other)


def down_grad(act, dy):
    return pl.pallas_call(
        down_grad_kernel,
        in_specs=[IN_VMEM, IN_VMEM],
        out_specs=IN_VMEM,
        out_shape=shape_of((dy.shape[2], act.shape[1]), bf16),
        compiler_params=params(False),
        cost_estimate=takes(8),
        name="down_grad",
    )(act, dy)


def qkv_grad(seq, grads, hat, gain, shift, weights):
    width = hat.shape[2]
    count = grads[0].shape[0]
    columns = -(-(2 * count // 3 + LANES - GRID) // LANES) * LANES
    return pl.pallas_call(
        partial(qkv_grad_kernel, len(grads) // 2),
        in_specs=[IN_SMEM] + [IN_VMEM] * 3 + [IN_HBM] * 5 + [IN_VMEM] * len(grads),
        out_specs=[IN_VMEM] * 2,
        out_shape=(shape_of((width, 2 * count), bf16), shape_of((8, width), f32)),
        scratch_shapes=[
            pltpu.VMEM((5, width, columns), bf16),
            pltpu.VMEM((5, columns, width), bf16),
            pltpu.SemaphoreType.DMA((5,)),
        ],
        compiler_params=params(False),
        cost_estimate=takes(8),
        name="qkv_grad",
    )(seq, hat, gain, shift, *weights, *grads)


def qkv_total(parts):
    _, rows, columns = parts.shape
    return pl.pallas_call(
        qkv_total_kernel,
        out_shape=(shape_of((rows, columns // 3), f32),) * 3,
        compiler_params=params(False),
        cost_estimate=takes(2),
        name="qkv_total",
    )(parts)


def token_grad(seq, grads, x, middle, gain, weights):
    count, width = x.shape
    return pl.pallas_call(
        partial(tokens_kernel, len(grads) // 2),
        in_specs=[IN_SMEM] + [IN_VMEM] * 3 + [IN_HBM] * 3 + [IN_VMEM] * len(grads),
        out_specs=IN_VMEM,
        out_shape=shape_of((count, width), bf16),
        scratch_shapes=[
            pltpu.VMEM((3, width, width), bf16),
            pltpu.VMEM((3, width, count), bf16),
            pltpu.SemaphoreType.DMA((3,)),
        ],
        compiler_params=params(False),
        cost_estimate=takes(9),
        name="token_grad",
    )(seq, x, middle, gain, *weights, *grads)


def exchange(array, axis, step):
    size = lax.axis_size(axis)
    return lax.ppermute(array, axis, [(i, i ^ step) for i in range(size)])


def sum_over(vector, axis):
    step = 1
    while step < lax.axis_size(axis):
        vector = vector + exchange(vector, axis, step)
        step *= 2
    return vector


def swap(parts, axis):
    return [parts[0]] + [exchange(parts[k], axis, k) for k in range(1, len(parts))]


def halve(array, axis, dim, step, bit):
    keep = lax.dynamic_index_in_dim(array, bit, dim, keepdims=False)
    send = lax.dynamic_index_in_dim(array, 1 - bit, dim, keepdims=False)
    return (keep.astype(f32) + exchange(send, axis, step).astype(f32)).astype(bf16)


def add_low(left, right):
    return (left.astype(f32) + right.astype(f32)).astype(bf16)


def tie(*arrays):
    return lax.optimization_barrier(arrays)


def key_places(rel_index):
    first = rel_index[0]
    top = jnp.max(first)
    row = top // SPAN - first // SPAN
    column = top % SPAN - first % SPAN
    return (row * GRID + column)[None, :].astype(jnp.int32)


def table_grad(folded):
    heads = folded.shape[0]
    parts = folded.reshape(heads, 2, STRIP // LANES, 2, LANES // 2)
    parts = jnp.transpose(parts, (0, 2, 3, 1, 4)).reshape(heads, 2 * GRID, LANES // 2)
    return parts[:, :SPAN, :SPAN].reshape(heads, SPAN * SPAN)


def per_device(
    tokens,
    timesteps,
    rel_index,
    time_table,
    bias_table,
    gain_one,
    shift_one,
    w_query,
    w_key,
    w_value,
    t_query,
    t_value,
    b_query,
    b_value,
    w_out,
    b_out,
    gain_two,
    shift_two,
    w_up,
    b_up,
    w_down,
    b_down,
    cotangent,
):
    _, local, width = tokens.shape
    hidden = w_up.shape[1]
    heads = bias_table.shape[0]
    head_size = width // heads
    n_dp, n_seq = lax.axis_size("dp"), lax.axis_size("seq")
    dp, seq = lax.axis_index("dp"), lax.axis_index("seq")
    own_heads = heads // n_seq
    group = own_heads * head_size
    half = group // 2
    scale = head_size ** (-0.5)
    table_rows = time_table.shape[0]
    down_rows, out_rows = hidden // n_dp, width // n_dp

    def own_columns(array):
        return lax.dynamic_slice_in_dim(array, seq * group, group, axis=array.ndim - 1)

    x, dy = tokens[0], cotangent[0]
    here = seq.astype(jnp.int32)[None]
    embed = lax.dynamic_slice_in_dim(time_table, timesteps[0], 1, 0)
    *mine, hat_one = project(
        here,
        x,
        embed,
        (gain_one, shift_one, b_query, b_value),
        (w_key, w_query, t_query, w_value, t_value),
        n_seq,
        scale,
    )
    own_0 = swap(mine[0], "seq")
    dy_all = lax.all_gather(dy, "dp", axis=0)
    place = key_places(rel_index)
    table = lax.dynamic_slice_in_dim(bias_table, seq * own_heads, own_heads, 0)
    table = jnp.pad(
        table.reshape(own_heads, SPAN, SPAN), ((0, 0), (0, 72 - SPAN), (0, LANES - SPAN))
    )
    table, hat_one = tie(table, hat_one)
    strips = bias_strips(table)
    own_0, parts_1, place, strips = tie(own_0, mine[1], place, strips)
    own_1 = swap(parts_1, "seq")
    tokens_0, saved_0 = attend(here, own_0, place, strips, 0, head_size)

    own_1, tokens_0, saved_0, place, dy_all = tie(own_1, tokens_0, saved_0, place, dy_all)
    mixed_0 = swap(tokens_0, "seq")
    tokens_1, saved_1 = attend(here, own_1, place, strips, 1, head_size)

    tokens_1, saved_1, mixed_0 = tie(tokens_1, saved_1, mixed_0)
    mixed_1 = swap(tokens_1, "seq")

    mixed_1, hat_one = tie(mixed_1, hat_one)
    hat_all = lax.all_gather(hat_one, "seq", axis=0)
    act, act_t, grad_inner, turned, middle, up_sum = mlp_first(
        here,
        mixed_0 + mixed_1,
        x,
        dy,
        (b_out, gain_two, shift_two),
        b_up[None],
        w_out,
        w_up,
        w_down,
    )

    core = dp % 2
    act_parts = lax.all_to_all(act_t.reshape(n_dp, down_rows, local), "dp", 0, 0)
    turned_other = exchange(turned, "dp", 1)
    inner_other = exchange(grad_inner, "dp", 1)
    grad_mixed, (result, grad_middle, branch, sums_two) = mlp_second(
        here, middle, dy, (b_down, gain_two), act, grad_inner, w_out, w_up, w_down, n_seq
    )

    grad_mixed, result, grad_middle, branch, sums_two, turned_other, inner_other = tie(
        grad_mixed, result, grad_middle, branch, sums_two, turned_other, inner_other
    )
    grad_mixed = swap(grad_mixed, "seq")
    branch_other = exchange(branch, "dp", 1)
    first = (2 * jnp.arange(n_dp // 2) + core) * out_rows
    turned_rows = [turned, turned_other]
    if out_rows % 16:
        first = jnp.zeros((1,), jnp.int32)
        turned_rows = [
            jnp.tile(
                lax.dynamic_index_in_dim(
                    a.reshape(2, n_dp // 2, 2, out_rows, local), core, 2, keepdims=False
                ).reshape(2, width // 2, local),
                (1, 2, 1),
            )
            for a in turned_rows
        ]
    pair = pair_grad(
        first.astype(jnp.int32),
        *turned_rows,
        grad_inner,
        inner_other,
        branch,
        branch_other,
        n_seq,
    )

    pair, act_parts, hat_all, grad_mixed = tie(pair, act_parts, hat_all, grad_mixed)
    if out_rows % 16:
        pair = jnp.swapaxes(pair.reshape(n_seq + 1, n_dp // 2, out_rows, width), 0, 1)
    same_core = [list(range(c, n_dp, 2)) for c in range(2)]
    pair = lax.all_to_all(pair, "dp", 0, 0, axis_index_groups=same_core)
    part_down = down_grad(act_parts, dy_all)

    part_down, grad_mixed = tie(part_down, grad_mixed)
    grad_w_down = lax.psum_scatter(part_down, "seq", scatter_dimension=0, tiled=True)
    grads_0, (table_0, sums_0) = attend_back(here, 0, grad_mixed, *saved_0, place, head_size)

    grads_0, table_0, sums_0, grad_mixed, place = tie(grads_0, table_0, sums_0, grad_mixed, place)
    heads_0 = swap(grads_0, "seq")
    grads_1, (table_1, sums_1) = attend_back(here, 1, grad_mixed, *saved_1, place, head_size)

    grads_1, table_1, sums_1, heads_0, grad_w_down = tie(
        grads_1, table_1, sums_1, heads_0, grad_w_down
    )
    heads_1 = swap(grads_1, "seq")
    product, norms = qkv_grad(
        here,
        list(grads_0) + list(grads_1),
        hat_all,
        gain_one,
        shift_one,
        (w_query, w_key, w_value, t_query, t_value),
    )

    product, norms, pair = tie(product, norms, pair)

    def source_sum(parts):
        return jnp.sum(parts.astype(f32), axis=0).astype(bf16)

    by_near = pair[:, :n_seq].reshape((-1, n_seq // 2, 2) + pair.shape[2:])
    near_keep, near_send = (
        source_sum(lax.dynamic_index_in_dim(by_near, bit, 2, keepdims=False))
        for bit in (seq & 1, 1 - (seq & 1))
    )
    out_part = source_sum(pair[:, n_seq])

    (
        heads_1,
        near_keep,
        near_send,
        out_part,
        norms,
        table_0,
        table_1,
        sums_0,
        sums_1,
        up_sum,
        sums_two,
    ) = tie(
        heads_1,
        near_keep,
        near_send,
        out_part,
        norms,
        table_0,
        table_1,
        sums_0,
        sums_1,
        up_sum,
        sums_two,
    )
    near_received = exchange(near_send, "seq", 1)
    query_sum, value_sum = (
        jnp.concatenate([sums[0, n * half : (n + 1) * half] for sums in (sums_0, sums_1)])
        for n in (0, 2)
    )
    own_image = lax.broadcasted_iota(jnp.int32, (n_dp, 1), 0) == dp

    def slot(row):
        return jnp.where(own_image, row[None, :], 0.0).reshape(-1)

    apart = [table_grad(jnp.concatenate([table_0, table_1])).reshape(-1), query_sum, value_sum]
    summed = [
        slot(norms[2]),
        up_sum[0],
        sums_two[:4].reshape(-1),
        norms[:2].reshape(-1),
    ]
    images = [slot(jnp.concatenate([query_sum, value_sum, timesteps.astype(f32)]))]
    sizes = [sum(a.shape[0] for a in part) for part in (apart, summed, images)]
    vector = sum_over(jnp.concatenate(apart + summed + images), "dp")

    vector, out_part, product, heads_1, near_received = tie(
        vector, out_part, product, heads_1, near_received
    )
    far_keep, far_send = (
        add_low(*(lax.dynamic_index_in_dim(a, bit, 0, keepdims=False) for a in (near_keep, near_received)))
        for bit in (seq >> 1, 1 - (seq >> 1))
    )
    far_received = exchange(far_send, "seq", 2)
    grad_qkv = lax.all_to_all(product.reshape(n_dp, out_rows, 3 * group), "dp", 0, 0)
    grad_tokens = token_grad(
        here, heads_0 + heads_1, x, grad_middle, gain_one, (w_query, w_key, w_value)
    )
    image_sums = vector[sizes[0] + sizes[1] :].reshape(n_dp, 2 * group + 1)
    steps_all = image_sums[:, 2 * group].astype(jnp.int32)
    apart = vector[: sizes[0]].astype(bf16)[None]
    summed = vector[sizes[0] : sizes[0] + sizes[1]]
    apart = jnp.concatenate([apart, exchange(apart, "seq", 1)], axis=0)
    summed = summed + exchange(summed, "seq", 1)

    apart, summed, out_part, grad_tokens, far_received = tie(
        apart, summed, out_part, grad_tokens, far_received
    )
    grad_w_up = far_keep.astype(f32) + far_received.astype(f32)
    far_apart, far_summed = exchange(apart, "seq", 2), exchange(summed, "seq", 2)
    out_part = out_part.reshape(out_rows, 2, n_seq // 2, group)
    out_part = halve(out_part, "seq", 2, 1, seq & 1)
    grad_qkv = qkv_total(grad_qkv)

    far_apart, far_summed, out_part, grad_qkv = tie(far_apart, far_summed, out_part, grad_qkv)
    grad_w_out = halve(out_part, "seq", 1, 2, seq >> 1)
    grad_w_down = jnp.transpose(grad_w_down.astype(f32))
    grad_w_out = grad_w_out.astype(f32)
    apart = jnp.concatenate([apart, far_apart], axis=0)
    apart = jnp.concatenate(
        [lax.dynamic_index_in_dim(apart, n ^ seq, 0) for n in range(n_seq)], axis=0
    ).astype(f32)
    both = summed + far_summed
    table_size = own_heads * SPAN * SPAN
    grad_bias_table = apart[:, :table_size].reshape(heads, SPAN * SPAN)
    grad_b_query = apart[:, table_size : table_size + group].reshape(-1)
    grad_b_value = apart[:, table_size + group :].reshape(-1)
    embed_size = n_dp * width
    embed_rows = both[:embed_size].reshape(n_dp, width)
    grad_b_up = both[embed_size : embed_size + hidden]
    rest = both[embed_size + hidden :].reshape(6, width)
    grad_b_down, grad_gain_two, grad_shift_two, grad_b_out, grad_gain_one, grad_shift_one = (
        rest[r] for r in range(6)
    )

    embeds = lax.dynamic_slice_in_dim(
        jnp.take(time_table, steps_all, axis=0), dp * out_rows, out_rows, axis=1
    ).astype(f32)
    grad_t_query = jnp.dot(embeds.T, image_sums[:, :group], precision=HIGHEST)
    grad_t_value = jnp.dot(embeds.T, image_sums[:, group : 2 * group], precision=HIGHEST)
    onehot = (
        steps_all[:, None] == jnp.arange(table_rows, dtype=jnp.int32)[None, :]
    ).astype(f32)
    grad_time_table = jnp.dot(onehot.T, embed_rows, precision=HIGHEST)

    return (
        result[None],
        grad_tokens[None],
        *grad_qkv,
        grad_t_query,
        grad_t_value,
        grad_w_out,
        grad_w_up,
        grad_w_down,
        grad_gain_one,
        grad_shift_one,
        grad_b_query,
        grad_b_value,
        grad_b_out,
        grad_gain_two,
        grad_shift_two,
        grad_b_up,
        grad_b_down,
        grad_bias_table,
        grad_time_table,
    )


def solution(mesh):
    split, copied, by_block = P("dp", "seq", None), P(), P("dp", "seq")
    in_specs = (split, P("dp"), P("seq", None)) + (copied,) * 19 + (split,)
    out_specs = (split, split) + (by_block,) * 8 + (copied,) * 11
    return jax.shard_map(
        per_device, mesh=mesh, in_specs=in_specs, out_specs=out_specs, check_vma=False
    )
```

```python
from functools import partial

import jax
import jax.numpy as jnp
from jax import lax
from jax.experimental import pallas as pl
from jax.experimental.pallas import tpu as pltpu
from jax.sharding import PartitionSpec as P

GRID = 32
SPAN = 2 * GRID - 1
STRIP = 2 * GRID * GRID
LANES = 128
BLOCK = 256
NORM_EPS = 1e-06
f32, bf16 = jnp.float32, jnp.bfloat16
HIGHEST = lax.Precision.HIGHEST
SCALE = 0.2
VMEM_LIMIT = 58 * 1024 * 1024


def dot(left, right, left_dim=1, right_dim=0):
    return lax.dot_general(
        left, right, (((left_dim,), (right_dim,)), ((), ())), preferred_element_type=f32
    )


def normalize(values):
    centered = values - jnp.mean(values, axis=-1, keepdims=True)
    scaled = lax.rsqrt(jnp.mean(centered * centered, axis=-1, keepdims=True) + NORM_EPS)
    return centered * scaled, scaled


def norm_back(grad_norm, normed, scaled, gain):
    inner = grad_norm * gain
    return scaled * (
        inner
        - jnp.mean(inner, axis=-1, keepdims=True)
        - normed * jnp.mean(inner * normed, axis=-1, keepdims=True)
    )


def row_of(ref):
    return ref[...].reshape(1, ref.shape[0])


def fold_rows(values, op):
    return op(values.reshape(values.shape[0] // 8, 8, values.shape[1]), axis=0)


def strip_place(key_row):
    first = (GRID - 1 - key_row) * GRID
    return (first % LANES) // GRID, first // LANES * LANES


def widen(rows, height):
    fill = jnp.zeros((height - rows.shape[0], rows.shape[1]), rows.dtype)
    return jnp.concatenate([rows, fill], axis=0)


def rows_for(group, half, count):
    return pl.ds(pl.multiple_of((2 * group + half) * count, 16), count)


def block_of(index):
    return pl.ds(pl.multiple_of(index * BLOCK, BLOCK), BLOCK)


def build_permutation(place_ref, perm):
    length = perm.shape[0]

    def rows_of(i, carry):
        first = pl.multiple_of(i * BLOCK, BLOCK)
        spots = lax.broadcasted_iota(jnp.int32, (BLOCK, length), 0) + first
        hit = spots == place_ref[...]
        perm[pl.ds(first, BLOCK), :] = jnp.where(hit, 1.0, 0.0).astype(bf16)
        return carry

    lax.fori_loop(0, length // BLOCK, rows_of, 0)


def strips_kernel(table_ref, strips_ref):
    lane = lax.broadcasted_iota(jnp.int32, (GRID, LANES), 1)
    per_tile = LANES // GRID

    def tile_of(n):
        whole_tile = jnp.zeros((GRID, LANES), f32)
        for k in range(per_tile):
            row = table_ref[0, pl.ds(per_tile * n + k, 1), :]
            turned = pltpu.roll(
                jnp.broadcast_to(row, (GRID, LANES)),
                (GRID * k - GRID + 1) % LANES,
                1,
                stride=1,
                stride_axis=0,
            )
            whole_tile = jnp.where(lane // GRID == k, turned, whole_tile)
        return whole_tile

    tiles = [tile_of(n) for n in range(STRIP // LANES + 1)]
    for n in range(STRIP // LANES):
        span = slice(n * LANES, (n + 1) * LANES)
        strips_ref[0, 0, :, span] = tiles[n]
        for s in range(1, per_tile):
            back = LANES - GRID * s
            strips_ref[0, s, :, span] = jnp.where(
                lane < back, pltpu.roll(tiles[n], back, 1), pltpu.roll(tiles[n + 1], back, 1)
            )


def fold_strips(strips, table_ref):
    lane = lax.broadcasted_iota(jnp.int32, (GRID, LANES), 1)
    row = lax.broadcasted_iota(jnp.int32, (8, LANES), 0)
    per_tile = LANES // GRID

    before = [jnp.zeros((GRID, LANES), f32)] * (per_tile - 1)
    for n in range(STRIP // LANES):
        span = slice(n * LANES, (n + 1) * LANES)
        total = strips[0, 0, :, span]
        turned = []
        for s in range(1, per_tile):
            turned.append(pltpu.roll(strips[0, s, :, span], GRID * s, 1))
            total = total + jnp.where(lane >= GRID * s, turned[-1], before[s - 1])
        before = turned
        for parity in range(2):
            part = jnp.where(lane // GRID % 2 == parity, total, 0.0)
            if parity:
                part = pltpu.roll(part, LANES - GRID, 1)
            part = pltpu.roll(part[:16], 16, 1) + part[16:]
            part = pltpu.roll(part[:8], 8, 1) + part[8:]
            for step in (4, 2, 1):
                part = jnp.where(row % (2 * step) < step, pltpu.roll(part, step, 1), part)
            table_ref[0, parity, n : n + 1, :] = jnp.sum(part, axis=0, keepdims=True)


def project_kernel(
    scale,
    groups,
    seq_ref,
    x_ref,
    embed_ref,
    gain_ref,
    shift_ref,
    b_query_ref,
    b_value_ref,
    wk_hbm,
    wq_hbm,
    tq_hbm,
    wv_hbm,
    tv_hbm,
    *refs,
):
    outs, (hat_ref, held, turned, sems) = refs[: 2 * groups], refs[2 * groups :]
    sources = (wk_hbm, wq_hbm, tq_hbm, wv_hbm, tv_hbm)
    copies = [
        pltpu.make_async_copy(source, held.at[n], sems.at[n]) for n, source in enumerate(sources)
    ]
    for copy in copies:
        copy.start()
    hat, _ = normalize(x_ref[...].astype(f32))
    hat_ref[...] = hat.astype(bf16)
    act = (hat * row_of(gain_ref) + row_of(shift_ref)).astype(bf16)
    embed = jnp.broadcast_to(embed_ref[...].astype(f32), (16, embed_ref.shape[1])).astype(bf16)
    count = outs[0].shape[0] // 3
    seq = seq_ref[0]

    def put(which, value):
        turned[which] = jnp.transpose(value.astype(bf16))
        for k in range(groups):
            for h in range(2):
                outs[h * groups + k][which * count : (which + 1) * count, :] = turned[
                    which, rows_for(k ^ seq, h, count), :
                ]

    copies[0].wait()
    put(1, dot(act, held[0]))
    copies[1].wait()
    copies[2].wait()
    time_query = dot(embed, held[2])[0:1]
    put(0, (dot(act, held[1]) + time_query + row_of(b_query_ref)) * scale)
    copies[3].wait()
    copies[4].wait()
    time_value = dot(embed, held[4])[0:1]
    put(2, dot(act, held[3]) + time_value + row_of(b_value_ref))


def attend_kernel(
    head_size,
    groups,
    seq_ref,
    place_ref,
    strips_ref,
    *refs,
):
    own, outs = refs[:groups], refs[groups : 2 * groups]
    qkv_ref, expo_ref, inverse_ref, mixed_ref = refs[2 * groups : 2 * groups + 4]
    perm, by_place, query_s, key_s, value_s, scores_s = refs[2 * groups + 4 :]
    seq = seq_ref[0]
    head = pl.program_id(0)
    group, length = mixed_ref.shape
    tiles = length // BLOCK

    @pl.when(head == 0)
    def _():
        build_permutation(place_ref, perm)

        def arrange(i, carry):
            span = pl.ds(pl.multiple_of(i * BLOCK, BLOCK), BLOCK)
            part = jnp.zeros((3 * group, BLOCK), f32)
            for k in range(groups):
                part = part + dot(own[k][...], perm[span, block_of(k ^ seq)], 1, 1)
            by_place[:, span] = part
            qkv_ref[:, span] = part.astype(bf16)
            return carry

        lax.fori_loop(0, tiles, arrange, 0)

    def rows_of(which):
        first = pl.multiple_of(which * group + head * head_size, 8)
        return by_place[pl.ds(first, head_size), :]

    query_s[...] = widen(rows_of(0), LANES).astype(bf16)
    key_s[...] = jnp.transpose(widen(rows_of(1), LANES)).astype(bf16)
    value_s[...] = widen(rows_of(2), value_s.shape[0]).astype(bf16)
    own_rows = pl.ds(pl.multiple_of(head * head_size, 8), head_size)

    def tile(t, carry):
        first = pl.multiple_of(t * BLOCK, BLOCK)
        span = pl.ds(first, BLOCK)
        query = query_s[:, span]
        peak = jnp.full((8, BLOCK), -jnp.inf, f32)
        for c in range(tiles):
            keys = slice(c * BLOCK, (c + 1) * BLOCK)
            pieces = []
            for key_row in range(c * BLOCK // GRID, (c + 1) * BLOCK // GRID):
                shift, start = strip_place(key_row)
                pieces.append(strips_ref[0, shift, :, pl.ds(first + start, BLOCK)])
            scores = dot(key_s[keys, :], query) + jnp.concatenate(pieces, axis=0)
            scores_s[keys, :] = scores
            peak = jnp.maximum(peak, fold_rows(scores, jnp.max))
        peak = jnp.max(peak, axis=0, keepdims=True)
        total = jnp.zeros((8, BLOCK), f32)
        mixed = jnp.zeros((value_s.shape[0], BLOCK), f32)
        for c in range(tiles):
            keys = slice(c * BLOCK, (c + 1) * BLOCK)
            expo = jnp.exp(scores_s[keys, :] - peak)
            total = total + fold_rows(expo, jnp.sum)
            low = expo.astype(bf16)
            expo_ref[0, keys, span] = low
            mixed = mixed + dot(value_s[:, keys], low)
        inverse = 1.0 / jnp.sum(total, axis=0, keepdims=True)
        inverse_ref[0, :, span] = inverse
        mixed_ref[own_rows, span] = (mixed * inverse)[:head_size]
        return carry

    lax.fori_loop(0, tiles, tile, 0)

    @pl.when(head == pl.num_programs(0) - 1)
    def _():
        low = mixed_ref[...].astype(bf16)
        for k in range(groups):
            outs[k][...] = dot(low, perm[:, block_of(k ^ seq)]).astype(bf16)


def attend_back_kernel(
    head_size,
    groups,
    seq_ref,
    qkv_ref,
    expo_ref,
    inverse_ref,
    mixed_ref,
    place_ref,
    *refs,
):
    given, outs = refs[:groups], refs[groups : 2 * groups]
    (
        table_ref,
        sums_ref,
        strips_ref,
        perm,
        by_place,
        grad_place,
        grads,
        query_s,
        key_s,
        value_s,
        grad_s,
        grad_t,
        offset_s,
        grad_key,
        grad_value,
    ) = refs[2 * groups :]
    seq = seq_ref[0]
    head = pl.program_id(0)
    group, length = mixed_ref.shape
    tiles = length // BLOCK
    scale = head_size ** (-0.5)

    @pl.when(head == 0)
    def _():
        build_permutation(place_ref, perm)

        def arrange(i, carry):
            span = pl.ds(pl.multiple_of(i * BLOCK, BLOCK), BLOCK)
            part = jnp.zeros((group, BLOCK), f32)
            for k in range(groups):
                part = part + dot(given[k][...], perm[span, block_of(k ^ seq)], 1, 1)
            grad_place[:, span] = part
            by_place[:, span] = qkv_ref[:, span].astype(f32)
            return carry

        lax.fori_loop(0, tiles, arrange, 0)

    own_rows = pl.ds(pl.multiple_of(head * head_size, 8), head_size)

    def rows_of(which):
        first = pl.multiple_of(which * group + head * head_size, 8)
        return by_place[pl.ds(first, head_size), :]

    query_s[...] = jnp.transpose(widen(rows_of(0), LANES)).astype(bf16)
    key_s[...] = widen(rows_of(1), key_s.shape[0]).astype(bf16)
    value_s[...] = jnp.transpose(widen(rows_of(2), LANES)).astype(bf16)
    grad = grad_place[own_rows, :]
    inverse = inverse_ref[0]
    offset_s[...] = inverse * jnp.sum(grad * mixed_ref[own_rows, :], axis=0, keepdims=True)
    grad = widen(grad * inverse, LANES)
    grad_s[...] = grad.astype(bf16)
    grad_t[...] = jnp.transpose(grad).astype(bf16)
    grad_key[...] = jnp.zeros_like(grad_key)
    grad_value[...] = jnp.zeros_like(grad_value)
    strips_ref[...] = jnp.zeros_like(strips_ref)

    def tile(t, carry):
        first = pl.multiple_of(t * BLOCK, BLOCK)
        span = pl.ds(first, BLOCK)
        grad_tile = grad_s[:, span]
        offset = offset_s[:, span]
        grad_query = jnp.zeros((key_s.shape[0], BLOCK), f32)
        for c in range(tiles):
            keys = slice(c * BLOCK, (c + 1) * BLOCK)
            expo = expo_ref[0, keys, span]
            grad_scores = expo.astype(f32) * (dot(value_s[keys, :], grad_tile) - offset)
            for row in range(BLOCK // GRID):
                shift, start = strip_place(c * BLOCK // GRID + row)
                strips_ref[0, shift, :, pl.ds(first + start, BLOCK)] += grad_scores[
                    row * GRID : (row + 1) * GRID
                ]
            low = grad_scores.astype(bf16)
            grad_query = grad_query + dot(key_s[:, keys], low)
            grad_key[keys, :] += dot(low, query_s[span, :])
            grad_value[keys, :] += dot(expo, grad_t[span, :])
        grads[own_rows, span] = grad_query[:head_size] * scale
        return carry

    lax.fori_loop(0, tiles, tile, 0)
    for which, total in ((1, grad_key), (2, grad_value)):
        first = pl.multiple_of(which * group + head * head_size, 8)
        grads[pl.ds(first, head_size), :] = jnp.transpose(total[...])[:head_size]

    @pl.when(head >= 0)
    def _():
        fold_strips(strips_ref, table_ref)

    @pl.when(head == pl.num_programs(0) - 1)
    def _():
        low = grads[...].astype(bf16)
        sums_ref[...] = dot(jnp.ones((8, length), bf16), low, 1, 1)
        for k in range(groups):
            outs[k][...] = dot(low, perm[:, block_of(k ^ seq)]).astype(bf16)


def mlp_first_kernel(
    groups,
    step,
    seq_ref,
    x_ref,
    dy_ref,
    b_out_ref,
    gain_ref,
    shift_ref,
    b_up_ref,
    w_out_hbm,
    w_up_hbm,
    w_down_hbm,
    *refs,
):
    given = refs[: 2 * groups]
    act_hbm, act_t_hbm, inner_hbm, turned_ref, middle_ref, up_sum_ref = refs[
        2 * groups : 2 * groups + 6
    ]
    (
        w_out_s,
        w_up_s,
        w_down_s,
        act_s,
        act_t_s,
        inner_s,
        norm_s,
        sem,
        up_sems,
        down_sems,
        act_sems,
        act_t_sems,
        inner_sems,
    ) = refs[2 * groups + 6 :]
    chunks = w_up_s.shape[0]
    seq = seq_ref[0]

    def span_of(i):
        return pl.ds(pl.multiple_of(i * step, step), step)

    def fetch(i):
        return (
            pltpu.make_async_copy(w_up_hbm.at[:, span_of(i)], w_up_s.at[i], up_sems.at[i]),
            pltpu.make_async_copy(w_down_hbm.at[span_of(i), :], w_down_s.at[i], down_sems.at[i]),
        )

    def put(i):
        return (
            pltpu.make_async_copy(act_s.at[i], act_hbm.at[:, span_of(i)], act_sems.at[i]),
            pltpu.make_async_copy(act_t_s.at[i], act_t_hbm.at[span_of(i), :], act_t_sems.at[i]),
            pltpu.make_async_copy(inner_s.at[i], inner_hbm.at[:, span_of(i)], inner_sems.at[i]),
        )

    def begin(i, carry):
        for copy in fetch(i):
            copy.start()
        return carry

    out_copy = pltpu.make_async_copy(w_out_hbm, w_out_s, sem.at[0])
    out_copy.start()
    lax.fori_loop(0, chunks, begin, 0)
    count = given[0].shape[0]
    for k in range(groups):
        for h in range(2):
            turned_ref[1, rows_for(k ^ seq, h, count), :] = given[h * groups + k][...]
    mixed = jnp.transpose(turned_ref[1])
    out_copy.wait()
    middle = x_ref[...].astype(f32) + dot(mixed, w_out_s[...]) + row_of(b_out_ref)
    hat, _ = normalize(middle)
    middle_ref[...] = middle
    norm = (hat * row_of(gain_ref) + row_of(shift_ref)).astype(bf16)
    norm_s[...] = norm
    turned_ref[0] = jnp.transpose(norm)

    def chunk(i, carry):
        for copy in fetch(i):
            copy.wait()
        inner = dot(norm_s[...], w_up_s[i]) + b_up_ref[:, span_of(i)]
        cdf = 0.5 * (1.0 + lax.erf(inner * (0.5**0.5)))
        pdf = jnp.exp(-0.5 * inner * inner) * 0.3989422804014327
        act = (inner * cdf).astype(bf16)
        low = (dot(dy_ref[...], w_down_s[i], 1, 1) * (cdf + inner * pdf)).astype(bf16)
        act_s[i] = act
        act_t_s[i] = jnp.transpose(act)
        inner_s[i] = low
        up_sum_ref[:, span_of(i)] = jnp.sum(low.astype(f32), axis=0, keepdims=True)
        for copy in put(i):
            copy.start()
        return carry

    lax.fori_loop(0, chunks, chunk, 0)

    def finish(i, carry):
        for copy in put(i):
            copy.wait()
        return carry

    lax.fori_loop(0, chunks, finish, 0)


def mlp_second_kernel(
    groups,
    step,
    seq_ref,
    middle_ref,
    dy_ref,
    b_down_ref,
    gain_ref,
    act_ref,
    inner_ref,
    w_out_hbm,
    w_up_hbm,
    w_down_hbm,
    *refs,
):
    outs = refs[:groups]
    result_ref, grad_middle_ref, branch_ref, sums_ref = refs[groups : groups + 4]
    (
        w_out_s,
        w_up_s,
        w_down_s,
        result_s,
        grad_s,
        mixed_s,
        sem,
        up_sems,
        down_sems,
    ) = refs[groups + 4 :]
    chunks = w_up_s.shape[0]

    def span_of(i):
        return pl.ds(pl.multiple_of(i * step, step), step)

    def fetch(i):
        return (
            pltpu.make_async_copy(w_up_hbm.at[:, span_of(i)], w_up_s.at[i], up_sems.at[i]),
            pltpu.make_async_copy(w_down_hbm.at[span_of(i), :], w_down_s.at[i], down_sems.at[i]),
        )

    def begin(i, carry):
        for copy in fetch(i):
            copy.start()
        return carry

    lax.fori_loop(0, chunks, begin, 0)
    out_copy = pltpu.make_async_copy(w_out_hbm, w_out_s, sem.at[0])
    out_copy.start()
    result_s[...] = middle_ref[...] + row_of(b_down_ref)
    grad_s[...] = jnp.zeros_like(grad_s)

    def chunk(i, carry):
        for copy in fetch(i):
            copy.wait()
        result_s[...] += dot(act_ref[:, span_of(i)], w_down_s[i])
        grad_s[...] += dot(inner_ref[:, span_of(i)], w_up_s[i], 1, 1)
        return carry

    lax.fori_loop(0, chunks, chunk, 0)
    result_ref[...] = result_s[...].astype(bf16)
    hat, scaled = normalize(middle_ref[...])
    dy = dy_ref[...].astype(f32)
    grad_norm = grad_s[...]
    grad_middle = dy + norm_back(grad_norm, hat, scaled, row_of(gain_ref))
    branch = grad_middle.astype(bf16)
    grad_middle_ref[...] = grad_middle
    branch_ref[...] = branch
    out_copy.wait()
    mixed_s[...] = dot(w_out_s[...], branch, 1, 1).astype(bf16)
    count = outs[0].shape[0]
    for k in range(groups):
        rows = pl.ds(pl.multiple_of((k ^ seq_ref[0]) * count, 16), count)
        outs[k][...] = mixed_s[rows, :]
    sums_ref[...] = jnp.concatenate(
        [
            jnp.sum(dy, axis=0, keepdims=True),
            jnp.sum(grad_norm * hat, axis=0, keepdims=True),
            jnp.sum(grad_norm, axis=0, keepdims=True),
            jnp.sum(branch.astype(f32), axis=0, keepdims=True),
            jnp.zeros((4, dy.shape[1]), f32),
        ],
        axis=0,
    )


def pair_grad_kernel(
    order_ref,
    first_ref,
    own_ref,
    other_ref,
    inner_ref,
    inner_other,
    branch_ref,
    branch_other,
    out_ref,
    own_s,
    other_s,
):
    step = pl.program_id(0)
    last = pl.num_programs(0) - 1
    blocks = first_ref.shape[0]
    count = own_s.shape[0] // blocks

    def choose(which):
        for n in range(blocks):
            source = pl.ds(pl.multiple_of(first_ref[n], 16), count)
            own_s[n * count : (n + 1) * count, :] = own_ref[which, source, :]
            other_s[n * count : (n + 1) * count, :] = other_ref[which, source, :]

    def put(right, right_other):
        low = (dot(own_s[...], right[...]) + dot(other_s[...], right_other[...])).astype(bf16)
        for n in range(blocks):
            out_ref[n, 0] = low[n * count : (n + 1) * count]

    @pl.when(step == 0)
    def _():
        choose(0)

    @pl.when(step < last)
    def _():
        put(inner_ref, inner_other)

    @pl.when(step == last)
    def _():
        choose(1)
        put(branch_ref, branch_other)


def down_grad_kernel(act_ref, dy_ref, out_ref):
    total = dot(act_ref[0], dy_ref[0])
    for source in range(1, act_ref.shape[0]):
        total = total + dot(act_ref[source], dy_ref[source])
    out_ref[...] = jnp.transpose(total.astype(bf16))


def qkv_grad_kernel(groups, seq_ref, hat_ref, gain_ref, shift_ref, *refs):
    sources, given = refs[:5], refs[5 : 2 * groups + 5]
    out_ref, norms_ref, held, turned, sems = refs[2 * groups + 5 :]
    seq = seq_ref[0]
    count = given[0].shape[0]
    rows = count // 3
    skipped = lax.rem(2 * rows * seq, LANES)
    window = pl.ds(pl.multiple_of(2 * rows * seq - skipped, LANES), held.shape[2])
    copies = [
        pltpu.make_async_copy(source.at[:, window], held.at[n], sems.at[n])
        for n, source in enumerate(sources)
    ]
    for copy in copies:
        copy.start()
    gain, shift = row_of(gain_ref), row_of(shift_ref)
    grad_gain, grad_shift = jnp.zeros_like(gain), jnp.zeros_like(shift)
    grad_embed = jnp.zeros_like(gain)
    for n, copy in enumerate(copies):
        copy.wait()
        turned[n] = jnp.transpose(held[n])
    for h in range(2):
        span = slice(h * count, (h + 1) * count)
        product = jnp.zeros((count, hat_ref.shape[2]), f32)
        sums = jnp.zeros((count, 1), f32)
        for k in range(groups):
            grads = given[h * groups + k][...]
            product = product + dot(grads, hat_ref[k ^ seq])
            sums = sums + jnp.sum(grads.astype(f32), axis=1, keepdims=True)
        out_ref[:, span] = jnp.transpose((product * gain + sums * shift).astype(bf16))
        for n in range(3):
            own = slice(n * rows, (n + 1) * rows)
            first = pl.multiple_of(skipped + h * rows, 16)
            weight = turned[n, pl.ds(first, rows), :].astype(f32)
            grad_gain = grad_gain + jnp.sum(weight * product[own], axis=0, keepdims=True)
            grad_shift = grad_shift + jnp.sum(weight * sums[own], axis=0, keepdims=True)
        for n, which in ((3, 0), (4, 2)):
            own = slice(which * rows, (which + 1) * rows)
            first = pl.multiple_of(skipped + h * rows, 16)
            weight = turned[n, pl.ds(first, rows), :].astype(f32)
            grad_embed = grad_embed + jnp.sum(weight * sums[own], axis=0, keepdims=True)
    norms_ref[...] = jnp.concatenate(
        [grad_gain, grad_shift, grad_embed, jnp.zeros((5, gain.shape[1]), f32)], axis=0
    )


def qkv_total_kernel(parts_ref, *out_refs):
    total = parts_ref[0].astype(f32)
    for n in range(1, parts_ref.shape[0]):
        total = total + parts_ref[n].astype(f32)
    count = out_refs[0].shape[1] // 2
    for n, out_ref in enumerate(out_refs):
        second = (n + 3) * count
        out_ref[...] = jnp.concatenate(
            [total[:, n * count : (n + 1) * count], total[:, second : second + count]], axis=1
        )


def tokens_kernel(groups, seq_ref, x_ref, middle_ref, gain_ref, wq_hbm, wk_hbm, wv_hbm, *refs):
    given, (out_ref, held, grads_s, sems) = refs[: 2 * groups], refs[2 * groups :]
    copies = [
        pltpu.make_async_copy(source, held.at[n], sems.at[n])
        for n, source in enumerate((wq_hbm, wk_hbm, wv_hbm))
    ]
    for copy in copies:
        copy.start()
    seq = seq_ref[0]
    count = given[0].shape[0] // 3
    for k in range(groups):
        for h in range(2):
            for which in range(3):
                grads_s[which, rows_for(k ^ seq, h, count), :] = given[h * groups + k][
                    which * count : (which + 1) * count
                ]
    hat, scaled = normalize(x_ref[...].astype(f32))
    total = jnp.zeros(middle_ref.shape, f32)
    for which, copy in enumerate(copies):
        grads = jnp.transpose(grads_s[which])
        copy.wait()
        total = total + dot(grads, held[which], 1, 1)
    out_ref[...] = (
        middle_ref[...] + norm_back(total, hat, scaled, row_of(gain_ref))
    ).astype(bf16)


def whole(shape):
    zeros = (0,) * len(shape)
    return pl.BlockSpec(shape, lambda s: zeros, pipeline_mode=pl.Buffered(1))


def kept(shape):
    zeros = (0,) * len(shape)
    return pl.BlockSpec(shape, lambda s: zeros)


def per_head(shape):
    rest = (0,) * (len(shape) - 1)
    return pl.BlockSpec((1,) + tuple(shape[1:]), lambda s: (s,) + rest)


def params(grid=True):
    return pltpu.CompilerParams(
        dimension_semantics=("arbitrary",) if grid else None, vmem_limit_bytes=VMEM_LIMIT
    )


def takes(microseconds):
    return pl.CostEstimate(
        flops=int(microseconds * SCALE * 1e9), bytes_accessed=int(microseconds * SCALE * 3e6), transcendentals=0
    )


IN_VMEM = pl.BlockSpec(memory_space=pltpu.VMEM)
IN_SMEM = pl.BlockSpec(memory_space=pltpu.SMEM)
IN_HBM = pl.BlockSpec(memory_space=pl.ANY)


def shape_of(shape, kind):
    return jax.ShapeDtypeStruct(shape, kind)


def bias_strips(table):
    heads = table.shape[0]
    out = shape_of((heads, LANES // GRID, GRID, STRIP), f32)
    return pl.pallas_call(
        strips_kernel,
        grid=(heads,),
        in_specs=[per_head(table.shape)],
        out_specs=per_head(out.shape),
        out_shape=out,
        compiler_params=params(),
        cost_estimate=takes(9),
        name="strips",
    )(table)


def project(seq, x, embed, vectors, weights, groups, scale):
    count, width = x.shape
    part = shape_of((3 * width // groups // 2, count), bf16)
    outs = pl.pallas_call(
        partial(project_kernel, scale, groups),
        in_specs=[IN_SMEM] + [IN_VMEM] * 6 + [IN_HBM] * 5,
        out_specs=[IN_VMEM] * (2 * groups + 1),
        out_shape=(part,) * (2 * groups) + (shape_of((count, width), bf16),),
        scratch_shapes=[
            pltpu.VMEM((5, width, width), bf16),
            pltpu.VMEM((3, width, count), bf16),
            pltpu.SemaphoreType.DMA((5,)),
        ],
        compiler_params=params(False),
        cost_estimate=takes(9),
        name="project",
    )(seq, x, embed, *vectors, *weights)
    return outs[:groups], outs[groups : 2 * groups], outs[2 * groups]


def attend(seq, own, place, strips, half, head_size):
    heads = strips.shape[0] // 2
    length = place.shape[1]
    group = heads * head_size
    groups = len(own)
    tall = -(-head_size // 16) * 16
    saved = (
        shape_of((3 * group, length), bf16),
        shape_of((heads, length, length), bf16),
        shape_of((heads, 1, length), f32),
        shape_of((group, length), f32),
    )
    own_strips = pl.BlockSpec(
        (1,) + strips.shape[1:], lambda s: (half * heads + s, 0, 0, 0)
    )
    outs = pl.pallas_call(
        partial(attend_kernel, head_size, groups),
        grid=(heads,),
        in_specs=[IN_SMEM, whole(place.shape), own_strips] + [whole(a.shape) for a in own],
        out_specs=[kept((group, BLOCK))] * groups
        + [
            kept(saved[0].shape),
            per_head(saved[1].shape),
            per_head(saved[2].shape),
            kept(saved[3].shape),
        ],
        out_shape=(shape_of((group, BLOCK), bf16),) * groups + saved,
        scratch_shapes=[
            pltpu.VMEM((length, length), bf16),
            pltpu.VMEM((3 * group, length), f32),
            pltpu.VMEM((LANES, length), bf16),
            pltpu.VMEM((length, LANES), bf16),
            pltpu.VMEM((tall, length), bf16),
            pltpu.VMEM((length, BLOCK), f32),
        ],
        compiler_params=params(),
        cost_estimate=takes(13),
        name="attend",
    )(seq, place, strips, *own)
    return outs[:groups], outs[groups:]


def attend_back(seq, half, grad_mixed, qkv, expo, inverse, mixed, place, head_size):
    heads, length, _ = expo.shape
    group = heads * head_size
    groups = len(grad_mixed)
    tall = -(-head_size // 16) * 16
    table = shape_of((heads, 2, STRIP // LANES, LANES), f32)
    given = pl.BlockSpec((group, BLOCK), lambda s: (half, 0), pipeline_mode=pl.Buffered(1))
    outs = pl.pallas_call(
        partial(attend_back_kernel, head_size, groups),
        grid=(heads,),
        in_specs=[
            IN_SMEM,
            whole(qkv.shape),
            per_head(expo.shape),
            per_head(inverse.shape),
            whole(mixed.shape),
            whole(place.shape),
        ]
        + [given] * groups,
        out_specs=[kept((3 * group, BLOCK))] * groups
        + [per_head(table.shape), kept((8, 3 * group))],
        out_shape=(shape_of((3 * group, BLOCK), bf16),) * groups
        + (table, shape_of((8, 3 * group), f32)),
        scratch_shapes=[
            pltpu.VMEM((1, LANES // GRID, GRID, STRIP), f32),
            pltpu.VMEM((length, length), bf16),
            pltpu.VMEM((3 * group, length), f32),
            pltpu.VMEM((group, length), f32),
            pltpu.VMEM((3 * group, length), f32),
            pltpu.VMEM((length, LANES), bf16),
            pltpu.VMEM((tall, length), bf16),
            pltpu.VMEM((length, LANES), bf16),
            pltpu.VMEM((LANES, length), bf16),
            pltpu.VMEM((length, LANES), bf16),
            pltpu.VMEM((1, length), f32),
            pltpu.VMEM((length, LANES), f32),
            pltpu.VMEM((length, LANES), f32),
        ],
        compiler_params=params(),
        cost_estimate=takes(16),
        name="attend_back",
    )(seq, qkv, expo, inverse, mixed, place, *grad_mixed)
    return outs[:groups], outs[groups:]


def mlp_first(seq, mixed, x, dy, vectors, b_up, w_out, w_up, w_down):
    count, width = x.shape
    hidden = w_up.shape[1]
    step = 512
    chunks = hidden // step
    dma = pltpu.SemaphoreType.DMA
    return pl.pallas_call(
        partial(mlp_first_kernel, len(mixed) // 2, step),
        in_specs=[IN_SMEM] + [IN_VMEM] * 6 + [IN_HBM] * 3 + [IN_VMEM] * len(mixed),
        out_specs=[IN_HBM] * 3 + [IN_VMEM] * 3,
        out_shape=(
            shape_of((count, hidden), bf16),
            shape_of((hidden, count), bf16),
            shape_of((count, hidden), bf16),
            shape_of((2, width, count), bf16),
            shape_of((count, width), f32),
            shape_of((1, hidden), f32),
        ),
        scratch_shapes=[
            pltpu.VMEM((width, width), bf16),
            pltpu.VMEM((chunks, width, step), bf16),
            pltpu.VMEM((chunks, step, width), bf16),
            pltpu.VMEM((chunks, count, step), bf16),
            pltpu.VMEM((chunks, step, count), bf16),
            pltpu.VMEM((chunks, count, step), bf16),
            pltpu.VMEM((count, width), bf16),
            dma((1,)),
        ]
        + [dma((chunks,))] * 5,
        compiler_params=params(False),
        cost_estimate=takes(14),
        name="mlp_first",
    )(seq, x, dy, *vectors, b_up, w_out, w_up, w_down, *mixed)


def mlp_second(seq, middle, dy, vectors, act, inner, w_out, w_up, w_down, groups):
    count, width = middle.shape
    hidden = w_up.shape[1]
    step = 512
    chunks = hidden // step
    part = shape_of((width // groups, count), bf16)
    dma = pltpu.SemaphoreType.DMA
    outs = pl.pallas_call(
        partial(mlp_second_kernel, groups, step),
        in_specs=[IN_SMEM] + [IN_VMEM] * 6 + [IN_HBM] * 3,
        out_specs=[IN_VMEM] * (groups + 4),
        out_shape=(part,) * groups
        + (
            shape_of((count, width), bf16),
            shape_of((count, width), f32),
            shape_of((count, width), bf16),
            shape_of((8, width), f32),
        ),
        scratch_shapes=[
            pltpu.VMEM((width, width), bf16),
            pltpu.VMEM((chunks, width, step), bf16),
            pltpu.VMEM((chunks, step, width), bf16),
            pltpu.VMEM((count, width), f32),
            pltpu.VMEM((count, width), f32),
            pltpu.VMEM((width, count), bf16),
            dma((1,)),
            dma((chunks,)),
            dma((chunks,)),
        ],
        compiler_params=params(False),
        cost_estimate=takes(14),
        name="mlp_second",
    )(seq, middle, dy, *vectors, act, inner, w_out, w_up, w_down)
    return outs[:groups], outs[groups:]


def pair_grad(order, first, own, other, inner, inner_other, branch, branch_other):
    _, rows, count = own.shape
    blocks, groups = first.shape[0], order.shape[0]
    width = inner.shape[1] // groups
    wide = pl.BlockSpec(
        (count, width),
        lambda s, order_ref, first_ref: (0, order_ref[jnp.minimum(s, groups - 1)]),
    )
    narrow = pl.BlockSpec((count, width), lambda s, order_ref, first_ref: (0, 0))
    left = pl.BlockSpec((2, rows, count), lambda s, order_ref, first_ref: (0, 0, 0))
    block = (blocks, 1, rows // 2 // blocks, width)
    return pl.pallas_call(
        pair_grad_kernel,
        grid_spec=pltpu.PrefetchScalarGridSpec(
            num_scalar_prefetch=2,
            grid=(groups + 1,),
            in_specs=[left, left, wide, wide, narrow, narrow],
            out_specs=pl.BlockSpec(block, lambda s, order_ref, first_ref: (0, s, 0, 0)),
            scratch_shapes=[pltpu.VMEM((rows // 2, count), bf16)] * 2,
        ),
        out_shape=shape_of((blocks, groups + 1) + block[2:], bf16),
        compiler_params=params(),
        cost_estimate=takes(10),
        name="pair_grad",
    )(order, first, own, other, inner, inner_other, branch, branch_other)


def down_grad(act, dy):
    return pl.pallas_call(
        down_grad_kernel,
        in_specs=[IN_VMEM, IN_VMEM],
        out_specs=IN_VMEM,
        out_shape=shape_of((dy.shape[2], act.shape[1]), bf16),
        compiler_params=params(False),
        cost_estimate=takes(8),
        name="down_grad",
    )(act, dy)


def qkv_grad(seq, grads, hat, gain, shift, weights):
    width = hat.shape[2]
    count = grads[0].shape[0]
    columns = -(-(2 * count // 3 + LANES - GRID) // LANES) * LANES
    return pl.pallas_call(
        partial(qkv_grad_kernel, len(grads) // 2),
        in_specs=[IN_SMEM] + [IN_VMEM] * 3 + [IN_HBM] * 5 + [IN_VMEM] * len(grads),
        out_specs=[IN_VMEM] * 2,
        out_shape=(shape_of((width, 2 * count), bf16), shape_of((8, width), f32)),
        scratch_shapes=[
            pltpu.VMEM((5, width, columns), bf16),
            pltpu.VMEM((5, columns, width), bf16),
            pltpu.SemaphoreType.DMA((5,)),
        ],
        compiler_params=params(False),
        cost_estimate=takes(8),
        name="qkv_grad",
    )(seq, hat, gain, shift, *weights, *grads)


def qkv_total(parts):
    _, rows, columns = parts.shape
    return pl.pallas_call(
        qkv_total_kernel,
        out_shape=(shape_of((rows, columns // 3), f32),) * 3,
        compiler_params=params(False),
        cost_estimate=takes(2),
        name="qkv_total",
    )(parts)


def token_grad(seq, grads, x, middle, gain, weights):
    count, width = x.shape
    return pl.pallas_call(
        partial(tokens_kernel, len(grads) // 2),
        in_specs=[IN_SMEM] + [IN_VMEM] * 3 + [IN_HBM] * 3 + [IN_VMEM] * len(grads),
        out_specs=IN_VMEM,
        out_shape=shape_of((count, width), bf16),
        scratch_shapes=[
            pltpu.VMEM((3, width, width), bf16),
            pltpu.VMEM((3, width, count), bf16),
            pltpu.SemaphoreType.DMA((3,)),
        ],
        compiler_params=params(False),
        cost_estimate=takes(9),
        name="token_grad",
    )(seq, x, middle, gain, *weights, *grads)


def exchange(array, axis, step):
    size = lax.axis_size(axis)
    return lax.ppermute(array, axis, [(i, i ^ step) for i in range(size)])


def sum_over(vector, axis):
    step = 1
    while step < lax.axis_size(axis):
        vector = vector + exchange(vector, axis, step)
        step *= 2
    return vector


def swap(parts, axis):
    return [parts[0]] + [exchange(parts[k], axis, k) for k in range(1, len(parts))]


def halve(array, axis, dim, step, bit):
    keep = lax.dynamic_index_in_dim(array, bit, dim, keepdims=False)
    send = lax.dynamic_index_in_dim(array, 1 - bit, dim, keepdims=False)
    return (keep.astype(f32) + exchange(send, axis, step).astype(f32)).astype(bf16)


def add_low(left, right):
    return (left.astype(f32) + right.astype(f32)).astype(bf16)


def tie(*arrays):
    return lax.optimization_barrier(arrays)


def key_places(rel_index):
    first = rel_index[0]
    top = jnp.max(first)
    row = top // SPAN - first // SPAN
    column = top % SPAN - first % SPAN
    return (row * GRID + column)[None, :].astype(jnp.int32)


def table_grad(folded):
    heads = folded.shape[0]
    parts = folded.reshape(heads, 2, STRIP // LANES, 2, LANES // 2)
    parts = jnp.transpose(parts, (0, 2, 3, 1, 4)).reshape(heads, 2 * GRID, LANES // 2)
    return parts[:, :SPAN, :SPAN].reshape(heads, SPAN * SPAN)


def per_device(
    tokens,
    timesteps,
    rel_index,
    time_table,
    bias_table,
    gain_one,
    shift_one,
    w_query,
    w_key,
    w_value,
    t_query,
    t_value,
    b_query,
    b_value,
    w_out,
    b_out,
    gain_two,
    shift_two,
    w_up,
    b_up,
    w_down,
    b_down,
    cotangent,
):
    _, local, width = tokens.shape
    hidden = w_up.shape[1]
    heads = bias_table.shape[0]
    head_size = width // heads
    n_dp, n_seq = lax.axis_size("dp"), lax.axis_size("seq")
    dp, seq = lax.axis_index("dp"), lax.axis_index("seq")
    own_heads = heads // n_seq
    group = own_heads * head_size
    half = group // 2
    scale = head_size ** (-0.5)
    table_rows = time_table.shape[0]
    down_rows, out_rows = hidden // n_dp, width // n_dp

    def own_columns(array):
        return lax.dynamic_slice_in_dim(array, seq * group, group, axis=array.ndim - 1)

    x, dy = tokens[0], cotangent[0]
    here = seq.astype(jnp.int32)[None]
    embed = lax.dynamic_slice_in_dim(time_table, timesteps[0], 1, 0)
    *mine, hat_one = project(
        here,
        x,
        embed,
        (gain_one, shift_one, b_query, b_value),
        (w_key, w_query, t_query, w_value, t_value),
        n_seq,
        scale,
    )
    own_0 = swap(mine[0], "seq")
    dy_all = lax.all_gather(dy, "dp", axis=0)
    place = key_places(rel_index)
    table = lax.dynamic_slice_in_dim(bias_table, seq * own_heads, own_heads, 0)
    table = jnp.pad(
        table.reshape(own_heads, SPAN, SPAN), ((0, 0), (0, 72 - SPAN), (0, LANES - SPAN))
    )
    table, hat_one = tie(table, hat_one)
    strips = bias_strips(table)
    own_0, parts_1, place, strips = tie(own_0, mine[1], place, strips)
    own_1 = swap(parts_1, "seq")
    tokens_0, saved_0 = attend(here, own_0, place, strips, 0, head_size)

    own_1, tokens_0, saved_0, place, dy_all = tie(own_1, tokens_0, saved_0, place, dy_all)
    mixed_0 = swap(tokens_0, "seq")
    tokens_1, saved_1 = attend(here, own_1, place, strips, 1, head_size)

    tokens_1, saved_1, mixed_0 = tie(tokens_1, saved_1, mixed_0)
    mixed_1 = swap(tokens_1, "seq")

    mixed_1, hat_one = tie(mixed_1, hat_one)
    hat_all = lax.all_gather(hat_one, "seq", axis=0)
    act, act_t, grad_inner, turned, middle, up_sum = mlp_first(
        here,
        mixed_0 + mixed_1,
        x,
        dy,
        (b_out, gain_two, shift_two),
        b_up[None],
        w_out,
        w_up,
        w_down,
    )

    core = dp % 2
    act_parts = lax.all_to_all(act_t.reshape(n_dp, down_rows, local), "dp", 0, 0)
    turned_other = exchange(turned, "dp", 1)
    inner_other = exchange(grad_inner, "dp", 1)
    grad_mixed, (result, grad_middle, branch, sums_two) = mlp_second(
        here, middle, dy, (b_down, gain_two), act, grad_inner, w_out, w_up, w_down, n_seq
    )

    grad_mixed, result, grad_middle, branch, sums_two, turned_other, inner_other = tie(
        grad_mixed, result, grad_middle, branch, sums_two, turned_other, inner_other
    )
    grad_mixed = swap(grad_mixed, "seq")
    branch_other = exchange(branch, "dp", 1)
    first = (2 * jnp.arange(n_dp // 2) + core) * out_rows
    turned_rows = [turned, turned_other]
    if out_rows % 16:
        first = jnp.zeros((1,), jnp.int32)
        turned_rows = [
            jnp.tile(
                lax.dynamic_index_in_dim(
                    a.reshape(2, n_dp // 2, 2, out_rows, local), core, 2, keepdims=False
                ).reshape(2, width // 2, local),
                (1, 2, 1),
            )
            for a in turned_rows
        ]
    pair = pair_grad(
        (jnp.arange(n_seq) ^ seq).astype(jnp.int32),
        first.astype(jnp.int32),
        *turned_rows,
        grad_inner,
        inner_other,
        branch,
        branch_other,
    )

    pair, act_parts = tie(pair, act_parts)
    part_down = down_grad(act_parts, dy_all)

    part_down, grad_mixed, pair, hat_all = tie(part_down, grad_mixed, pair, hat_all)
    grad_w_down = lax.psum_scatter(part_down, "seq", scatter_dimension=0, tiled=True)
    if out_rows % 16:
        pair = jnp.swapaxes(pair.reshape(n_seq + 1, n_dp // 2, out_rows, width), 0, 1)
    same_core = [list(range(c, n_dp, 2)) for c in range(2)]
    pair = lax.all_to_all(pair, "dp", 0, 0, axis_index_groups=same_core)
    grads_0, (table_0, sums_0) = attend_back(here, 0, grad_mixed, *saved_0, place, head_size)

    grads_0, table_0, sums_0, grad_mixed, place = tie(grads_0, table_0, sums_0, grad_mixed, place)
    heads_0 = swap(grads_0, "seq")
    grads_1, (table_1, sums_1) = attend_back(here, 1, grad_mixed, *saved_1, place, head_size)

    grads_1, table_1, sums_1, heads_0, grad_w_down = tie(
        grads_1, table_1, sums_1, heads_0, grad_w_down
    )
    heads_1 = swap(grads_1, "seq")
    product, norms = qkv_grad(
        here,
        list(grads_0) + list(grads_1),
        hat_all,
        gain_one,
        shift_one,
        (w_query, w_key, w_value, t_query, t_value),
    )

    product, norms, pair = tie(product, norms, pair)

    def source_sum(parts):
        return jnp.sum(parts.astype(f32), axis=0).astype(bf16)

    near_keep, near_send = (source_sum(pair[:, n:n_seq:2]) for n in range(2))
    out_part = source_sum(pair[:, n_seq])

    (
        heads_1,
        near_keep,
        near_send,
        out_part,
        norms,
        table_0,
        table_1,
        sums_0,
        sums_1,
        up_sum,
        sums_two,
    ) = tie(
        heads_1,
        near_keep,
        near_send,
        out_part,
        norms,
        table_0,
        table_1,
        sums_0,
        sums_1,
        up_sum,
        sums_two,
    )
    near_received = exchange(near_send, "seq", 1)
    grad_tokens = token_grad(
        here, heads_0 + heads_1, x, grad_middle, gain_one, (w_query, w_key, w_value)
    )
    query_sum, value_sum = (
        jnp.concatenate([sums[0, n * half : (n + 1) * half] for sums in (sums_0, sums_1)])
        for n in (0, 2)
    )
    own_image = lax.broadcasted_iota(jnp.int32, (n_dp, 1), 0) == dp

    def slot(row):
        return jnp.where(own_image, row[None, :], 0.0).reshape(-1)

    apart = [table_grad(jnp.concatenate([table_0, table_1])).reshape(-1), query_sum, value_sum]
    summed = [
        slot(norms[2]),
        up_sum[0],
        sums_two[:4].reshape(-1),
        norms[:2].reshape(-1),
    ]
    images = [slot(jnp.concatenate([query_sum, value_sum, timesteps.astype(f32)]))]
    sizes = [sum(a.shape[0] for a in part) for part in (apart, summed, images)]
    vector = sum_over(jnp.concatenate(apart + summed + images), "dp")

    vector, out_part, product, grad_tokens, near_received = tie(
        vector, out_part, product, grad_tokens, near_received
    )
    far_keep, far_send = (
        add_low(near_keep[n], near_received[n]) for n in range(2)
    )
    far_received = exchange(far_send, "seq", 2)
    grad_qkv = lax.all_to_all(product.reshape(n_dp, out_rows, 3 * group), "dp", 0, 0)
    image_sums = vector[sizes[0] + sizes[1] :].reshape(n_dp, 2 * group + 1)
    steps_all = image_sums[:, 2 * group].astype(jnp.int32)
    apart = vector[: sizes[0]].astype(bf16)[None]
    summed = vector[sizes[0] : sizes[0] + sizes[1]]
    apart = jnp.concatenate([apart, exchange(apart, "seq", 1)], axis=0)
    summed = summed + exchange(summed, "seq", 1)

    apart, summed, out_part = tie(apart, summed, out_part)
    far_apart, far_summed = exchange(apart, "seq", 2), exchange(summed, "seq", 2)
    out_part = out_part.reshape(out_rows, 2, n_seq // 2, group)
    out_part = halve(out_part, "seq", 2, 1, seq & 1)

    far_apart, far_summed, out_part, far_received = tie(
        far_apart, far_summed, out_part, far_received
    )
    grad_qkv = qkv_total(grad_qkv)
    grad_w_up = far_keep.astype(f32) + far_received.astype(f32)
    grad_w_out = halve(out_part, "seq", 1, 2, seq >> 1)
    grad_w_down = jnp.transpose(grad_w_down.astype(f32))
    grad_w_out = grad_w_out.astype(f32)
    apart = jnp.concatenate([apart, far_apart], axis=0)
    apart = jnp.concatenate(
        [lax.dynamic_index_in_dim(apart, n ^ seq, 0) for n in range(n_seq)], axis=0
    ).astype(f32)
    both = summed + far_summed
    table_size = own_heads * SPAN * SPAN
    grad_bias_table = apart[:, :table_size].reshape(heads, SPAN * SPAN)
    grad_b_query = apart[:, table_size : table_size + group].reshape(-1)
    grad_b_value = apart[:, table_size + group :].reshape(-1)
    embed_size = n_dp * width
    embed_rows = both[:embed_size].reshape(n_dp, width)
    grad_b_up = both[embed_size : embed_size + hidden]
    rest = both[embed_size + hidden :].reshape(6, width)
    grad_b_down, grad_gain_two, grad_shift_two, grad_b_out, grad_gain_one, grad_shift_one = (
        rest[r] for r in range(6)
    )

    embeds = lax.dynamic_slice_in_dim(
        jnp.take(time_table, steps_all, axis=0), dp * out_rows, out_rows, axis=1
    ).astype(f32)
    grad_t_query = jnp.dot(embeds.T, image_sums[:, :group], precision=HIGHEST)
    grad_t_value = jnp.dot(embeds.T, image_sums[:, group : 2 * group], precision=HIGHEST)
    onehot = (
        steps_all[:, None] == jnp.arange(table_rows, dtype=jnp.int32)[None, :]
    ).astype(f32)
    grad_time_table = jnp.dot(onehot.T, embed_rows, precision=HIGHEST)

    return (
        result[None],
        grad_tokens[None],
        *grad_qkv,
        grad_t_query,
        grad_t_value,
        grad_w_out,
        grad_w_up,
        grad_w_down,
        grad_gain_one,
        grad_shift_one,
        grad_b_query,
        grad_b_value,
        grad_b_out,
        grad_gain_two,
        grad_shift_two,
        grad_b_up,
        grad_b_down,
        grad_bias_table,
        grad_time_table,
    )


def solution(mesh):
    split, copied, by_block = P("dp", "seq", None), P(), P("dp", "seq")
    in_specs = (split, P("dp"), P("seq", None)) + (copied,) * 19 + (split,)
    out_specs = (split, split) + (by_block,) * 8 + (copied,) * 11
    return jax.shard_map(
        per_device, mesh=mesh, in_specs=in_specs, out_specs=out_specs, check_vma=False
    )
```

```python
from functools import partial

import jax
import jax.numpy as jnp
from jax import lax
from jax.experimental import pallas as pl
from jax.experimental.pallas import tpu as pltpu
from jax.sharding import PartitionSpec as P

GRID = 32
SPAN = 2 * GRID - 1
STRIP = 2 * GRID * GRID
LANES = 128
BLOCK = 256
NORM_EPS = 1e-06
f32, bf16 = jnp.float32, jnp.bfloat16
HIGHEST = lax.Precision.HIGHEST
SCALE = 0.2
VMEM_LIMIT = 58 * 1024 * 1024


def dot(left, right, left_dim=1, right_dim=0):
    return lax.dot_general(
        left, right, (((left_dim,), (right_dim,)), ((), ())), preferred_element_type=f32
    )


def normalize(values):
    centered = values - jnp.mean(values, axis=-1, keepdims=True)
    scaled = lax.rsqrt(jnp.mean(centered * centered, axis=-1, keepdims=True) + NORM_EPS)
    return centered * scaled, scaled


def norm_back(grad_norm, normed, scaled, gain):
    inner = grad_norm * gain
    return scaled * (
        inner
        - jnp.mean(inner, axis=-1, keepdims=True)
        - normed * jnp.mean(inner * normed, axis=-1, keepdims=True)
    )


def row_of(ref):
    return ref[...].reshape(1, ref.shape[0])


def fold_rows(values, op):
    return op(values.reshape(values.shape[0] // 8, 8, values.shape[1]), axis=0)


def strip_place(key_row):
    first = (GRID - 1 - key_row) * GRID
    return (first % LANES) // GRID, first // LANES * LANES


def widen(rows, height):
    fill = jnp.zeros((height - rows.shape[0], rows.shape[1]), rows.dtype)
    return jnp.concatenate([rows, fill], axis=0)


def rows_for(group, half, count):
    return pl.ds(pl.multiple_of((2 * group + half) * count, 16), count)


def block_of(index):
    return pl.ds(pl.multiple_of(index * BLOCK, BLOCK), BLOCK)


def build_permutation(place_ref, perm):
    length = perm.shape[0]

    def rows_of(i, carry):
        first = pl.multiple_of(i * BLOCK, BLOCK)
        spots = lax.broadcasted_iota(jnp.int32, (BLOCK, length), 0) + first
        hit = spots == place_ref[...]
        perm[pl.ds(first, BLOCK), :] = jnp.where(hit, 1.0, 0.0).astype(bf16)
        return carry

    lax.fori_loop(0, length // BLOCK, rows_of, 0)


def strips_kernel(table_ref, strips_ref):
    lane = lax.broadcasted_iota(jnp.int32, (GRID, LANES), 1)
    per_tile = LANES // GRID

    def tile_of(n):
        whole_tile = jnp.zeros((GRID, LANES), f32)
        for k in range(per_tile):
            row = table_ref[0, pl.ds(per_tile * n + k, 1), :]
            turned = pltpu.roll(
                jnp.broadcast_to(row, (GRID, LANES)),
                (GRID * k - GRID + 1) % LANES,
                1,
                stride=1,
                stride_axis=0,
            )
            whole_tile = jnp.where(lane // GRID == k, turned, whole_tile)
        return whole_tile

    tiles = [tile_of(n) for n in range(STRIP // LANES + 1)]
    for n in range(STRIP // LANES):
        span = slice(n * LANES, (n + 1) * LANES)
        strips_ref[0, 0, :, span] = tiles[n]
        for s in range(1, per_tile):
            back = LANES - GRID * s
            strips_ref[0, s, :, span] = jnp.where(
                lane < back, pltpu.roll(tiles[n], back, 1), pltpu.roll(tiles[n + 1], back, 1)
            )


def fold_strips(strips, table_ref):
    lane = lax.broadcasted_iota(jnp.int32, (GRID, LANES), 1)
    row = lax.broadcasted_iota(jnp.int32, (8, LANES), 0)
    per_tile = LANES // GRID

    before = [jnp.zeros((GRID, LANES), f32)] * (per_tile - 1)
    for n in range(STRIP // LANES):
        span = slice(n * LANES, (n + 1) * LANES)
        total = strips[0, 0, :, span]
        turned = []
        for s in range(1, per_tile):
            turned.append(pltpu.roll(strips[0, s, :, span], GRID * s, 1))
            total = total + jnp.where(lane >= GRID * s, turned[-1], before[s - 1])
        before = turned
        for parity in range(2):
            part = jnp.where(lane // GRID % 2 == parity, total, 0.0)
            if parity:
                part = pltpu.roll(part, LANES - GRID, 1)
            part = pltpu.roll(part[:16], 16, 1) + part[16:]
            part = pltpu.roll(part[:8], 8, 1) + part[8:]
            for step in (4, 2, 1):
                part = jnp.where(row % (2 * step) < step, pltpu.roll(part, step, 1), part)
            table_ref[0, parity, n : n + 1, :] = jnp.sum(part, axis=0, keepdims=True)


def project_kernel(
    scale,
    groups,
    seq_ref,
    x_ref,
    embed_ref,
    gain_ref,
    shift_ref,
    b_query_ref,
    b_value_ref,
    wk_hbm,
    wq_hbm,
    tq_hbm,
    wv_hbm,
    tv_hbm,
    *refs,
):
    outs, (hat_ref, held, turned, sems) = refs[: 2 * groups], refs[2 * groups :]
    sources = (wk_hbm, wq_hbm, tq_hbm, wv_hbm, tv_hbm)
    copies = [
        pltpu.make_async_copy(source, held.at[n], sems.at[n]) for n, source in enumerate(sources)
    ]
    for copy in copies:
        copy.start()
    hat, _ = normalize(x_ref[...].astype(f32))
    hat_ref[...] = hat.astype(bf16)
    act = (hat * row_of(gain_ref) + row_of(shift_ref)).astype(bf16)
    embed = jnp.broadcast_to(embed_ref[...].astype(f32), (16, embed_ref.shape[1])).astype(bf16)
    count = outs[0].shape[0] // 3
    seq = seq_ref[0]

    def put(which, value):
        turned[which] = jnp.transpose(value.astype(bf16))
        for k in range(groups):
            for h in range(2):
                outs[h * groups + k][which * count : (which + 1) * count, :] = turned[
                    which, rows_for(k ^ seq, h, count), :
                ]

    copies[0].wait()
    put(1, dot(act, held[0]))
    copies[1].wait()
    copies[2].wait()
    time_query = dot(embed, held[2])[0:1]
    put(0, (dot(act, held[1]) + time_query + row_of(b_query_ref)) * scale)
    copies[3].wait()
    copies[4].wait()
    time_value = dot(embed, held[4])[0:1]
    put(2, dot(act, held[3]) + time_value + row_of(b_value_ref))


def attend_kernel(
    head_size,
    groups,
    seq_ref,
    place_ref,
    strips_ref,
    *refs,
):
    own, outs = refs[:groups], refs[groups : 2 * groups]
    qkv_ref, expo_ref, inverse_ref, mixed_ref = refs[2 * groups : 2 * groups + 4]
    perm, by_place, query_s, key_s, value_s, scores_s = refs[2 * groups + 4 :]
    seq = seq_ref[0]
    head = pl.program_id(0)
    group, length = mixed_ref.shape
    tiles = length // BLOCK

    @pl.when(head == 0)
    def _():
        build_permutation(place_ref, perm)

        def arrange(i, carry):
            span = pl.ds(pl.multiple_of(i * BLOCK, BLOCK), BLOCK)
            part = jnp.zeros((3 * group, BLOCK), f32)
            for k in range(groups):
                part = part + dot(own[k][...], perm[span, block_of(k ^ seq)], 1, 1)
            by_place[:, span] = part
            qkv_ref[:, span] = part.astype(bf16)
            return carry

        lax.fori_loop(0, tiles, arrange, 0)

    def rows_of(which):
        first = pl.multiple_of(which * group + head * head_size, 8)
        return by_place[pl.ds(first, head_size), :]

    query_s[...] = widen(rows_of(0), LANES).astype(bf16)
    key_s[...] = jnp.transpose(widen(rows_of(1), LANES)).astype(bf16)
    value_s[...] = widen(rows_of(2), value_s.shape[0]).astype(bf16)
    own_rows = pl.ds(pl.multiple_of(head * head_size, 8), head_size)

    def tile(t, carry):
        first = pl.multiple_of(t * BLOCK, BLOCK)
        span = pl.ds(first, BLOCK)
        query = query_s[:, span]
        peak = jnp.full((8, BLOCK), -jnp.inf, f32)
        for c in range(tiles):
            keys = slice(c * BLOCK, (c + 1) * BLOCK)
            pieces = []
            for key_row in range(c * BLOCK // GRID, (c + 1) * BLOCK // GRID):
                shift, start = strip_place(key_row)
                pieces.append(strips_ref[0, shift, :, pl.ds(first + start, BLOCK)])
            scores = dot(key_s[keys, :], query) + jnp.concatenate(pieces, axis=0)
            scores_s[keys, :] = scores
            peak = jnp.maximum(peak, fold_rows(scores, jnp.max))
        peak = jnp.max(peak, axis=0, keepdims=True)
        total = jnp.zeros((8, BLOCK), f32)
        mixed = jnp.zeros((value_s.shape[0], BLOCK), f32)
        for c in range(tiles):
            keys = slice(c * BLOCK, (c + 1) * BLOCK)
            expo = jnp.exp(scores_s[keys, :] - peak)
            total = total + fold_rows(expo, jnp.sum)
            low = expo.astype(bf16)
            expo_ref[0, keys, span] = low
            mixed = mixed + dot(value_s[:, keys], low)
        inverse = 1.0 / jnp.sum(total, axis=0, keepdims=True)
        inverse_ref[0, :, span] = inverse
        mixed_ref[own_rows, span] = (mixed * inverse)[:head_size]
        return carry

    lax.fori_loop(0, tiles, tile, 0)

    @pl.when(head == pl.num_programs(0) - 1)
    def _():
        low = mixed_ref[...].astype(bf16)
        for k in range(groups):
            outs[k][...] = dot(low, perm[:, block_of(k ^ seq)]).astype(bf16)


def attend_back_kernel(
    head_size,
    groups,
    seq_ref,
    qkv_ref,
    expo_ref,
    inverse_ref,
    mixed_ref,
    place_ref,
    *refs,
):
    given, outs = refs[:groups], refs[groups : 2 * groups]
    (
        table_ref,
        sums_ref,
        strips_ref,
        perm,
        by_place,
        grad_place,
        grads,
        query_s,
        key_s,
        value_s,
        grad_s,
        grad_t,
        offset_s,
        grad_key,
        grad_value,
    ) = refs[2 * groups :]
    seq = seq_ref[0]
    head = pl.program_id(0)
    group, length = mixed_ref.shape
    tiles = length // BLOCK
    scale = head_size ** (-0.5)

    @pl.when(head == 0)
    def _():
        build_permutation(place_ref, perm)

        def arrange(i, carry):
            span = pl.ds(pl.multiple_of(i * BLOCK, BLOCK), BLOCK)
            part = jnp.zeros((group, BLOCK), f32)
            for k in range(groups):
                part = part + dot(given[k][...], perm[span, block_of(k ^ seq)], 1, 1)
            grad_place[:, span] = part
            by_place[:, span] = qkv_ref[:, span].astype(f32)
            return carry

        lax.fori_loop(0, tiles, arrange, 0)

    own_rows = pl.ds(pl.multiple_of(head * head_size, 8), head_size)

    def rows_of(which):
        first = pl.multiple_of(which * group + head * head_size, 8)
        return by_place[pl.ds(first, head_size), :]

    query_s[...] = jnp.transpose(widen(rows_of(0), LANES)).astype(bf16)
    key_s[...] = widen(rows_of(1), key_s.shape[0]).astype(bf16)
    value_s[...] = jnp.transpose(widen(rows_of(2), LANES)).astype(bf16)
    grad = grad_place[own_rows, :]
    inverse = inverse_ref[0]
    offset_s[...] = inverse * jnp.sum(grad * mixed_ref[own_rows, :], axis=0, keepdims=True)
    grad = widen(grad * inverse, LANES)
    grad_s[...] = grad.astype(bf16)
    grad_t[...] = jnp.transpose(grad).astype(bf16)
    grad_key[...] = jnp.zeros_like(grad_key)
    grad_value[...] = jnp.zeros_like(grad_value)
    strips_ref[...] = jnp.zeros_like(strips_ref)

    def tile(t, carry):
        first = pl.multiple_of(t * BLOCK, BLOCK)
        span = pl.ds(first, BLOCK)
        grad_tile = grad_s[:, span]
        offset = offset_s[:, span]
        grad_query = jnp.zeros((key_s.shape[0], BLOCK), f32)
        for c in range(tiles):
            keys = slice(c * BLOCK, (c + 1) * BLOCK)
            expo = expo_ref[0, keys, span]
            grad_scores = expo.astype(f32) * (dot(value_s[keys, :], grad_tile) - offset)
            for row in range(BLOCK // GRID):
                shift, start = strip_place(c * BLOCK // GRID + row)
                strips_ref[0, shift, :, pl.ds(first + start, BLOCK)] += grad_scores[
                    row * GRID : (row + 1) * GRID
                ]
            low = grad_scores.astype(bf16)
            grad_query = grad_query + dot(key_s[:, keys], low)
            grad_key[keys, :] += dot(low, query_s[span, :])
            grad_value[keys, :] += dot(expo, grad_t[span, :])
        grads[own_rows, span] = grad_query[:head_size] * scale
        return carry

    lax.fori_loop(0, tiles, tile, 0)
    for which, total in ((1, grad_key), (2, grad_value)):
        first = pl.multiple_of(which * group + head * head_size, 8)
        grads[pl.ds(first, head_size), :] = jnp.transpose(total[...])[:head_size]

    @pl.when(head >= 0)
    def _():
        fold_strips(strips_ref, table_ref)

    @pl.when(head == pl.num_programs(0) - 1)
    def _():
        low = grads[...].astype(bf16)
        sums_ref[...] = dot(jnp.ones((8, length), bf16), low, 1, 1)
        for k in range(groups):
            outs[k][...] = dot(low, perm[:, block_of(k ^ seq)]).astype(bf16)


def mlp_first_kernel(
    groups,
    step,
    seq_ref,
    x_ref,
    dy_ref,
    b_out_ref,
    gain_ref,
    shift_ref,
    b_up_ref,
    w_out_hbm,
    w_up_hbm,
    w_down_hbm,
    *refs,
):
    given = refs[: 2 * groups]
    act_hbm, act_t_hbm, inner_hbm, turned_ref, middle_ref, up_sum_ref = refs[
        2 * groups : 2 * groups + 6
    ]
    (
        w_out_s,
        w_up_s,
        w_down_s,
        act_s,
        act_t_s,
        inner_s,
        norm_s,
        sem,
        up_sems,
        down_sems,
        act_sems,
        act_t_sems,
        inner_sems,
    ) = refs[2 * groups + 6 :]
    chunks = w_up_s.shape[0]
    seq = seq_ref[0]

    def span_of(i):
        return pl.ds(pl.multiple_of(i * step, step), step)

    def fetch(i):
        return (
            pltpu.make_async_copy(w_up_hbm.at[:, span_of(i)], w_up_s.at[i], up_sems.at[i]),
            pltpu.make_async_copy(w_down_hbm.at[span_of(i), :], w_down_s.at[i], down_sems.at[i]),
        )

    def put(i):
        return (
            pltpu.make_async_copy(act_s.at[i], act_hbm.at[:, span_of(i)], act_sems.at[i]),
            pltpu.make_async_copy(act_t_s.at[i], act_t_hbm.at[span_of(i), :], act_t_sems.at[i]),
            pltpu.make_async_copy(inner_s.at[i], inner_hbm.at[:, span_of(i)], inner_sems.at[i]),
        )

    def begin(i, carry):
        for copy in fetch(i):
            copy.start()
        return carry

    out_copy = pltpu.make_async_copy(w_out_hbm, w_out_s, sem.at[0])
    out_copy.start()
    lax.fori_loop(0, chunks, begin, 0)
    count = given[0].shape[0]
    for k in range(groups):
        for h in range(2):
            turned_ref[1, rows_for(k ^ seq, h, count), :] = given[h * groups + k][...]
    mixed = jnp.transpose(turned_ref[1])
    out_copy.wait()
    middle = x_ref[...].astype(f32) + dot(mixed, w_out_s[...]) + row_of(b_out_ref)
    hat, _ = normalize(middle)
    middle_ref[...] = middle
    norm = (hat * row_of(gain_ref) + row_of(shift_ref)).astype(bf16)
    norm_s[...] = norm
    turned_ref[0] = jnp.transpose(norm)

    def chunk(i, carry):
        for copy in fetch(i):
            copy.wait()
        inner = dot(norm_s[...], w_up_s[i]) + b_up_ref[:, span_of(i)]
        cdf = 0.5 * (1.0 + lax.erf(inner * (0.5**0.5)))
        pdf = jnp.exp(-0.5 * inner * inner) * 0.3989422804014327
        act = (inner * cdf).astype(bf16)
        low = (dot(dy_ref[...], w_down_s[i], 1, 1) * (cdf + inner * pdf)).astype(bf16)
        act_s[i] = act
        act_t_s[i] = jnp.transpose(act)
        inner_s[i] = low
        up_sum_ref[:, span_of(i)] = jnp.sum(low.astype(f32), axis=0, keepdims=True)
        for copy in put(i):
            copy.start()
        return carry

    lax.fori_loop(0, chunks, chunk, 0)

    def finish(i, carry):
        for copy in put(i):
            copy.wait()
        return carry

    lax.fori_loop(0, chunks, finish, 0)


def mlp_second_kernel(
    groups,
    step,
    seq_ref,
    middle_ref,
    dy_ref,
    b_down_ref,
    gain_ref,
    act_hbm,
    inner_hbm,
    w_out_hbm,
    w_up_hbm,
    w_down_hbm,
    *refs,
):
    outs = refs[:groups]
    result_ref, grad_middle_ref, branch_ref, sums_ref = refs[groups : groups + 4]
    (
        w_out_s,
        w_up_s,
        w_down_s,
        act_s,
        inner_s,
        result_s,
        grad_s,
        mixed_s,
        sem,
        up_sems,
        down_sems,
        act_sems,
        inner_sems,
    ) = refs[groups + 4 :]
    chunks = w_up_s.shape[0]

    def span_of(i):
        return pl.ds(pl.multiple_of(i * step, step), step)

    def fetch(i):
        return (
            pltpu.make_async_copy(w_up_hbm.at[:, span_of(i)], w_up_s.at[i], up_sems.at[i]),
            pltpu.make_async_copy(w_down_hbm.at[span_of(i), :], w_down_s.at[i], down_sems.at[i]),
            pltpu.make_async_copy(act_hbm.at[:, span_of(i)], act_s.at[i], act_sems.at[i]),
            pltpu.make_async_copy(inner_hbm.at[:, span_of(i)], inner_s.at[i], inner_sems.at[i]),
        )

    def begin(i, carry):
        for copy in fetch(i):
            copy.start()
        return carry

    lax.fori_loop(0, chunks, begin, 0)
    out_copy = pltpu.make_async_copy(w_out_hbm, w_out_s, sem.at[0])
    out_copy.start()
    result_s[...] = middle_ref[...] + row_of(b_down_ref)
    grad_s[...] = jnp.zeros_like(grad_s)

    def chunk(i, carry):
        for copy in fetch(i):
            copy.wait()
        result_s[...] += dot(act_s[i], w_down_s[i])
        grad_s[...] += dot(inner_s[i], w_up_s[i], 1, 1)
        return carry

    lax.fori_loop(0, chunks, chunk, 0)
    result_ref[...] = result_s[...].astype(bf16)
    hat, scaled = normalize(middle_ref[...])
    dy = dy_ref[...].astype(f32)
    grad_norm = grad_s[...]
    grad_middle = dy + norm_back(grad_norm, hat, scaled, row_of(gain_ref))
    branch = grad_middle.astype(bf16)
    grad_middle_ref[...] = grad_middle
    branch_ref[...] = branch
    out_copy.wait()
    mixed_s[...] = dot(w_out_s[...], branch, 1, 1).astype(bf16)
    count = outs[0].shape[0]
    for k in range(groups):
        rows = pl.ds(pl.multiple_of((k ^ seq_ref[0]) * count, 16), count)
        outs[k][...] = mixed_s[rows, :]
    sums_ref[...] = jnp.concatenate(
        [
            jnp.sum(dy, axis=0, keepdims=True),
            jnp.sum(grad_norm * hat, axis=0, keepdims=True),
            jnp.sum(grad_norm, axis=0, keepdims=True),
            jnp.sum(branch.astype(f32), axis=0, keepdims=True),
            jnp.zeros((4, dy.shape[1]), f32),
        ],
        axis=0,
    )


def pair_grad_kernel(
    order_ref,
    first_ref,
    own_ref,
    other_ref,
    inner_ref,
    inner_other,
    branch_ref,
    branch_other,
    out_ref,
    own_s,
    other_s,
):
    step = pl.program_id(0)
    last = pl.num_programs(0) - 1
    blocks = first_ref.shape[0]
    count = own_s.shape[0] // blocks

    def choose(which):
        for n in range(blocks):
            source = pl.ds(pl.multiple_of(first_ref[n], 16), count)
            own_s[n * count : (n + 1) * count, :] = own_ref[which, source, :]
            other_s[n * count : (n + 1) * count, :] = other_ref[which, source, :]

    def put(right, right_other):
        low = (dot(own_s[...], right[...]) + dot(other_s[...], right_other[...])).astype(bf16)
        for n in range(blocks):
            out_ref[n, 0] = low[n * count : (n + 1) * count]

    @pl.when(step == 0)
    def _():
        choose(0)

    @pl.when(step < last)
    def _():
        put(inner_ref, inner_other)

    @pl.when(step == last)
    def _():
        choose(1)
        put(branch_ref, branch_other)


def down_grad_kernel(act_ref, dy_ref, out_ref):
    total = dot(act_ref[0], dy_ref[0])
    for source in range(1, act_ref.shape[0]):
        total = total + dot(act_ref[source], dy_ref[source])
    out_ref[...] = jnp.transpose(total.astype(bf16))


def qkv_grad_kernel(groups, seq_ref, hat_ref, gain_ref, shift_ref, *refs):
    sources, given = refs[:5], refs[5 : 2 * groups + 5]
    out_ref, norms_ref, held, turned, sems = refs[2 * groups + 5 :]
    seq = seq_ref[0]
    count = given[0].shape[0]
    rows = count // 3
    skipped = lax.rem(2 * rows * seq, LANES)
    window = pl.ds(pl.multiple_of(2 * rows * seq - skipped, LANES), held.shape[2])
    copies = [
        pltpu.make_async_copy(source.at[:, window], held.at[n], sems.at[n])
        for n, source in enumerate(sources)
    ]
    for copy in copies:
        copy.start()
    gain, shift = row_of(gain_ref), row_of(shift_ref)
    grad_gain, grad_shift = jnp.zeros_like(gain), jnp.zeros_like(shift)
    grad_embed = jnp.zeros_like(gain)
    for n, copy in enumerate(copies):
        copy.wait()
        turned[n] = jnp.transpose(held[n])
    for h in range(2):
        span = slice(h * count, (h + 1) * count)
        product = jnp.zeros((count, hat_ref.shape[2]), f32)
        sums = jnp.zeros((count, 1), f32)
        for k in range(groups):
            grads = given[h * groups + k][...]
            product = product + dot(grads, hat_ref[k ^ seq])
            sums = sums + jnp.sum(grads.astype(f32), axis=1, keepdims=True)
        out_ref[:, span] = jnp.transpose((product * gain + sums * shift).astype(bf16))
        for n in range(3):
            own = slice(n * rows, (n + 1) * rows)
            first = pl.multiple_of(skipped + h * rows, 16)
            weight = turned[n, pl.ds(first, rows), :].astype(f32)
            grad_gain = grad_gain + jnp.sum(weight * product[own], axis=0, keepdims=True)
            grad_shift = grad_shift + jnp.sum(weight * sums[own], axis=0, keepdims=True)
        for n, which in ((3, 0), (4, 2)):
            own = slice(which * rows, (which + 1) * rows)
            first = pl.multiple_of(skipped + h * rows, 16)
            weight = turned[n, pl.ds(first, rows), :].astype(f32)
            grad_embed = grad_embed + jnp.sum(weight * sums[own], axis=0, keepdims=True)
    norms_ref[...] = jnp.concatenate(
        [grad_gain, grad_shift, grad_embed, jnp.zeros((5, gain.shape[1]), f32)], axis=0
    )


def qkv_total_kernel(parts_ref, *out_refs):
    total = parts_ref[0].astype(f32)
    for n in range(1, parts_ref.shape[0]):
        total = total + parts_ref[n].astype(f32)
    count = out_refs[0].shape[1] // 2
    for n, out_ref in enumerate(out_refs):
        second = (n + 3) * count
        out_ref[...] = jnp.concatenate(
            [total[:, n * count : (n + 1) * count], total[:, second : second + count]], axis=1
        )


def tokens_kernel(groups, seq_ref, x_ref, middle_ref, gain_ref, wq_hbm, wk_hbm, wv_hbm, *refs):
    given, (out_ref, held, grads_s, sems) = refs[: 2 * groups], refs[2 * groups :]
    copies = [
        pltpu.make_async_copy(source, held.at[n], sems.at[n])
        for n, source in enumerate((wq_hbm, wk_hbm, wv_hbm))
    ]
    for copy in copies:
        copy.start()
    seq = seq_ref[0]
    count = given[0].shape[0] // 3
    for k in range(groups):
        for h in range(2):
            for which in range(3):
                grads_s[which, rows_for(k ^ seq, h, count), :] = given[h * groups + k][
                    which * count : (which + 1) * count
                ]
    hat, scaled = normalize(x_ref[...].astype(f32))
    total = jnp.zeros(middle_ref.shape, f32)
    for which, copy in enumerate(copies):
        grads = jnp.transpose(grads_s[which])
        copy.wait()
        total = total + dot(grads, held[which], 1, 1)
    out_ref[...] = (
        middle_ref[...] + norm_back(total, hat, scaled, row_of(gain_ref))
    ).astype(bf16)


def whole(shape):
    zeros = (0,) * len(shape)
    return pl.BlockSpec(shape, lambda s: zeros, pipeline_mode=pl.Buffered(1))


def kept(shape):
    zeros = (0,) * len(shape)
    return pl.BlockSpec(shape, lambda s: zeros)


def per_head(shape):
    rest = (0,) * (len(shape) - 1)
    return pl.BlockSpec((1,) + tuple(shape[1:]), lambda s: (s,) + rest)


def params(grid=True):
    return pltpu.CompilerParams(
        dimension_semantics=("arbitrary",) if grid else None, vmem_limit_bytes=VMEM_LIMIT
    )


def takes(microseconds):
    return pl.CostEstimate(
        flops=int(microseconds * SCALE * 1e9), bytes_accessed=int(microseconds * SCALE * 3e6), transcendentals=0
    )


IN_VMEM = pl.BlockSpec(memory_space=pltpu.VMEM)
IN_SMEM = pl.BlockSpec(memory_space=pltpu.SMEM)
IN_HBM = pl.BlockSpec(memory_space=pl.ANY)


def shape_of(shape, kind):
    return jax.ShapeDtypeStruct(shape, kind)


def bias_strips(table):
    heads = table.shape[0]
    out = shape_of((heads, LANES // GRID, GRID, STRIP), f32)
    return pl.pallas_call(
        strips_kernel,
        grid=(heads,),
        in_specs=[per_head(table.shape)],
        out_specs=per_head(out.shape),
        out_shape=out,
        compiler_params=params(),
        cost_estimate=takes(9),
        name="strips",
    )(table)


def project(seq, x, embed, vectors, weights, groups, scale):
    count, width = x.shape
    part = shape_of((3 * width // groups // 2, count), bf16)
    outs = pl.pallas_call(
        partial(project_kernel, scale, groups),
        in_specs=[IN_SMEM] + [IN_VMEM] * 6 + [IN_HBM] * 5,
        out_specs=[IN_VMEM] * (2 * groups + 1),
        out_shape=(part,) * (2 * groups) + (shape_of((count, width), bf16),),
        scratch_shapes=[
            pltpu.VMEM((5, width, width), bf16),
            pltpu.VMEM((3, width, count), bf16),
            pltpu.SemaphoreType.DMA((5,)),
        ],
        compiler_params=params(False),
        cost_estimate=takes(9),
        name="project",
    )(seq, x, embed, *vectors, *weights)
    return outs[:groups], outs[groups : 2 * groups], outs[2 * groups]


def attend(seq, own, place, strips, half, head_size):
    heads = strips.shape[0] // 2
    length = place.shape[1]
    group = heads * head_size
    groups = len(own)
    tall = -(-head_size // 16) * 16
    saved = (
        shape_of((3 * group, length), bf16),
        shape_of((heads, length, length), bf16),
        shape_of((heads, 1, length), f32),
        shape_of((group, length), f32),
    )
    own_strips = pl.BlockSpec(
        (1,) + strips.shape[1:], lambda s: (half * heads + s, 0, 0, 0)
    )
    outs = pl.pallas_call(
        partial(attend_kernel, head_size, groups),
        grid=(heads,),
        in_specs=[IN_SMEM, whole(place.shape), own_strips] + [whole(a.shape) for a in own],
        out_specs=[kept((group, BLOCK))] * groups
        + [
            kept(saved[0].shape),
            per_head(saved[1].shape),
            per_head(saved[2].shape),
            kept(saved[3].shape),
        ],
        out_shape=(shape_of((group, BLOCK), bf16),) * groups + saved,
        scratch_shapes=[
            pltpu.VMEM((length, length), bf16),
            pltpu.VMEM((3 * group, length), f32),
            pltpu.VMEM((LANES, length), bf16),
            pltpu.VMEM((length, LANES), bf16),
            pltpu.VMEM((tall, length), bf16),
            pltpu.VMEM((length, BLOCK), f32),
        ],
        compiler_params=params(),
        cost_estimate=takes(13),
        name="attend",
    )(seq, place, strips, *own)
    return outs[:groups], outs[groups:]


def attend_back(seq, half, grad_mixed, qkv, expo, inverse, mixed, place, head_size):
    heads, length, _ = expo.shape
    group = heads * head_size
    groups = len(grad_mixed)
    tall = -(-head_size // 16) * 16
    table = shape_of((heads, 2, STRIP // LANES, LANES), f32)
    given = pl.BlockSpec((group, BLOCK), lambda s: (half, 0), pipeline_mode=pl.Buffered(1))
    outs = pl.pallas_call(
        partial(attend_back_kernel, head_size, groups),
        grid=(heads,),
        in_specs=[
            IN_SMEM,
            whole(qkv.shape),
            per_head(expo.shape),
            per_head(inverse.shape),
            whole(mixed.shape),
            whole(place.shape),
        ]
        + [given] * groups,
        out_specs=[kept((3 * group, BLOCK))] * groups
        + [per_head(table.shape), kept((8, 3 * group))],
        out_shape=(shape_of((3 * group, BLOCK), bf16),) * groups
        + (table, shape_of((8, 3 * group), f32)),
        scratch_shapes=[
            pltpu.VMEM((1, LANES // GRID, GRID, STRIP), f32),
            pltpu.VMEM((length, length), bf16),
            pltpu.VMEM((3 * group, length), f32),
            pltpu.VMEM((group, length), f32),
            pltpu.VMEM((3 * group, length), f32),
            pltpu.VMEM((length, LANES), bf16),
            pltpu.VMEM((tall, length), bf16),
            pltpu.VMEM((length, LANES), bf16),
            pltpu.VMEM((LANES, length), bf16),
            pltpu.VMEM((length, LANES), bf16),
            pltpu.VMEM((1, length), f32),
            pltpu.VMEM((length, LANES), f32),
            pltpu.VMEM((length, LANES), f32),
        ],
        compiler_params=params(),
        cost_estimate=takes(16),
        name="attend_back",
    )(seq, qkv, expo, inverse, mixed, place, *grad_mixed)
    return outs[:groups], outs[groups:]


def mlp_first(seq, mixed, x, dy, vectors, b_up, w_out, w_up, w_down):
    count, width = x.shape
    hidden = w_up.shape[1]
    step = 512
    chunks = hidden // step
    dma = pltpu.SemaphoreType.DMA
    return pl.pallas_call(
        partial(mlp_first_kernel, len(mixed) // 2, step),
        in_specs=[IN_SMEM] + [IN_VMEM] * 6 + [IN_HBM] * 3 + [IN_VMEM] * len(mixed),
        out_specs=[IN_HBM] * 3 + [IN_VMEM] * 3,
        out_shape=(
            shape_of((count, hidden), bf16),
            shape_of((hidden, count), bf16),
            shape_of((count, hidden), bf16),
            shape_of((2, width, count), bf16),
            shape_of((count, width), f32),
            shape_of((1, hidden), f32),
        ),
        scratch_shapes=[
            pltpu.VMEM((width, width), bf16),
            pltpu.VMEM((chunks, width, step), bf16),
            pltpu.VMEM((chunks, step, width), bf16),
            pltpu.VMEM((chunks, count, step), bf16),
            pltpu.VMEM((chunks, step, count), bf16),
            pltpu.VMEM((chunks, count, step), bf16),
            pltpu.VMEM((count, width), bf16),
            dma((1,)),
        ]
        + [dma((chunks,))] * 5,
        compiler_params=params(False),
        cost_estimate=takes(14),
        name="mlp_first",
    )(seq, x, dy, *vectors, b_up, w_out, w_up, w_down, *mixed)


def mlp_second(seq, middle, dy, vectors, act, inner, w_out, w_up, w_down, groups):
    count, width = middle.shape
    hidden = w_up.shape[1]
    step = 512
    chunks = hidden // step
    part = shape_of((width // groups, count), bf16)
    dma = pltpu.SemaphoreType.DMA
    outs = pl.pallas_call(
        partial(mlp_second_kernel, groups, step),
        in_specs=[IN_SMEM] + [IN_VMEM] * 4 + [IN_HBM] * 5,
        out_specs=[IN_VMEM] * (groups + 4),
        out_shape=(part,) * groups
        + (
            shape_of((count, width), bf16),
            shape_of((count, width), f32),
            shape_of((count, width), bf16),
            shape_of((8, width), f32),
        ),
        scratch_shapes=[
            pltpu.VMEM((width, width), bf16),
            pltpu.VMEM((chunks, width, step), bf16),
            pltpu.VMEM((chunks, step, width), bf16),
            pltpu.VMEM((chunks, count, step), bf16),
            pltpu.VMEM((chunks, count, step), bf16),
            pltpu.VMEM((count, width), f32),
            pltpu.VMEM((count, width), f32),
            pltpu.VMEM((width, count), bf16),
            dma((1,)),
            dma((chunks,)),
            dma((chunks,)),
            dma((chunks,)),
            dma((chunks,)),
        ],
        compiler_params=params(False),
        cost_estimate=takes(14),
        name="mlp_second",
    )(seq, middle, dy, *vectors, act, inner, w_out, w_up, w_down)
    return outs[:groups], outs[groups:]


def pair_grad(order, first, own, other, inner, inner_other, branch, branch_other):
    _, rows, count = own.shape
    blocks, groups = first.shape[0], order.shape[0]
    width = inner.shape[1] // groups
    wide = pl.BlockSpec(
        (count, width),
        lambda s, order_ref, first_ref: (0, order_ref[jnp.minimum(s, groups - 1)]),
    )
    narrow = pl.BlockSpec((count, width), lambda s, order_ref, first_ref: (0, 0))
    left = pl.BlockSpec((2, rows, count), lambda s, order_ref, first_ref: (0, 0, 0))
    block = (blocks, 1, rows // 2 // blocks, width)
    return pl.pallas_call(
        pair_grad_kernel,
        grid_spec=pltpu.PrefetchScalarGridSpec(
            num_scalar_prefetch=2,
            grid=(groups + 1,),
            in_specs=[left, left, wide, wide, narrow, narrow],
            out_specs=pl.BlockSpec(block, lambda s, order_ref, first_ref: (0, s, 0, 0)),
            scratch_shapes=[pltpu.VMEM((rows // 2, count), bf16)] * 2,
        ),
        out_shape=shape_of((blocks, groups + 1) + block[2:], bf16),
        compiler_params=params(),
        cost_estimate=takes(10),
        name="pair_grad",
    )(order, first, own, other, inner, inner_other, branch, branch_other)


def down_grad(act, dy):
    return pl.pallas_call(
        down_grad_kernel,
        in_specs=[IN_VMEM, IN_VMEM],
        out_specs=IN_VMEM,
        out_shape=shape_of((dy.shape[2], act.shape[1]), bf16),
        compiler_params=params(False),
        cost_estimate=takes(8),
        name="down_grad",
    )(act, dy)


def qkv_grad(seq, grads, hat, gain, shift, weights):
    width = hat.shape[2]
    count = grads[0].shape[0]
    columns = -(-(2 * count // 3 + LANES - GRID) // LANES) * LANES
    return pl.pallas_call(
        partial(qkv_grad_kernel, len(grads) // 2),
        in_specs=[IN_SMEM] + [IN_VMEM] * 3 + [IN_HBM] * 5 + [IN_VMEM] * len(grads),
        out_specs=[IN_VMEM] * 2,
        out_shape=(shape_of((width, 2 * count), bf16), shape_of((8, width), f32)),
        scratch_shapes=[
            pltpu.VMEM((5, width, columns), bf16),
            pltpu.VMEM((5, columns, width), bf16),
            pltpu.SemaphoreType.DMA((5,)),
        ],
        compiler_params=params(False),
        cost_estimate=takes(8),
        name="qkv_grad",
    )(seq, hat, gain, shift, *weights, *grads)


def qkv_total(parts):
    _, rows, columns = parts.shape
    return pl.pallas_call(
        qkv_total_kernel,
        out_shape=(shape_of((rows, columns // 3), f32),) * 3,
        compiler_params=params(False),
        cost_estimate=takes(2),
        name="qkv_total",
    )(parts)


def token_grad(seq, grads, x, middle, gain, weights):
    count, width = x.shape
    return pl.pallas_call(
        partial(tokens_kernel, len(grads) // 2),
        in_specs=[IN_SMEM] + [IN_VMEM] * 3 + [IN_HBM] * 3 + [IN_VMEM] * len(grads),
        out_specs=IN_VMEM,
        out_shape=shape_of((count, width), bf16),
        scratch_shapes=[
            pltpu.VMEM((3, width, width), bf16),
            pltpu.VMEM((3, width, count), bf16),
            pltpu.SemaphoreType.DMA((3,)),
        ],
        compiler_params=params(False),
        cost_estimate=takes(9),
        name="token_grad",
    )(seq, x, middle, gain, *weights, *grads)


def exchange(array, axis, step):
    size = lax.axis_size(axis)
    return lax.ppermute(array, axis, [(i, i ^ step) for i in range(size)])


def sum_over(vector, axis):
    step = 1
    while step < lax.axis_size(axis):
        vector = vector + exchange(vector, axis, step)
        step *= 2
    return vector


def swap(parts, axis):
    return [parts[0]] + [exchange(parts[k], axis, k) for k in range(1, len(parts))]


def halve(array, axis, dim, step, bit):
    keep = lax.dynamic_index_in_dim(array, bit, dim, keepdims=False)
    send = lax.dynamic_index_in_dim(array, 1 - bit, dim, keepdims=False)
    return (keep.astype(f32) + exchange(send, axis, step).astype(f32)).astype(bf16)


def add_low(left, right):
    return (left.astype(f32) + right.astype(f32)).astype(bf16)


def tie(*arrays):
    return lax.optimization_barrier(arrays)


def key_places(rel_index):
    first = rel_index[0]
    top = jnp.max(first)
    row = top // SPAN - first // SPAN
    column = top % SPAN - first % SPAN
    return (row * GRID + column)[None, :].astype(jnp.int32)


def table_grad(folded):
    heads = folded.shape[0]
    parts = folded.reshape(heads, 2, STRIP // LANES, 2, LANES // 2)
    parts = jnp.transpose(parts, (0, 2, 3, 1, 4)).reshape(heads, 2 * GRID, LANES // 2)
    return parts[:, :SPAN, :SPAN].reshape(heads, SPAN * SPAN)


def per_device(
    tokens,
    timesteps,
    rel_index,
    time_table,
    bias_table,
    gain_one,
    shift_one,
    w_query,
    w_key,
    w_value,
    t_query,
    t_value,
    b_query,
    b_value,
    w_out,
    b_out,
    gain_two,
    shift_two,
    w_up,
    b_up,
    w_down,
    b_down,
    cotangent,
):
    _, local, width = tokens.shape
    hidden = w_up.shape[1]
    heads = bias_table.shape[0]
    head_size = width // heads
    n_dp, n_seq = lax.axis_size("dp"), lax.axis_size("seq")
    dp, seq = lax.axis_index("dp"), lax.axis_index("seq")
    own_heads = heads // n_seq
    group = own_heads * head_size
    half = group // 2
    scale = head_size ** (-0.5)
    table_rows = time_table.shape[0]
    down_rows, out_rows = hidden // n_dp, width // n_dp

    def own_columns(array):
        return lax.dynamic_slice_in_dim(array, seq * group, group, axis=array.ndim - 1)

    x, dy = tokens[0], cotangent[0]
    here = seq.astype(jnp.int32)[None]
    embed = lax.dynamic_slice_in_dim(time_table, timesteps[0], 1, 0)
    *mine, hat_one = project(
        here,
        x,
        embed,
        (gain_one, shift_one, b_query, b_value),
        (w_key, w_query, t_query, w_value, t_value),
        n_seq,
        scale,
    )
    own_0 = swap(mine[0], "seq")
    dy_all = lax.all_gather(dy, "dp", axis=0)
    place = key_places(rel_index)
    table = lax.dynamic_slice_in_dim(bias_table, seq * own_heads, own_heads, 0)
    table = jnp.pad(
        table.reshape(own_heads, SPAN, SPAN), ((0, 0), (0, 72 - SPAN), (0, LANES - SPAN))
    )
    table, hat_one = tie(table, hat_one)
    strips = bias_strips(table)
    own_0, parts_1, place, strips = tie(own_0, mine[1], place, strips)
    own_1 = swap(parts_1, "seq")
    tokens_0, saved_0 = attend(here, own_0, place, strips, 0, head_size)

    own_1, tokens_0, saved_0, place, dy_all = tie(own_1, tokens_0, saved_0, place, dy_all)
    mixed_0 = swap(tokens_0, "seq")
    tokens_1, saved_1 = attend(here, own_1, place, strips, 1, head_size)

    tokens_1, saved_1, mixed_0 = tie(tokens_1, saved_1, mixed_0)
    mixed_1 = swap(tokens_1, "seq")

    mixed_1, hat_one = tie(mixed_1, hat_one)
    hat_all = lax.all_gather(hat_one, "seq", axis=0)
    act, act_t, grad_inner, turned, middle, up_sum = mlp_first(
        here,
        mixed_0 + mixed_1,
        x,
        dy,
        (b_out, gain_two, shift_two),
        b_up[None],
        w_out,
        w_up,
        w_down,
    )

    core = dp % 2
    act_parts = lax.all_to_all(act_t.reshape(n_dp, down_rows, local), "dp", 0, 0)
    turned_other = exchange(turned, "dp", 1)
    inner_other = exchange(grad_inner, "dp", 1)
    grad_mixed, (result, grad_middle, branch, sums_two) = mlp_second(
        here, middle, dy, (b_down, gain_two), act, grad_inner, w_out, w_up, w_down, n_seq
    )

    grad_mixed, result, grad_middle, branch, sums_two, turned_other, inner_other = tie(
        grad_mixed, result, grad_middle, branch, sums_two, turned_other, inner_other
    )
    grad_mixed = swap(grad_mixed, "seq")
    branch_other = exchange(branch, "dp", 1)
    first = (2 * jnp.arange(n_dp // 2) + core) * out_rows
    turned_rows = [turned, turned_other]
    if out_rows % 16:
        first = jnp.zeros((1,), jnp.int32)
        turned_rows = [
            jnp.tile(
                lax.dynamic_index_in_dim(
                    a.reshape(2, n_dp // 2, 2, out_rows, local), core, 2, keepdims=False
                ).reshape(2, width // 2, local),
                (1, 2, 1),
            )
            for a in turned_rows
        ]
    pair = pair_grad(
        (jnp.arange(n_seq) ^ seq).astype(jnp.int32),
        first.astype(jnp.int32),
        *turned_rows,
        grad_inner,
        inner_other,
        branch,
        branch_other,
    )

    pair, act_parts = tie(pair, act_parts)
    part_down = down_grad(act_parts, dy_all)

    part_down, grad_mixed, pair, hat_all = tie(part_down, grad_mixed, pair, hat_all)
    grad_w_down = lax.psum_scatter(part_down, "seq", scatter_dimension=0, tiled=True)
    if out_rows % 16:
        pair = jnp.swapaxes(pair.reshape(n_seq + 1, n_dp // 2, out_rows, width), 0, 1)
    same_core = [list(range(c, n_dp, 2)) for c in range(2)]
    pair = lax.all_to_all(pair, "dp", 0, 0, axis_index_groups=same_core)
    grads_0, (table_0, sums_0) = attend_back(here, 0, grad_mixed, *saved_0, place, head_size)

    grads_0, table_0, sums_0, grad_mixed, place = tie(grads_0, table_0, sums_0, grad_mixed, place)
    heads_0 = swap(grads_0, "seq")
    grads_1, (table_1, sums_1) = attend_back(here, 1, grad_mixed, *saved_1, place, head_size)

    grads_1, table_1, sums_1, heads_0, grad_w_down = tie(
        grads_1, table_1, sums_1, heads_0, grad_w_down
    )
    heads_1 = swap(grads_1, "seq")
    product, norms = qkv_grad(
        here,
        list(grads_0) + list(grads_1),
        hat_all,
        gain_one,
        shift_one,
        (w_query, w_key, w_value, t_query, t_value),
    )

    product, norms, pair = tie(product, norms, pair)

    def source_sum(parts):
        return jnp.sum(parts.astype(f32), axis=0).astype(bf16)

    near_keep, near_send = (source_sum(pair[:, n:n_seq:2]) for n in range(2))

    (
        heads_1,
        near_keep,
        near_send,
        pair,
        norms,
        table_0,
        table_1,
        sums_0,
        sums_1,
        up_sum,
        sums_two,
    ) = tie(
        heads_1,
        near_keep,
        near_send,
        pair,
        norms,
        table_0,
        table_1,
        sums_0,
        sums_1,
        up_sum,
        sums_two,
    )
    near_received = exchange(near_send, "seq", 1)
    out_part = source_sum(pair[:, n_seq])
    grad_tokens = token_grad(
        here, heads_0 + heads_1, x, grad_middle, gain_one, (w_query, w_key, w_value)
    )
    query_sum, value_sum = (
        jnp.concatenate([sums[0, n * half : (n + 1) * half] for sums in (sums_0, sums_1)])
        for n in (0, 2)
    )
    own_image = lax.broadcasted_iota(jnp.int32, (n_dp, 1), 0) == dp

    def slot(row):
        return jnp.where(own_image, row[None, :], 0.0).reshape(-1)

    apart = [table_grad(jnp.concatenate([table_0, table_1])).reshape(-1), query_sum, value_sum]
    summed = [
        slot(norms[2]),
        up_sum[0],
        sums_two[:4].reshape(-1),
        norms[:2].reshape(-1),
    ]
    images = [slot(jnp.concatenate([query_sum, value_sum, timesteps.astype(f32)]))]
    sizes = [sum(a.shape[0] for a in part) for part in (apart, summed, images)]
    vector = sum_over(jnp.concatenate(apart + summed + images), "dp")

    vector, out_part, product, grad_tokens, near_received = tie(
        vector, out_part, product, grad_tokens, near_received
    )
    far_keep, far_send = (
        add_low(near_keep[n], near_received[n]) for n in range(2)
    )
    far_received = exchange(far_send, "seq", 2)
    grad_qkv = lax.all_to_all(product.reshape(n_dp, out_rows, 3 * group), "dp", 0, 0)
    image_sums = vector[sizes[0] + sizes[1] :].reshape(n_dp, 2 * group + 1)
    steps_all = image_sums[:, 2 * group].astype(jnp.int32)
    apart = vector[: sizes[0]].astype(bf16)[None]
    summed = vector[sizes[0] : sizes[0] + sizes[1]]
    apart = jnp.concatenate([apart, exchange(apart, "seq", 1)], axis=0)
    summed = summed + exchange(summed, "seq", 1)

    apart, summed, out_part = tie(apart, summed, out_part)
    far_apart, far_summed = exchange(apart, "seq", 2), exchange(summed, "seq", 2)
    out_part = out_part.reshape(out_rows, 2, n_seq // 2, group)
    out_part = halve(out_part, "seq", 2, 1, seq & 1)

    far_apart, far_summed, out_part, far_received = tie(
        far_apart, far_summed, out_part, far_received
    )
    grad_qkv = qkv_total(grad_qkv)
    grad_w_up = far_keep.astype(f32) + far_received.astype(f32)
    grad_w_out = halve(out_part, "seq", 1, 2, seq >> 1)
    grad_w_down = jnp.transpose(grad_w_down.astype(f32))
    grad_w_out = grad_w_out.astype(f32)
    apart = jnp.concatenate([apart, far_apart], axis=0)
    apart = jnp.concatenate(
        [lax.dynamic_index_in_dim(apart, n ^ seq, 0) for n in range(n_seq)], axis=0
    ).astype(f32)
    both = summed + far_summed
    table_size = own_heads * SPAN * SPAN
    grad_bias_table = apart[:, :table_size].reshape(heads, SPAN * SPAN)
    grad_b_query = apart[:, table_size : table_size + group].reshape(-1)
    grad_b_value = apart[:, table_size + group :].reshape(-1)
    embed_size = n_dp * width
    embed_rows = both[:embed_size].reshape(n_dp, width)
    grad_b_up = both[embed_size : embed_size + hidden]
    rest = both[embed_size + hidden :].reshape(6, width)
    grad_b_down, grad_gain_two, grad_shift_two, grad_b_out, grad_gain_one, grad_shift_one = (
        rest[r] for r in range(6)
    )

    embeds = lax.dynamic_slice_in_dim(
        jnp.take(time_table, steps_all, axis=0), dp * out_rows, out_rows, axis=1
    ).astype(f32)
    grad_t_query = jnp.dot(embeds.T, image_sums[:, :group], precision=HIGHEST)
    grad_t_value = jnp.dot(embeds.T, image_sums[:, group : 2 * group], precision=HIGHEST)
    onehot = (
        steps_all[:, None] == jnp.arange(table_rows, dtype=jnp.int32)[None, :]
    ).astype(f32)
    grad_time_table = jnp.dot(onehot.T, embed_rows, precision=HIGHEST)

    return (
        result[None],
        grad_tokens[None],
        *grad_qkv,
        grad_t_query,
        grad_t_value,
        grad_w_out,
        grad_w_up,
        grad_w_down,
        grad_gain_one,
        grad_shift_one,
        grad_b_query,
        grad_b_value,
        grad_b_out,
        grad_gain_two,
        grad_shift_two,
        grad_b_up,
        grad_b_down,
        grad_bias_table,
        grad_time_table,
    )


def solution(mesh):
    split, copied, by_block = P("dp", "seq", None), P(), P("dp", "seq")
    in_specs = (split, P("dp"), P("seq", None)) + (copied,) * 19 + (split,)
    out_specs = (split, split) + (by_block,) * 8 + (copied,) * 11
    return jax.shard_map(
        per_device, mesh=mesh, in_specs=in_specs, out_specs=out_specs, check_vma=False
    )
```

```python
from functools import partial

import jax
import jax.numpy as jnp
from jax import lax
from jax.experimental import pallas as pl
from jax.experimental.pallas import tpu as pltpu
from jax.sharding import PartitionSpec as P

GRID = 32
SPAN = 2 * GRID - 1
STRIP = 2 * GRID * GRID
LANES = 128
BLOCK = 256
NORM_EPS = 1e-06
f32, bf16 = jnp.float32, jnp.bfloat16
HIGHEST = lax.Precision.HIGHEST
SCALE = 0.2
VMEM_LIMIT = 58 * 1024 * 1024


def dot(left, right, left_dim=1, right_dim=0):
    return lax.dot_general(
        left, right, (((left_dim,), (right_dim,)), ((), ())), preferred_element_type=f32
    )


def normalize(values):
    centered = values - jnp.mean(values, axis=-1, keepdims=True)
    scaled = lax.rsqrt(jnp.mean(centered * centered, axis=-1, keepdims=True) + NORM_EPS)
    return centered * scaled, scaled


def norm_back(grad_norm, normed, scaled, gain):
    inner = grad_norm * gain
    return scaled * (
        inner
        - jnp.mean(inner, axis=-1, keepdims=True)
        - normed * jnp.mean(inner * normed, axis=-1, keepdims=True)
    )


def row_of(ref):
    return ref[...].reshape(1, ref.shape[0])


def fold_rows(values, op):
    return op(values.reshape(values.shape[0] // 8, 8, values.shape[1]), axis=0)


def strip_place(key_row):
    first = (GRID - 1 - key_row) * GRID
    return (first % LANES) // GRID, first // LANES * LANES


def widen(rows, height):
    fill = jnp.zeros((height - rows.shape[0], rows.shape[1]), rows.dtype)
    return jnp.concatenate([rows, fill], axis=0)


def rows_for(group, half, count):
    return pl.ds(pl.multiple_of((2 * group + half) * count, 16), count)


def block_of(index):
    return pl.ds(pl.multiple_of(index * BLOCK, BLOCK), BLOCK)


def build_permutation(place_ref, perm):
    length = perm.shape[0]

    def rows_of(i, carry):
        first = pl.multiple_of(i * BLOCK, BLOCK)
        spots = lax.broadcasted_iota(jnp.int32, (BLOCK, length), 0) + first
        hit = spots == place_ref[...]
        perm[pl.ds(first, BLOCK), :] = jnp.where(hit, 1.0, 0.0).astype(bf16)
        return carry

    lax.fori_loop(0, length // BLOCK, rows_of, 0)


def strips_kernel(table_ref, strips_ref):
    lane = lax.broadcasted_iota(jnp.int32, (GRID, LANES), 1)
    per_tile = LANES // GRID

    def tile_of(n):
        whole_tile = jnp.zeros((GRID, LANES), f32)
        for k in range(per_tile):
            row = table_ref[0, pl.ds(per_tile * n + k, 1), :]
            turned = pltpu.roll(
                jnp.broadcast_to(row, (GRID, LANES)),
                (GRID * k - GRID + 1) % LANES,
                1,
                stride=1,
                stride_axis=0,
            )
            whole_tile = jnp.where(lane // GRID == k, turned, whole_tile)
        return whole_tile

    tiles = [tile_of(n) for n in range(STRIP // LANES + 1)]
    for n in range(STRIP // LANES):
        span = slice(n * LANES, (n + 1) * LANES)
        strips_ref[0, 0, :, span] = tiles[n]
        for s in range(1, per_tile):
            back = LANES - GRID * s
            strips_ref[0, s, :, span] = jnp.where(
                lane < back, pltpu.roll(tiles[n], back, 1), pltpu.roll(tiles[n + 1], back, 1)
            )


def fold_strips(strips, table_ref):
    lane = lax.broadcasted_iota(jnp.int32, (GRID, LANES), 1)
    row = lax.broadcasted_iota(jnp.int32, (8, LANES), 0)
    per_tile = LANES // GRID

    before = [jnp.zeros((GRID, LANES), f32)] * (per_tile - 1)
    for n in range(STRIP // LANES):
        span = slice(n * LANES, (n + 1) * LANES)
        total = strips[0, 0, :, span]
        turned = []
        for s in range(1, per_tile):
            turned.append(pltpu.roll(strips[0, s, :, span], GRID * s, 1))
            total = total + jnp.where(lane >= GRID * s, turned[-1], before[s - 1])
        before = turned
        for parity in range(2):
            part = jnp.where(lane // GRID % 2 == parity, total, 0.0)
            if parity:
                part = pltpu.roll(part, LANES - GRID, 1)
            part = pltpu.roll(part[:16], 16, 1) + part[16:]
            part = pltpu.roll(part[:8], 8, 1) + part[8:]
            for step in (4, 2, 1):
                part = jnp.where(row % (2 * step) < step, pltpu.roll(part, step, 1), part)
            table_ref[0, parity, n : n + 1, :] = jnp.sum(part, axis=0, keepdims=True)


def project_kernel(
    scale,
    groups,
    seq_ref,
    x_ref,
    embed_ref,
    gain_ref,
    shift_ref,
    b_query_ref,
    b_value_ref,
    wk_hbm,
    wq_hbm,
    tq_hbm,
    wv_hbm,
    tv_hbm,
    *refs,
):
    outs, (hat_ref, held, turned, sems) = refs[: 2 * groups], refs[2 * groups :]
    sources = (wk_hbm, wq_hbm, tq_hbm, wv_hbm, tv_hbm)
    copies = [
        pltpu.make_async_copy(source, held.at[n], sems.at[n]) for n, source in enumerate(sources)
    ]
    for copy in copies:
        copy.start()
    hat, _ = normalize(x_ref[...].astype(f32))
    hat_ref[...] = hat.astype(bf16)
    act = (hat * row_of(gain_ref) + row_of(shift_ref)).astype(bf16)
    embed = jnp.broadcast_to(embed_ref[...].astype(f32), (16, embed_ref.shape[1])).astype(bf16)
    count = outs[0].shape[0] // 3
    seq = seq_ref[0]

    def put(which, value):
        turned[which] = jnp.transpose(value.astype(bf16))
        for k in range(groups):
            for h in range(2):
                outs[h * groups + k][which * count : (which + 1) * count, :] = turned[
                    which, rows_for(k ^ seq, h, count), :
                ]

    copies[0].wait()
    put(1, dot(act, held[0]))
    copies[1].wait()
    copies[2].wait()
    time_query = dot(embed, held[2])[0:1]
    put(0, (dot(act, held[1]) + time_query + row_of(b_query_ref)) * scale)
    copies[3].wait()
    copies[4].wait()
    time_value = dot(embed, held[4])[0:1]
    put(2, dot(act, held[3]) + time_value + row_of(b_value_ref))


def attend_kernel(
    head_size,
    groups,
    seq_ref,
    place_ref,
    strips_ref,
    *refs,
):
    own, outs = refs[:groups], refs[groups : 2 * groups]
    qkv_ref, expo_ref, inverse_ref, mixed_ref = refs[2 * groups : 2 * groups + 4]
    perm, by_place, query_s, key_s, value_s, scores_s = refs[2 * groups + 4 :]
    seq = seq_ref[0]
    head = pl.program_id(0)
    group, length = mixed_ref.shape
    tiles = length // BLOCK

    @pl.when(head == 0)
    def _():
        build_permutation(place_ref, perm)

        def arrange(i, carry):
            span = pl.ds(pl.multiple_of(i * BLOCK, BLOCK), BLOCK)
            part = jnp.zeros((3 * group, BLOCK), f32)
            for k in range(groups):
                part = part + dot(own[k][...], perm[span, block_of(k ^ seq)], 1, 1)
            by_place[:, span] = part
            qkv_ref[:, span] = part.astype(bf16)
            return carry

        lax.fori_loop(0, tiles, arrange, 0)

    def rows_of(which):
        first = pl.multiple_of(which * group + head * head_size, 8)
        return by_place[pl.ds(first, head_size), :]

    query_s[...] = widen(rows_of(0), LANES).astype(bf16)
    key_s[...] = jnp.transpose(widen(rows_of(1), LANES)).astype(bf16)
    value_s[...] = widen(rows_of(2), value_s.shape[0]).astype(bf16)
    own_rows = pl.ds(pl.multiple_of(head * head_size, 8), head_size)

    def tile(t, carry):
        first = pl.multiple_of(t * BLOCK, BLOCK)
        span = pl.ds(first, BLOCK)
        query = query_s[:, span]
        peak = jnp.full((8, BLOCK), -jnp.inf, f32)
        for c in range(tiles):
            keys = slice(c * BLOCK, (c + 1) * BLOCK)
            pieces = []
            for key_row in range(c * BLOCK // GRID, (c + 1) * BLOCK // GRID):
                shift, start = strip_place(key_row)
                pieces.append(strips_ref[0, shift, :, pl.ds(first + start, BLOCK)])
            scores = dot(key_s[keys, :], query) + jnp.concatenate(pieces, axis=0)
            scores_s[keys, :] = scores
            peak = jnp.maximum(peak, fold_rows(scores, jnp.max))
        peak = jnp.max(peak, axis=0, keepdims=True)
        total = jnp.zeros((8, BLOCK), f32)
        mixed = jnp.zeros((value_s.shape[0], BLOCK), f32)
        for c in range(tiles):
            keys = slice(c * BLOCK, (c + 1) * BLOCK)
            expo = jnp.exp(scores_s[keys, :] - peak)
            total = total + fold_rows(expo, jnp.sum)
            low = expo.astype(bf16)
            expo_ref[0, keys, span] = low
            mixed = mixed + dot(value_s[:, keys], low)
        inverse = 1.0 / jnp.sum(total, axis=0, keepdims=True)
        inverse_ref[0, :, span] = inverse
        mixed_ref[own_rows, span] = (mixed * inverse)[:head_size]
        return carry

    lax.fori_loop(0, tiles, tile, 0)

    @pl.when(head == pl.num_programs(0) - 1)
    def _():
        low = mixed_ref[...].astype(bf16)
        for k in range(groups):
            outs[k][...] = dot(low, perm[:, block_of(k ^ seq)]).astype(bf16)


def attend_back_kernel(
    head_size,
    groups,
    seq_ref,
    qkv_ref,
    expo_ref,
    inverse_ref,
    mixed_ref,
    place_ref,
    *refs,
):
    given, outs = refs[:groups], refs[groups : 2 * groups]
    (
        table_ref,
        sums_ref,
        strips_ref,
        perm,
        by_place,
        grad_place,
        grads,
        query_s,
        key_s,
        value_s,
        grad_s,
        grad_t,
        offset_s,
        grad_key,
        grad_value,
    ) = refs[2 * groups :]
    seq = seq_ref[0]
    head = pl.program_id(0)
    group, length = mixed_ref.shape
    tiles = length // BLOCK
    scale = head_size ** (-0.5)

    @pl.when(head == 0)
    def _():
        build_permutation(place_ref, perm)

        def arrange(i, carry):
            span = pl.ds(pl.multiple_of(i * BLOCK, BLOCK), BLOCK)
            part = jnp.zeros((group, BLOCK), f32)
            for k in range(groups):
                part = part + dot(given[k][...], perm[span, block_of(k ^ seq)], 1, 1)
            grad_place[:, span] = part
            by_place[:, span] = qkv_ref[:, span].astype(f32)
            return carry

        lax.fori_loop(0, tiles, arrange, 0)

    own_rows = pl.ds(pl.multiple_of(head * head_size, 8), head_size)

    def rows_of(which):
        first = pl.multiple_of(which * group + head * head_size, 8)
        return by_place[pl.ds(first, head_size), :]

    query_s[...] = jnp.transpose(widen(rows_of(0), LANES)).astype(bf16)
    key_s[...] = widen(rows_of(1), key_s.shape[0]).astype(bf16)
    value_s[...] = jnp.transpose(widen(rows_of(2), LANES)).astype(bf16)
    grad = grad_place[own_rows, :]
    inverse = inverse_ref[0]
    offset_s[...] = inverse * jnp.sum(grad * mixed_ref[own_rows, :], axis=0, keepdims=True)
    grad = widen(grad * inverse, LANES)
    grad_s[...] = grad.astype(bf16)
    grad_t[...] = jnp.transpose(grad).astype(bf16)
    grad_key[...] = jnp.zeros_like(grad_key)
    grad_value[...] = jnp.zeros_like(grad_value)
    strips_ref[...] = jnp.zeros_like(strips_ref)

    def tile(t, carry):
        first = pl.multiple_of(t * BLOCK, BLOCK)
        span = pl.ds(first, BLOCK)
        grad_tile = grad_s[:, span]
        offset = offset_s[:, span]
        grad_query = jnp.zeros((key_s.shape[0], BLOCK), f32)
        for c in range(tiles):
            keys = slice(c * BLOCK, (c + 1) * BLOCK)
            expo = expo_ref[0, keys, span]
            grad_scores = expo.astype(f32) * (dot(value_s[keys, :], grad_tile) - offset)
            for row in range(BLOCK // GRID):
                shift, start = strip_place(c * BLOCK // GRID + row)
                strips_ref[0, shift, :, pl.ds(first + start, BLOCK)] += grad_scores[
                    row * GRID : (row + 1) * GRID
                ]
            low = grad_scores.astype(bf16)
            grad_query = grad_query + dot(key_s[:, keys], low)
            grad_key[keys, :] += dot(low, query_s[span, :])
            grad_value[keys, :] += dot(expo, grad_t[span, :])
        grads[own_rows, span] = grad_query[:head_size] * scale
        return carry

    lax.fori_loop(0, tiles, tile, 0)
    for which, total in ((1, grad_key), (2, grad_value)):
        first = pl.multiple_of(which * group + head * head_size, 8)
        grads[pl.ds(first, head_size), :] = jnp.transpose(total[...])[:head_size]

    @pl.when(head >= 0)
    def _():
        fold_strips(strips_ref, table_ref)

    @pl.when(head == pl.num_programs(0) - 1)
    def _():
        low = grads[...].astype(bf16)
        sums_ref[...] = dot(jnp.ones((8, length), bf16), low, 1, 1)
        for k in range(groups):
            outs[k][...] = dot(low, perm[:, block_of(k ^ seq)]).astype(bf16)


def mlp_first_kernel(
    groups,
    step,
    seq_ref,
    x_ref,
    dy_ref,
    b_out_ref,
    gain_ref,
    shift_ref,
    b_up_ref,
    w_out_hbm,
    w_up_hbm,
    w_down_hbm,
    *refs,
):
    given = refs[: 2 * groups]
    act_hbm, act_t_hbm, inner_hbm, turned_ref, middle_ref, up_sum_ref = refs[
        2 * groups : 2 * groups + 6
    ]
    (
        w_out_s,
        w_up_s,
        w_down_s,
        act_s,
        act_t_s,
        inner_s,
        norm_s,
        sem,
        up_sems,
        down_sems,
        act_sems,
        act_t_sems,
        inner_sems,
    ) = refs[2 * groups + 6 :]
    chunks = w_up_s.shape[0]
    seq = seq_ref[0]

    def span_of(i):
        return pl.ds(pl.multiple_of(i * step, step), step)

    def fetch(i):
        return (
            pltpu.make_async_copy(w_up_hbm.at[:, span_of(i)], w_up_s.at[i], up_sems.at[i]),
            pltpu.make_async_copy(w_down_hbm.at[span_of(i), :], w_down_s.at[i], down_sems.at[i]),
        )

    def put(i):
        return (
            pltpu.make_async_copy(act_s.at[i], act_hbm.at[:, span_of(i)], act_sems.at[i]),
            pltpu.make_async_copy(act_t_s.at[i], act_t_hbm.at[span_of(i), :], act_t_sems.at[i]),
            pltpu.make_async_copy(inner_s.at[i], inner_hbm.at[:, span_of(i)], inner_sems.at[i]),
        )

    def begin(i, carry):
        for copy in fetch(i):
            copy.start()
        return carry

    out_copy = pltpu.make_async_copy(w_out_hbm, w_out_s, sem.at[0])
    out_copy.start()
    lax.fori_loop(0, chunks, begin, 0)
    count = given[0].shape[0]
    for k in range(groups):
        for h in range(2):
            turned_ref[1, rows_for(k ^ seq, h, count), :] = given[h * groups + k][...]
    mixed = jnp.transpose(turned_ref[1])
    out_copy.wait()
    middle = x_ref[...].astype(f32) + dot(mixed, w_out_s[...]) + row_of(b_out_ref)
    hat, _ = normalize(middle)
    middle_ref[...] = middle
    norm = (hat * row_of(gain_ref) + row_of(shift_ref)).astype(bf16)
    norm_s[...] = norm
    turned_ref[0] = jnp.transpose(norm)

    def chunk(i, carry):
        for copy in fetch(i):
            copy.wait()
        inner = dot(norm_s[...], w_up_s[i]) + b_up_ref[:, span_of(i)]
        cdf = 0.5 * (1.0 + lax.erf(inner * (0.5**0.5)))
        pdf = jnp.exp(-0.5 * inner * inner) * 0.3989422804014327
        act = (inner * cdf).astype(bf16)
        low = (dot(dy_ref[...], w_down_s[i], 1, 1) * (cdf + inner * pdf)).astype(bf16)
        act_s[i] = act
        act_t_s[i] = jnp.transpose(act)
        inner_s[i] = low
        up_sum_ref[:, span_of(i)] = jnp.sum(low.astype(f32), axis=0, keepdims=True)
        for copy in put(i):
            copy.start()
        return carry

    lax.fori_loop(0, chunks, chunk, 0)

    def finish(i, carry):
        for copy in put(i):
            copy.wait()
        return carry

    lax.fori_loop(0, chunks, finish, 0)


def mlp_second_kernel(
    groups,
    step,
    seq_ref,
    middle_ref,
    dy_ref,
    b_down_ref,
    gain_ref,
    act_hbm,
    inner_hbm,
    w_out_hbm,
    w_up_hbm,
    w_down_hbm,
    *refs,
):
    outs = refs[:groups]
    result_ref, grad_middle_ref, branch_ref, sums_ref = refs[groups : groups + 4]
    (
        w_out_s,
        w_up_s,
        w_down_s,
        act_s,
        inner_s,
        result_s,
        grad_s,
        mixed_s,
        sem,
        up_sems,
        down_sems,
        act_sems,
        inner_sems,
    ) = refs[groups + 4 :]
    chunks = w_up_s.shape[0]

    def span_of(i):
        return pl.ds(pl.multiple_of(i * step, step), step)

    def fetch(i):
        return (
            pltpu.make_async_copy(w_up_hbm.at[:, span_of(i)], w_up_s.at[i], up_sems.at[i]),
            pltpu.make_async_copy(w_down_hbm.at[span_of(i), :], w_down_s.at[i], down_sems.at[i]),
            pltpu.make_async_copy(act_hbm.at[:, span_of(i)], act_s.at[i], act_sems.at[i]),
            pltpu.make_async_copy(inner_hbm.at[:, span_of(i)], inner_s.at[i], inner_sems.at[i]),
        )

    def begin(i, carry):
        for copy in fetch(i):
            copy.start()
        return carry

    lax.fori_loop(0, chunks, begin, 0)
    out_copy = pltpu.make_async_copy(w_out_hbm, w_out_s, sem.at[0])
    out_copy.start()
    result_s[...] = middle_ref[...] + row_of(b_down_ref)
    grad_s[...] = jnp.zeros_like(grad_s)

    def chunk(i, carry):
        for copy in fetch(i):
            copy.wait()
        result_s[...] += dot(act_s[i], w_down_s[i])
        grad_s[...] += dot(inner_s[i], w_up_s[i], 1, 1)
        return carry

    lax.fori_loop(0, chunks, chunk, 0)
    result_ref[...] = result_s[...].astype(bf16)
    hat, scaled = normalize(middle_ref[...])
    dy = dy_ref[...].astype(f32)
    grad_norm = grad_s[...]
    grad_middle = dy + norm_back(grad_norm, hat, scaled, row_of(gain_ref))
    branch = grad_middle.astype(bf16)
    grad_middle_ref[...] = grad_middle
    branch_ref[...] = branch
    out_copy.wait()
    mixed_s[...] = dot(w_out_s[...], branch, 1, 1).astype(bf16)
    count = outs[0].shape[0]
    for k in range(groups):
        rows = pl.ds(pl.multiple_of((k ^ seq_ref[0]) * count, 16), count)
        outs[k][...] = mixed_s[rows, :]
    sums_ref[...] = jnp.concatenate(
        [
            jnp.sum(dy, axis=0, keepdims=True),
            jnp.sum(grad_norm * hat, axis=0, keepdims=True),
            jnp.sum(grad_norm, axis=0, keepdims=True),
            jnp.sum(branch.astype(f32), axis=0, keepdims=True),
            jnp.zeros((4, dy.shape[1]), f32),
        ],
        axis=0,
    )


def pair_grad_kernel(
    order_ref,
    first_ref,
    own_ref,
    other_ref,
    inner_ref,
    inner_other,
    branch_ref,
    branch_other,
    out_ref,
    own_s,
    other_s,
):
    step = pl.program_id(0)
    last = pl.num_programs(0) - 1
    blocks = first_ref.shape[0]
    count = own_s.shape[0] // blocks

    def choose(which):
        for n in range(blocks):
            source = pl.ds(pl.multiple_of(first_ref[n], 16), count)
            own_s[n * count : (n + 1) * count, :] = own_ref[which, source, :]
            other_s[n * count : (n + 1) * count, :] = other_ref[which, source, :]

    def put(right, right_other):
        low = (dot(own_s[...], right[...]) + dot(other_s[...], right_other[...])).astype(bf16)
        for n in range(blocks):
            out_ref[n, 0] = low[n * count : (n + 1) * count]

    @pl.when(step == 0)
    def _():
        choose(0)

    @pl.when(step < last)
    def _():
        put(inner_ref, inner_other)

    @pl.when(step == last)
    def _():
        choose(1)
        put(branch_ref, branch_other)


def down_grad_kernel(act_ref, dy_ref, out_ref):
    total = dot(act_ref[0], dy_ref[0])
    for source in range(1, act_ref.shape[0]):
        total = total + dot(act_ref[source], dy_ref[source])
    out_ref[...] = jnp.transpose(total.astype(bf16))


def qkv_grad_kernel(groups, seq_ref, hat_ref, gain_ref, shift_ref, *refs):
    sources, given = refs[:5], refs[5 : 2 * groups + 5]
    out_ref, norms_ref, held, turned, sems = refs[2 * groups + 5 :]
    seq = seq_ref[0]
    count = given[0].shape[0]
    rows = count // 3
    skipped = lax.rem(2 * rows * seq, LANES)
    window = pl.ds(pl.multiple_of(2 * rows * seq - skipped, LANES), held.shape[2])
    copies = [
        pltpu.make_async_copy(source.at[:, window], held.at[n], sems.at[n])
        for n, source in enumerate(sources)
    ]
    for copy in copies:
        copy.start()
    gain, shift = row_of(gain_ref), row_of(shift_ref)
    grad_gain, grad_shift = jnp.zeros_like(gain), jnp.zeros_like(shift)
    grad_embed = jnp.zeros_like(gain)
    for n, copy in enumerate(copies):
        copy.wait()
        turned[n] = jnp.transpose(held[n])
    for h in range(2):
        span = slice(h * count, (h + 1) * count)
        product = jnp.zeros((count, hat_ref.shape[2]), f32)
        sums = jnp.zeros((count, 1), f32)
        for k in range(groups):
            grads = given[h * groups + k][...]
            product = product + dot(grads, hat_ref[k ^ seq])
            sums = sums + jnp.sum(grads.astype(f32), axis=1, keepdims=True)
        out_ref[:, span] = jnp.transpose((product * gain + sums * shift).astype(bf16))
        for n in range(3):
            own = slice(n * rows, (n + 1) * rows)
            first = pl.multiple_of(skipped + h * rows, 16)
            weight = turned[n, pl.ds(first, rows), :].astype(f32)
            grad_gain = grad_gain + jnp.sum(weight * product[own], axis=0, keepdims=True)
            grad_shift = grad_shift + jnp.sum(weight * sums[own], axis=0, keepdims=True)
        for n, which in ((3, 0), (4, 2)):
            own = slice(which * rows, (which + 1) * rows)
            first = pl.multiple_of(skipped + h * rows, 16)
            weight = turned[n, pl.ds(first, rows), :].astype(f32)
            grad_embed = grad_embed + jnp.sum(weight * sums[own], axis=0, keepdims=True)
    norms_ref[...] = jnp.concatenate(
        [grad_gain, grad_shift, grad_embed, jnp.zeros((5, gain.shape[1]), f32)], axis=0
    )


def qkv_total_kernel(parts_ref, *out_refs):
    total = parts_ref[0].astype(f32)
    for n in range(1, parts_ref.shape[0]):
        total = total + parts_ref[n].astype(f32)
    count = out_refs[0].shape[1] // 2
    for n, out_ref in enumerate(out_refs):
        second = (n + 3) * count
        out_ref[...] = jnp.concatenate(
            [total[:, n * count : (n + 1) * count], total[:, second : second + count]], axis=1
        )


def add_rows_kernel(steps_ref, rows_ref, out_ref):
    out_ref[...] = jnp.zeros_like(out_ref)
    for n in range(rows_ref.shape[0]):
        out_ref[pl.ds(steps_ref[n], 1), :] += rows_ref[n : n + 1, :]


def tokens_kernel(groups, seq_ref, x_ref, middle_ref, gain_ref, wq_hbm, wk_hbm, wv_hbm, *refs):
    given, (out_ref, held, grads_s, sems) = refs[: 2 * groups], refs[2 * groups :]
    copies = [
        pltpu.make_async_copy(source, held.at[n], sems.at[n])
        for n, source in enumerate((wq_hbm, wk_hbm, wv_hbm))
    ]
    for copy in copies:
        copy.start()
    seq = seq_ref[0]
    count = given[0].shape[0] // 3
    for k in range(groups):
        for h in range(2):
            for which in range(3):
                grads_s[which, rows_for(k ^ seq, h, count), :] = given[h * groups + k][
                    which * count : (which + 1) * count
                ]
    hat, scaled = normalize(x_ref[...].astype(f32))
    total = jnp.zeros(middle_ref.shape, f32)
    for which, copy in enumerate(copies):
        grads = jnp.transpose(grads_s[which])
        copy.wait()
        total = total + dot(grads, held[which], 1, 1)
    out_ref[...] = (
        middle_ref[...] + norm_back(total, hat, scaled, row_of(gain_ref))
    ).astype(bf16)


def whole(shape):
    zeros = (0,) * len(shape)
    return pl.BlockSpec(shape, lambda s: zeros, pipeline_mode=pl.Buffered(1))


def kept(shape):
    zeros = (0,) * len(shape)
    return pl.BlockSpec(shape, lambda s: zeros)


def per_head(shape):
    rest = (0,) * (len(shape) - 1)
    return pl.BlockSpec((1,) + tuple(shape[1:]), lambda s: (s,) + rest)


def params(grid=True):
    return pltpu.CompilerParams(
        dimension_semantics=("arbitrary",) if grid else None, vmem_limit_bytes=VMEM_LIMIT
    )


def takes(microseconds):
    return pl.CostEstimate(
        flops=int(microseconds * SCALE * 1e9), bytes_accessed=int(microseconds * SCALE * 3e6), transcendentals=0
    )


IN_VMEM = pl.BlockSpec(memory_space=pltpu.VMEM)
IN_SMEM = pl.BlockSpec(memory_space=pltpu.SMEM)
IN_HBM = pl.BlockSpec(memory_space=pl.ANY)


def shape_of(shape, kind):
    return jax.ShapeDtypeStruct(shape, kind)


def bias_strips(table):
    heads = table.shape[0]
    out = shape_of((heads, LANES // GRID, GRID, STRIP), f32)
    return pl.pallas_call(
        strips_kernel,
        grid=(heads,),
        in_specs=[per_head(table.shape)],
        out_specs=per_head(out.shape),
        out_shape=out,
        compiler_params=params(),
        cost_estimate=takes(9),
        name="strips",
    )(table)


def project(seq, x, embed, vectors, weights, groups, scale):
    count, width = x.shape
    part = shape_of((3 * width // groups // 2, count), bf16)
    outs = pl.pallas_call(
        partial(project_kernel, scale, groups),
        in_specs=[IN_SMEM] + [IN_VMEM] * 6 + [IN_HBM] * 5,
        out_specs=[IN_VMEM] * (2 * groups + 1),
        out_shape=(part,) * (2 * groups) + (shape_of((count, width), bf16),),
        scratch_shapes=[
            pltpu.VMEM((5, width, width), bf16),
            pltpu.VMEM((3, width, count), bf16),
            pltpu.SemaphoreType.DMA((5,)),
        ],
        compiler_params=params(False),
        cost_estimate=takes(9),
        name="project",
    )(seq, x, embed, *vectors, *weights)
    return outs[:groups], outs[groups : 2 * groups], outs[2 * groups]


def attend(seq, own, place, strips, half, head_size):
    heads = strips.shape[0] // 2
    length = place.shape[1]
    group = heads * head_size
    groups = len(own)
    tall = -(-head_size // 16) * 16
    saved = (
        shape_of((3 * group, length), bf16),
        shape_of((heads, length, length), bf16),
        shape_of((heads, 1, length), f32),
        shape_of((group, length), f32),
    )
    own_strips = pl.BlockSpec(
        (1,) + strips.shape[1:], lambda s: (half * heads + s, 0, 0, 0)
    )
    outs = pl.pallas_call(
        partial(attend_kernel, head_size, groups),
        grid=(heads,),
        in_specs=[IN_SMEM, whole(place.shape), own_strips] + [whole(a.shape) for a in own],
        out_specs=[kept((group, BLOCK))] * groups
        + [
            kept(saved[0].shape),
            per_head(saved[1].shape),
            per_head(saved[2].shape),
            kept(saved[3].shape),
        ],
        out_shape=(shape_of((group, BLOCK), bf16),) * groups + saved,
        scratch_shapes=[
            pltpu.VMEM((length, length), bf16),
            pltpu.VMEM((3 * group, length), f32),
            pltpu.VMEM((LANES, length), bf16),
            pltpu.VMEM((length, LANES), bf16),
            pltpu.VMEM((tall, length), bf16),
            pltpu.VMEM((length, BLOCK), f32),
        ],
        compiler_params=params(),
        cost_estimate=takes(13),
        name="attend",
    )(seq, place, strips, *own)
    return outs[:groups], outs[groups:]


def attend_back(seq, half, grad_mixed, qkv, expo, inverse, mixed, place, head_size):
    heads, length, _ = expo.shape
    group = heads * head_size
    groups = len(grad_mixed)
    tall = -(-head_size // 16) * 16
    table = shape_of((heads, 2, STRIP // LANES, LANES), f32)
    given = pl.BlockSpec((group, BLOCK), lambda s: (half, 0), pipeline_mode=pl.Buffered(1))
    outs = pl.pallas_call(
        partial(attend_back_kernel, head_size, groups),
        grid=(heads,),
        in_specs=[
            IN_SMEM,
            whole(qkv.shape),
            per_head(expo.shape),
            per_head(inverse.shape),
            whole(mixed.shape),
            whole(place.shape),
        ]
        + [given] * groups,
        out_specs=[kept((3 * group, BLOCK))] * groups
        + [per_head(table.shape), kept((8, 3 * group))],
        out_shape=(shape_of((3 * group, BLOCK), bf16),) * groups
        + (table, shape_of((8, 3 * group), f32)),
        scratch_shapes=[
            pltpu.VMEM((1, LANES // GRID, GRID, STRIP), f32),
            pltpu.VMEM((length, length), bf16),
            pltpu.VMEM((3 * group, length), f32),
            pltpu.VMEM((group, length), f32),
            pltpu.VMEM((3 * group, length), f32),
            pltpu.VMEM((length, LANES), bf16),
            pltpu.VMEM((tall, length), bf16),
            pltpu.VMEM((length, LANES), bf16),
            pltpu.VMEM((LANES, length), bf16),
            pltpu.VMEM((length, LANES), bf16),
            pltpu.VMEM((1, length), f32),
            pltpu.VMEM((length, LANES), f32),
            pltpu.VMEM((length, LANES), f32),
        ],
        compiler_params=params(),
        cost_estimate=takes(16),
        name="attend_back",
    )(seq, qkv, expo, inverse, mixed, place, *grad_mixed)
    return outs[:groups], outs[groups:]


def mlp_first(seq, mixed, x, dy, vectors, b_up, w_out, w_up, w_down):
    count, width = x.shape
    hidden = w_up.shape[1]
    step = 512
    chunks = hidden // step
    dma = pltpu.SemaphoreType.DMA
    return pl.pallas_call(
        partial(mlp_first_kernel, len(mixed) // 2, step),
        in_specs=[IN_SMEM] + [IN_VMEM] * 6 + [IN_HBM] * 3 + [IN_VMEM] * len(mixed),
        out_specs=[IN_HBM] * 3 + [IN_VMEM] * 3,
        out_shape=(
            shape_of((count, hidden), bf16),
            shape_of((hidden, count), bf16),
            shape_of((count, hidden), bf16),
            shape_of((2, width, count), bf16),
            shape_of((count, width), f32),
            shape_of((1, hidden), f32),
        ),
        scratch_shapes=[
            pltpu.VMEM((width, width), bf16),
            pltpu.VMEM((chunks, width, step), bf16),
            pltpu.VMEM((chunks, step, width), bf16),
            pltpu.VMEM((chunks, count, step), bf16),
            pltpu.VMEM((chunks, step, count), bf16),
            pltpu.VMEM((chunks, count, step), bf16),
            pltpu.VMEM((count, width), bf16),
            dma((1,)),
        ]
        + [dma((chunks,))] * 5,
        compiler_params=params(False),
        cost_estimate=takes(14),
        name="mlp_first",
    )(seq, x, dy, *vectors, b_up, w_out, w_up, w_down, *mixed)


def mlp_second(seq, middle, dy, vectors, act, inner, w_out, w_up, w_down, groups):
    count, width = middle.shape
    hidden = w_up.shape[1]
    step = 512
    chunks = hidden // step
    part = shape_of((width // groups, count), bf16)
    dma = pltpu.SemaphoreType.DMA
    outs = pl.pallas_call(
        partial(mlp_second_kernel, groups, step),
        in_specs=[IN_SMEM] + [IN_VMEM] * 4 + [IN_HBM] * 5,
        out_specs=[IN_VMEM] * (groups + 4),
        out_shape=(part,) * groups
        + (
            shape_of((count, width), bf16),
            shape_of((count, width), f32),
            shape_of((count, width), bf16),
            shape_of((8, width), f32),
        ),
        scratch_shapes=[
            pltpu.VMEM((width, width), bf16),
            pltpu.VMEM((chunks, width, step), bf16),
            pltpu.VMEM((chunks, step, width), bf16),
            pltpu.VMEM((chunks, count, step), bf16),
            pltpu.VMEM((chunks, count, step), bf16),
            pltpu.VMEM((count, width), f32),
            pltpu.VMEM((count, width), f32),
            pltpu.VMEM((width, count), bf16),
            dma((1,)),
            dma((chunks,)),
            dma((chunks,)),
            dma((chunks,)),
            dma((chunks,)),
        ],
        compiler_params=params(False),
        cost_estimate=takes(14),
        name="mlp_second",
    )(seq, middle, dy, *vectors, act, inner, w_out, w_up, w_down)
    return outs[:groups], outs[groups:]


def pair_grad(order, first, own, other, inner, inner_other, branch, branch_other):
    _, rows, count = own.shape
    blocks, groups = first.shape[0], order.shape[0]
    width = inner.shape[1] // groups
    wide = pl.BlockSpec(
        (count, width),
        lambda s, order_ref, first_ref: (0, order_ref[jnp.minimum(s, groups - 1)]),
    )
    narrow = pl.BlockSpec((count, width), lambda s, order_ref, first_ref: (0, 0))
    left = pl.BlockSpec((2, rows, count), lambda s, order_ref, first_ref: (0, 0, 0))
    block = (blocks, 1, rows // 2 // blocks, width)
    return pl.pallas_call(
        pair_grad_kernel,
        grid_spec=pltpu.PrefetchScalarGridSpec(
            num_scalar_prefetch=2,
            grid=(groups + 1,),
            in_specs=[left, left, wide, wide, narrow, narrow],
            out_specs=pl.BlockSpec(block, lambda s, order_ref, first_ref: (0, s, 0, 0)),
            scratch_shapes=[pltpu.VMEM((rows // 2, count), bf16)] * 2,
        ),
        out_shape=shape_of((blocks, groups + 1) + block[2:], bf16),
        compiler_params=params(),
        cost_estimate=takes(10),
        name="pair_grad",
    )(order, first, own, other, inner, inner_other, branch, branch_other)


def down_grad(act, dy):
    return pl.pallas_call(
        down_grad_kernel,
        in_specs=[IN_VMEM, IN_VMEM],
        out_specs=IN_VMEM,
        out_shape=shape_of((dy.shape[2], act.shape[1]), bf16),
        compiler_params=params(False),
        cost_estimate=takes(8),
        name="down_grad",
    )(act, dy)


def qkv_grad(seq, grads, hat, gain, shift, weights):
    width = hat.shape[2]
    count = grads[0].shape[0]
    columns = -(-(2 * count // 3 + LANES - GRID) // LANES) * LANES
    return pl.pallas_call(
        partial(qkv_grad_kernel, len(grads) // 2),
        in_specs=[IN_SMEM] + [IN_VMEM] * 3 + [IN_HBM] * 5 + [IN_VMEM] * len(grads),
        out_specs=[IN_VMEM] * 2,
        out_shape=(shape_of((width, 2 * count), bf16), shape_of((8, width), f32)),
        scratch_shapes=[
            pltpu.VMEM((5, width, columns), bf16),
            pltpu.VMEM((5, columns, width), bf16),
            pltpu.SemaphoreType.DMA((5,)),
        ],
        compiler_params=params(False),
        cost_estimate=takes(8),
        name="qkv_grad",
    )(seq, hat, gain, shift, *weights, *grads)


def add_rows(steps, rows, count):
    return pl.pallas_call(
        add_rows_kernel,
        in_specs=[IN_SMEM, IN_VMEM],
        out_specs=IN_VMEM,
        out_shape=shape_of((count, rows.shape[1]), f32),
        compiler_params=params(False),
        cost_estimate=takes(3),
        name="add_rows",
    )(steps, rows)


def qkv_total(parts):
    _, rows, columns = parts.shape
    return pl.pallas_call(
        qkv_total_kernel,
        out_shape=(shape_of((rows, columns // 3), f32),) * 3,
        compiler_params=params(False),
        cost_estimate=takes(2),
        name="qkv_total",
    )(parts)


def token_grad(seq, grads, x, middle, gain, weights):
    count, width = x.shape
    return pl.pallas_call(
        partial(tokens_kernel, len(grads) // 2),
        in_specs=[IN_SMEM] + [IN_VMEM] * 3 + [IN_HBM] * 3 + [IN_VMEM] * len(grads),
        out_specs=IN_VMEM,
        out_shape=shape_of((count, width), bf16),
        scratch_shapes=[
            pltpu.VMEM((3, width, width), bf16),
            pltpu.VMEM((3, width, count), bf16),
            pltpu.SemaphoreType.DMA((3,)),
        ],
        compiler_params=params(False),
        cost_estimate=takes(9),
        name="token_grad",
    )(seq, x, middle, gain, *weights, *grads)


def exchange(array, axis, step):
    size = lax.axis_size(axis)
    return lax.ppermute(array, axis, [(i, i ^ step) for i in range(size)])


def sum_over(vector, axis):
    step = 1
    while step < lax.axis_size(axis):
        vector = vector + exchange(vector, axis, step)
        step *= 2
    return vector


def swap(parts, axis):
    return [parts[0]] + [exchange(parts[k], axis, k) for k in range(1, len(parts))]


def halve(array, axis, dim, step, bit):
    keep = lax.dynamic_index_in_dim(array, bit, dim, keepdims=False)
    send = lax.dynamic_index_in_dim(array, 1 - bit, dim, keepdims=False)
    return (keep.astype(f32) + exchange(send, axis, step).astype(f32)).astype(bf16)


def add_low(left, right):
    return (left.astype(f32) + right.astype(f32)).astype(bf16)


def tie(*arrays):
    return lax.optimization_barrier(arrays)


def key_places(rel_index):
    first = rel_index[0]
    top = jnp.max(first)
    row = top // SPAN - first // SPAN
    column = top % SPAN - first % SPAN
    return (row * GRID + column)[None, :].astype(jnp.int32)


def table_grad(folded):
    heads = folded.shape[0]
    parts = folded.reshape(heads, 2, STRIP // LANES, 2, LANES // 2)
    parts = jnp.transpose(parts, (0, 2, 3, 1, 4)).reshape(heads, 2 * GRID, LANES // 2)
    return parts[:, :SPAN, :SPAN].reshape(heads, SPAN * SPAN)


def per_device(
    tokens,
    timesteps,
    rel_index,
    time_table,
    bias_table,
    gain_one,
    shift_one,
    w_query,
    w_key,
    w_value,
    t_query,
    t_value,
    b_query,
    b_value,
    w_out,
    b_out,
    gain_two,
    shift_two,
    w_up,
    b_up,
    w_down,
    b_down,
    cotangent,
):
    _, local, width = tokens.shape
    hidden = w_up.shape[1]
    heads = bias_table.shape[0]
    head_size = width // heads
    n_dp, n_seq = lax.axis_size("dp"), lax.axis_size("seq")
    dp, seq = lax.axis_index("dp"), lax.axis_index("seq")
    own_heads = heads // n_seq
    group = own_heads * head_size
    half = group // 2
    scale = head_size ** (-0.5)
    table_rows = time_table.shape[0]
    down_rows, out_rows = hidden // n_dp, width // n_dp

    def own_columns(array):
        return lax.dynamic_slice_in_dim(array, seq * group, group, axis=array.ndim - 1)

    x, dy = tokens[0], cotangent[0]
    here = seq.astype(jnp.int32)[None]
    embed = lax.dynamic_slice_in_dim(time_table, timesteps[0], 1, 0)
    *mine, hat_one = project(
        here,
        x,
        embed,
        (gain_one, shift_one, b_query, b_value),
        (w_key, w_query, t_query, w_value, t_value),
        n_seq,
        scale,
    )
    own_0 = swap(mine[0], "seq")
    dy_all = lax.all_gather(dy, "dp", axis=0)
    place = key_places(rel_index)
    table = lax.dynamic_slice_in_dim(bias_table, seq * own_heads, own_heads, 0)
    table = jnp.pad(
        table.reshape(own_heads, SPAN, SPAN), ((0, 0), (0, 72 - SPAN), (0, LANES - SPAN))
    )
    table, hat_one = tie(table, hat_one)
    strips = bias_strips(table)
    own_0, parts_1, place, strips = tie(own_0, mine[1], place, strips)
    own_1 = swap(parts_1, "seq")
    tokens_0, saved_0 = attend(here, own_0, place, strips, 0, head_size)

    own_1, tokens_0, saved_0, place, dy_all = tie(own_1, tokens_0, saved_0, place, dy_all)
    mixed_0 = swap(tokens_0, "seq")
    tokens_1, saved_1 = attend(here, own_1, place, strips, 1, head_size)

    tokens_1, saved_1, mixed_0 = tie(tokens_1, saved_1, mixed_0)
    mixed_1 = swap(tokens_1, "seq")

    mixed_1, hat_one = tie(mixed_1, hat_one)
    hat_all = lax.all_gather(hat_one, "seq", axis=0)
    act, act_t, grad_inner, turned, middle, up_sum = mlp_first(
        here,
        mixed_0 + mixed_1,
        x,
        dy,
        (b_out, gain_two, shift_two),
        b_up[None],
        w_out,
        w_up,
        w_down,
    )

    core = dp % 2
    act_parts = lax.all_to_all(act_t.reshape(n_dp, down_rows, local), "dp", 0, 0)
    turned_other = exchange(turned, "dp", 1)
    inner_other = exchange(grad_inner, "dp", 1)
    grad_mixed, (result, grad_middle, branch, sums_two) = mlp_second(
        here, middle, dy, (b_down, gain_two), act, grad_inner, w_out, w_up, w_down, n_seq
    )

    grad_mixed, result, grad_middle, branch, sums_two, turned_other, inner_other = tie(
        grad_mixed, result, grad_middle, branch, sums_two, turned_other, inner_other
    )
    grad_mixed = swap(grad_mixed, "seq")
    branch_other = exchange(branch, "dp", 1)
    first = (2 * jnp.arange(n_dp // 2) + core) * out_rows
    turned_rows = [turned, turned_other]
    if out_rows % 16:
        first = jnp.zeros((1,), jnp.int32)
        turned_rows = [
            jnp.tile(
                lax.dynamic_index_in_dim(
                    a.reshape(2, n_dp // 2, 2, out_rows, local), core, 2, keepdims=False
                ).reshape(2, width // 2, local),
                (1, 2, 1),
            )
            for a in turned_rows
        ]
    pair = pair_grad(
        (jnp.arange(n_seq) ^ seq).astype(jnp.int32),
        first.astype(jnp.int32),
        *turned_rows,
        grad_inner,
        inner_other,
        branch,
        branch_other,
    )

    pair, act_parts = tie(pair, act_parts)
    part_down = down_grad(act_parts, dy_all)

    part_down, grad_mixed, pair, hat_all = tie(part_down, grad_mixed, pair, hat_all)
    grad_w_down = lax.psum_scatter(part_down, "seq", scatter_dimension=0, tiled=True)
    if out_rows % 16:
        pair = jnp.swapaxes(pair.reshape(n_seq + 1, n_dp // 2, out_rows, width), 0, 1)
    same_core = [list(range(c, n_dp, 2)) for c in range(2)]
    pair = lax.all_to_all(pair, "dp", 0, 0, axis_index_groups=same_core)
    grads_0, (table_0, sums_0) = attend_back(here, 0, grad_mixed, *saved_0, place, head_size)

    grads_0, table_0, sums_0, grad_mixed, place = tie(grads_0, table_0, sums_0, grad_mixed, place)
    heads_0 = swap(grads_0, "seq")
    grads_1, (table_1, sums_1) = attend_back(here, 1, grad_mixed, *saved_1, place, head_size)

    grads_1, table_1, sums_1, heads_0, grad_w_down = tie(
        grads_1, table_1, sums_1, heads_0, grad_w_down
    )
    heads_1 = swap(grads_1, "seq")
    product, norms = qkv_grad(
        here,
        list(grads_0) + list(grads_1),
        hat_all,
        gain_one,
        shift_one,
        (w_query, w_key, w_value, t_query, t_value),
    )

    product, norms, pair = tie(product, norms, pair)

    def source_sum(parts):
        return jnp.sum(parts.astype(f32), axis=0).astype(bf16)

    near_keep, near_send = (source_sum(pair[:, n:n_seq:2]) for n in range(2))

    (
        heads_1,
        near_keep,
        near_send,
        pair,
        norms,
        table_0,
        table_1,
        sums_0,
        sums_1,
        up_sum,
        sums_two,
    ) = tie(
        heads_1,
        near_keep,
        near_send,
        pair,
        norms,
        table_0,
        table_1,
        sums_0,
        sums_1,
        up_sum,
        sums_two,
    )
    near_received = exchange(near_send, "seq", 1)
    out_part = source_sum(pair[:, n_seq])
    grad_tokens = token_grad(
        here, heads_0 + heads_1, x, grad_middle, gain_one, (w_query, w_key, w_value)
    )
    query_sum, value_sum = (
        jnp.concatenate([sums[0, n * half : (n + 1) * half] for sums in (sums_0, sums_1)])
        for n in (0, 2)
    )
    own_image = lax.broadcasted_iota(jnp.int32, (n_dp, 1), 0) == dp

    def slot(row):
        return jnp.where(own_image, row[None, :], 0.0).reshape(-1)

    apart = [table_grad(jnp.concatenate([table_0, table_1])).reshape(-1), query_sum, value_sum]
    summed = [
        slot(norms[2]),
        up_sum[0],
        sums_two[:4].reshape(-1),
        norms[:2].reshape(-1),
    ]
    images = [slot(jnp.concatenate([query_sum, value_sum, timesteps.astype(f32)]))]
    sizes = [sum(a.shape[0] for a in part) for part in (apart, summed, images)]
    vector = sum_over(jnp.concatenate(apart + summed + images), "dp")

    vector, out_part, product, grad_tokens, near_received = tie(
        vector, out_part, product, grad_tokens, near_received
    )
    far_keep, far_send = (
        add_low(near_keep[n], near_received[n]) for n in range(2)
    )
    far_received = exchange(far_send, "seq", 2)
    grad_qkv = lax.all_to_all(product.reshape(n_dp, out_rows, 3 * group), "dp", 0, 0)
    image_sums = vector[sizes[0] + sizes[1] :].reshape(n_dp, 2 * group + 1)
    apart = vector[: sizes[0]].astype(bf16)[None]
    summed = vector[sizes[0] : sizes[0] + sizes[1]]
    apart = jnp.concatenate([apart, exchange(apart, "seq", 1)], axis=0)
    summed = summed + exchange(summed, "seq", 1)

    apart, summed, out_part = tie(apart, summed, out_part)
    far_apart, far_summed = exchange(apart, "seq", 2), exchange(summed, "seq", 2)
    out_part = out_part.reshape(out_rows, 2, n_seq // 2, group)
    out_part = halve(out_part, "seq", 2, 1, seq & 1)

    far_apart, far_summed, out_part, far_received, image_sums = tie(
        far_apart, far_summed, out_part, far_received, image_sums
    )
    steps_all = image_sums[:, 2 * group].astype(jnp.int32)
    grad_qkv = qkv_total(grad_qkv)
    grad_w_up = far_keep.astype(f32) + far_received.astype(f32)
    grad_w_out = halve(out_part, "seq", 1, 2, seq >> 1)
    grad_w_down = jnp.transpose(grad_w_down.astype(f32))
    grad_w_out = grad_w_out.astype(f32)
    apart = jnp.concatenate([apart, far_apart], axis=0)
    apart = jnp.concatenate(
        [lax.dynamic_index_in_dim(apart, n ^ seq, 0) for n in range(n_seq)], axis=0
    ).astype(f32)
    both = summed + far_summed
    table_size = own_heads * SPAN * SPAN
    grad_bias_table = apart[:, :table_size].reshape(heads, SPAN * SPAN)
    grad_b_query = apart[:, table_size : table_size + group].reshape(-1)
    grad_b_value = apart[:, table_size + group :].reshape(-1)
    embed_size = n_dp * width
    embed_rows = both[:embed_size].reshape(n_dp, width)
    grad_b_up = both[embed_size : embed_size + hidden]
    rest = both[embed_size + hidden :].reshape(6, width)
    grad_b_down, grad_gain_two, grad_shift_two, grad_b_out, grad_gain_one, grad_shift_one = (
        rest[r] for r in range(6)
    )

    embeds = lax.dynamic_slice_in_dim(
        jnp.take(time_table, steps_all, axis=0), dp * out_rows, out_rows, axis=1
    ).astype(f32)
    grad_t_query = jnp.dot(embeds.T, image_sums[:, :group], precision=HIGHEST)
    grad_t_value = jnp.dot(embeds.T, image_sums[:, group : 2 * group], precision=HIGHEST)
    grad_time_table = add_rows(steps_all, embed_rows, table_rows)

    return (
        result[None],
        grad_tokens[None],
        *grad_qkv,
        grad_t_query,
        grad_t_value,
        grad_w_out,
        grad_w_up,
        grad_w_down,
        grad_gain_one,
        grad_shift_one,
        grad_b_query,
        grad_b_value,
        grad_b_out,
        grad_gain_two,
        grad_shift_two,
        grad_b_up,
        grad_b_down,
        grad_bias_table,
        grad_time_table,
    )


def solution(mesh):
    split, copied, by_block = P("dp", "seq", None), P(), P("dp", "seq")
    in_specs = (split, P("dp"), P("seq", None)) + (copied,) * 19 + (split,)
    out_specs = (split, split) + (by_block,) * 8 + (copied,) * 11
    return jax.shard_map(
        per_device, mesh=mesh, in_specs=in_specs, out_specs=out_specs, check_vma=False
    )
```
